32 devices in a mesh: blk: 16 (over z, y, core), rep: 2 (over x).
Axes of the slice: x: 2, y: 2, z: 4, core: 2. Of those that a mesh axis runs over, the one named last changes fastest.
Arguments:
- cell_values: bfloat16 [2, 1024, 6, 192], P('rep', 'blk'), may hold values from -6 to 6
- table_ids: int32 [2, 1024], P('rep', 'blk'), may hold values from 0 to 15, as said below
- train_mask: int32 [2, 1024], P('rep', 'blk'), may hold values from 0 to 1, as said below
- feat_count: int32 [2, 16], P('rep'), may hold values from 3 to 6, as said below
- w_attn: bfloat16 [1536, 192], P(('blk', 'rep'))
- w_mlp: bfloat16 [768, 192], P(('blk', 'rep')), may hold values from -0.4375 to 0.4375
- vectors: bfloat16 [1536], P(('blk', 'rep'))
- cotangent: bfloat16 [2, 1024, 6, 192], P('rep', 'blk'), may hold values from -6 to 6
Outputs:
- layer_out: bfloat16 [2, 1024, 6, 192], P('rep', 'blk')
- cell_grads: float32 [2, 1024, 6, 192], P('rep', 'blk')
- attn_grads: float32 [1536, 192], P(('blk', 'rep'))
- mlp_grads: float32 [768, 192], P(('blk', 'rep'))
- vector_grads: float32 [1536], P(('blk', 'rep'))
The draws below stay inside these ranges and needn't reach their ends.
Inputs may be any that keep to these rules, and one draw needn't show every extreme that they name: `table_ids`: within a pack the numbers never fall from row to row and each appears; one table runs from the first device's 64 rows to the last device's. `train_mask`: the first row of every table is 1. `feat_count`: some table of each pack has all 6.
All inputs are finite; a program needn't handle non-finite values.
Results may differ from the reference program's by a relative error of at most 0.03.
Values may be sent and summed in bfloat16 or wider, within the bound.
No kernel may reach another device: no remote copies, remote signals or barrier semaphores. Data moves between devices by JAX's collectives and lax.ppermute only.
A program may use at most 448 MiB of HBM per device.

```python
import jax
import jax.numpy as jnp
from jax import lax

D = 192
HEADS = 6
HEAD_DIM = 32
HIDDEN_SIZE = 384
FEAT = 6
ROWS_DEV = 64
TABLES = 16
PACKS = 2
ROWS = 1024


def one_table_pack(key):
    front_key, tail_key, shuffle_key, coin_key = jax.random.split(key, 4)
    front_rows = jax.random.randint(front_key, (), TABLES // 2, ROWS_DEV)
    tail_rows = jax.random.randint(tail_key, (), TABLES // 2, ROWS_DEV)
    position = jnp.arange(ROWS)
    usable = (position >= 1) & (position < front_rows) | (position > ROWS - tail_rows) & (position < ROWS)
    shuffled = jax.random.permutation(shuffle_key, ROWS)
    ranked = jnp.where(usable, shuffled + ROWS, shuffled)
    chosen = lax.top_k(ranked, TABLES - 3)[1]
    starts = jnp.zeros((ROWS,), jnp.int32).at[chosen].set(1)
    starts = starts.at[front_rows].set(1).at[ROWS - tail_rows].set(1)
    tables = jnp.cumsum(starts).astype(jnp.int32)
    coin_flips = jax.random.randint(coin_key, (ROWS,), 0, 2)
    first_rows = jnp.maximum(starts, (position == 0).astype(jnp.int32))
    train_flags = jnp.maximum(coin_flips, first_rows)
    return (tables, train_flags.astype(jnp.int32))


def table_layout(key):
    return jax.vmap(one_table_pack)(jax.random.split(key, PACKS))


def draw_table_ids(key, part):
    return table_layout(key)[0]


def draw_train_mask(key, part):
    return table_layout(key)[1]


def draw_feat_count(key, part):
    key = jax.random.fold_in(key, 3)
    count_key, pick_key = jax.random.split(key)
    counts_now = jax.random.randint(count_key, (PACKS, TABLES), FEAT // 2, FEAT + 1)
    widest = jax.random.randint(pick_key, (PACKS, 1), 0, TABLES)
    return jnp.where(jnp.arange(TABLES)[None, :] == widest, FEAT, counts_now).astype(jnp.int32)


def draw_w_attn(key, part):
    key = jax.random.fold_in(key, 5)
    base_draw = jax.random.normal(key, (8 * D, D), jnp.float32)
    factor = jnp.array([1.0, 1.0, 1.0, 2.0, 1.0, 1.0, 1.0, 16.0], jnp.float32)[jnp.arange(8 * D) // D]
    return (base_draw * factor[:, None] * D ** (-0.5)).astype(jnp.bfloat16)


def draw_vectors(key, part):
    key = jax.random.fold_in(key, 7)
    gain_key, shift_key = jax.random.split(key)
    gain_rows = 1.0 + 0.3 * jax.random.uniform(gain_key, (3, D), jnp.float32, -1.0, 1.0)
    shift_rows = 0.3 * jax.random.normal(shift_key, (5, D), jnp.float32)
    return jnp.concatenate([gain_rows, shift_rows], axis=0).reshape(8 * D).astype(jnp.bfloat16)


def levels(own_key, extent, cuts, least, largest):
    def one(axis_at, shards_of):
        steps = jax.random.uniform(jax.random.fold_in(jax.random.fold_in(own_key, 6), axis_at), (shards_of,), jnp.float32, least / len(cuts), largest / len(cuts))
        return jnp.repeat(jnp.exp(steps), extent[axis_at] // shards_of).reshape((-1,) + (1,) * (len(extent) - axis_at - 1))

    level = one(*cuts[0])
    for cut in cuts[1:]:
        level = level * one(*cut)
    return level


def noise(rng, extent, scale, most, pieces=(), kind=jnp.bfloat16):
    values = scale * jax.random.normal(rng, extent, jnp.float32)
    if pieces:
        values = values * levels(rng, extent, pieces, -0.22, 0.18)
    return jnp.clip(values, -most, most).astype(kind)


def setup_inputs(seed: int = 0) -> dict:
    seeds = jax.random.split(jax.random.key(seed), 9)
    cell_values = noise(seeds[0], (PACKS, ROWS, FEAT, D), 1.0, 6.0, ((0, 2), (1, 16)))
    table_ids = draw_table_ids(jax.random.fold_in(seeds[8], 71), 0)
    train_mask = draw_train_mask(jax.random.fold_in(seeds[8], 71), 0)
    feat_count = draw_feat_count(jax.random.fold_in(seeds[8], 71), 0)
    w_attn = draw_w_attn(jax.random.fold_in(seeds[8], 71), 0)
    w_mlp = noise(seeds[5], (2 * HIDDEN_SIZE, D), D ** -0.5, 0.4375, ((0, 32),))
    vectors = draw_vectors(jax.random.fold_in(seeds[8], 71), 0)
    cotangent = noise(seeds[7], (PACKS, ROWS, FEAT, D), 1.0, 6.0, ((0, 2), (1, 16)))
    return dict(cell_values=cell_values, table_ids=table_ids, train_mask=train_mask, feat_count=feat_count, w_attn=w_attn, w_mlp=w_mlp, vectors=vectors, cotangent=cotangent)


@jax.custom_vjp
def low(v):
    return lax.optimization_barrier(v.astype(jnp.bfloat16)).astype(jnp.float32)

@jax.custom_vjp
def low_back(v):
    return v

def low_keep(v):
    return (low(v), None)

def low_pass(kept, grad):
    return (grad,)

def back_keep(v):
    return (v, None)

def back_low(kept, grad):
    return (low(grad),)
low.defvjp(low_keep, low_pass)
low_back.defvjp(back_keep, back_low)
highest = lax.Precision.HIGHEST
norm_eps = 1e-05
neg_fill = -1e+30

def layer_norm(inputs, gain_row, shift_row):
    centre = inputs - lax.optimization_barrier(jnp.mean(inputs, axis=-1, keepdims=True))
    spread = lax.optimization_barrier(jnp.mean(centre * centre, axis=-1, keepdims=True))
    return centre * lax.rsqrt(spread + norm_eps) * gain_row + shift_row

def project(inputs, matrix):
    return jnp.dot(inputs, matrix, precision=highest)

def rounded(inputs):
    return low_back(low(inputs))

def split_heads(inputs):
    return inputs.reshape(inputs.shape[:-1] + (HEADS, HEAD_DIM))

def softmax_rows(scores):
    top_score = lax.optimization_barrier(jnp.max(scores, axis=-1, keepdims=True))
    powers = jnp.exp(scores - top_score)
    return powers / lax.optimization_barrier(jnp.sum(powers, axis=-1, keepdims=True))

def feature_attention(cell_rows, attn_mats, valid_feat):
    queries = split_heads(rounded(project(cell_rows, attn_mats[0])))
    key_rows = split_heads(rounded(project(cell_rows, attn_mats[1])))
    value_rows = split_heads(rounded(project(cell_rows, attn_mats[2])))
    scores = low_back(jnp.einsum('rfhe,rghe->rhfg', queries, key_rows, precision=highest) * HEAD_DIM ** (-0.5))
    scores = jnp.where(valid_feat[:, None, None, :], scores, neg_fill)
    attn_probs = low(softmax_rows(scores))
    mixed = jnp.einsum('rhfg,rghe->rfhe', attn_probs, value_rows, precision=highest)
    mixed = rounded(mixed.reshape(cell_rows.shape))
    return low_back(project(mixed, attn_mats[3]))

def item_block(queries, query_tables, key_rows, value_rows, key_tags):
    scores = low_back(jnp.einsum('rfhe,jfhe->fhrj', queries, key_rows, precision=highest) * HEAD_DIM ** (-0.5))
    allowed = query_tables[:, None] == key_tags[None, :]
    scores = jnp.where(allowed[None, None], scores, neg_fill)
    attn_probs = low(softmax_rows(scores))
    return jnp.einsum('fhrj,jfhe->rfhe', attn_probs, value_rows, precision=highest)

def item_attention(normed, attn_mats, table_row, train_row):
    queries = split_heads(rounded(project(normed, attn_mats[4])))
    key_rows = split_heads(rounded(project(normed, attn_mats[5])))
    value_rows = split_heads(rounded(project(normed, attn_mats[6])))
    key_tags = jnp.where(train_row > 0, table_row, -1)
    block_rows = min(ROWS, 256)
    query_blocks = queries.reshape((ROWS // block_rows, block_rows) + queries.shape[1:])
    table_blocks = table_row.reshape(ROWS // block_rows, block_rows)

    def one_block(inputs):
        return item_block(inputs[0], inputs[1], key_rows, value_rows, key_tags)
    mixed = lax.map(jax.checkpoint(one_block), (query_blocks, table_blocks))
    mixed = rounded(mixed.reshape(normed.shape))
    return low_back(project(mixed, attn_mats[7]))

def forward(cell_rows, attn_flat, mlp_mats, vector_flat, table_row, train_row, feat_counts):
    attn_mats = attn_flat.reshape(8, D, D)
    vector_rows = vector_flat.reshape(8, D)
    counted = lax.optimization_barrier(jnp.sum(jnp.where(table_row[:, None] == jnp.arange(TABLES)[None, :], feat_counts[None, :], 0), axis=1))
    valid_feat = jnp.arange(FEAT)[None, :] < counted[:, None]
    mixed_one = cell_rows + feature_attention(cell_rows, attn_mats, valid_feat) + vector_rows[6]
    normed_one = layer_norm(mixed_one, vector_rows[0], vector_rows[3])
    mixed_two = normed_one + item_attention(low(normed_one), attn_mats, table_row, train_row)
    normed_two = layer_norm(mixed_two, vector_rows[1], vector_rows[4])
    up_proj = low_back(jnp.dot(low(normed_two), mlp_mats[:HIDDEN_SIZE].T, precision=highest))
    hidden = low(jax.nn.gelu(up_proj))
    down_proj = low_back(project(hidden, mlp_mats[HIDDEN_SIZE:])) + vector_rows[7]
    return layer_norm(normed_two + down_proj, vector_rows[2], vector_rows[5])

def reference(cell_values, table_ids, train_mask, feat_count, w_attn, w_mlp, vectors, cotangent):
    attn_flat = w_attn.astype(jnp.float32)
    mlp_mats = w_mlp.astype(jnp.float32)
    vector_flat = vectors.astype(jnp.float32)
    outputs = []
    input_grads = []
    attn_grad = jnp.zeros_like(attn_flat)
    mlp_grad = jnp.zeros_like(mlp_mats)
    vector_grad = jnp.zeros_like(vector_flat)
    for pack_index in range(PACKS):

        def pack_forward(cells_in, attn_in, mlp_in, vector_in):
            return forward(cells_in, attn_in, mlp_in, vector_in, table_ids[pack_index], train_mask[pack_index], feat_count[pack_index])
        result, pull_back = jax.vjp(pack_forward, cell_values[pack_index].astype(jnp.float32), attn_flat, mlp_mats, vector_flat)
        pack_grads = pull_back(cotangent[pack_index].astype(jnp.float32))
        outputs.append(result)
        input_grads.append(pack_grads[0])
        attn_grad = attn_grad + pack_grads[1]
        mlp_grad = mlp_grad + pack_grads[2]
        vector_grad = vector_grad + pack_grads[3]
    return (jnp.stack(outputs).astype(jnp.bfloat16), jnp.stack(input_grads), attn_grad, mlp_grad, vector_grad)
```

```python
import functools
import math

import jax
import jax.numpy as jnp
from jax import lax
from jax.experimental import pallas as pl
from jax.experimental.pallas import tpu as pltpu
from jax.sharding import Mesh
from jax.sharding import PartitionSpec as P

D = 192
HEADS = 6
HEAD_DIM = 32
HIDDEN = 384
FEAT = 6
TABLES = 16

Z = 4
SLOTS = 3
SLOT_HEADS = 3
SLOT_COLS = SLOT_HEADS * HEAD_DIM
PAIR = 2 * D
LANES = 128
KEY_TILE = 256

EPS = 1e-05
FAR = -1e30
BLOCKED = -(2.0**100)
SCALE = HEAD_DIM ** (-0.5)
LOG2E = 1.4426950408889634
SCALE2 = SCALE * LOG2E

bf16 = jnp.bfloat16
f32 = jnp.float32
BLK = ("zh", "zl", "y", "core")
FAN = ("zh", "zl", "y", "rep")
TASK_AXES = ("zl", "y")
Z_AXES = ("zh", "zl")
PLANE_AXES = ("y", "rep")
TASK_ORDER = (0, 2, 1, 3)
FAR_ORDER = (0, 3, 2, 1)


def dot(a, b):
    return lax.dot_general(a, b, (((1,), (0,)), ((), ())), preferred_element_type=f32)


def dot_t(a, b):
    return lax.dot_general(a, b, (((1,), (1,)), ((), ())), preferred_element_type=f32)


def t_dot(a, b):
    return lax.dot_general(a, b, (((0,), (0,)), ((), ())), preferred_element_type=f32)


def loop(count, body, carry=None):
    if count > 8:
        return lax.fori_loop(0, count, body, carry)
    for i in range(count):
        carry = body(i, carry)
    return carry


def span(i, size):
    if isinstance(i, int):
        return slice(i * size, (i + 1) * size)
    return pl.ds(pl.multiple_of(i * size, size), size)


def task_place():
    return lax.axis_index("zl") * 2 + lax.axis_index("y")


def partner(step):
    return lax.bitwise_xor(task_place(), TASK_ORDER[step])


def own_feature(t):
    return (3 * t + 1) // 2 if isinstance(t, int) else lax.div(3 * t + 1, 2)


def shared_feature(t):
    return 1 + 3 * (t // 2) if isinstance(t, int) else 1 + 3 * lax.div(t, 2)


def is_odd():
    return lax.axis_index("y") == 1


def normed(z):
    centre = z - jnp.mean(z, axis=-1, keepdims=True)
    rstd = lax.rsqrt(jnp.mean(centre * centre, axis=-1, keepdims=True) + EPS)
    return centre * rstd, rstd


def norm_back(xhat, rstd, gain, grad):
    scaled = grad * gain
    mean_a = jnp.mean(scaled, axis=-1, keepdims=True)
    mean_b = jnp.mean(scaled * xhat, axis=-1, keepdims=True)
    return rstd * (scaled - mean_a - xhat * mean_b)


def col_sum(a):
    return jnp.sum(a, axis=0, keepdims=True)


def head_ones():
    a = lax.broadcasted_iota(jnp.int32, (D, D), 0) // HEAD_DIM
    b = lax.broadcasted_iota(jnp.int32, (D, D), 1) // HEAD_DIM
    return (a == b).astype(bf16)


def row_to_col(row, size):
    a = lax.broadcasted_iota(jnp.int32, (size, size), 0)
    b = lax.broadcasted_iota(jnp.int32, (size, size), 1)
    return jnp.sum(jnp.where(a == b, row, 0.0), axis=1, keepdims=True)


def feat_probs(query, keys, valid, ones, rows):
    prod = (keys * query[None]).reshape(FEAT * rows, D).astype(bf16)
    scores = dot(prod, ones).reshape(FEAT, rows, D)
    scores = [jnp.where(valid[g], scores[g] * SCALE2, FAR) for g in range(FEAT)]
    top = functools.reduce(jnp.maximum, scores)
    powers = [jnp.exp2(s - top) for s in scores]
    total = functools.reduce(jnp.add, powers)
    inv = 1.0 / total
    return [p * inv for p in powers]


def make_pairs(full, pair_s):
    rows = pair_s.shape[1]
    for t in range(Z):
        f, g = own_feature(t) * rows, shared_feature(t) * rows
        pair_s[t] = jnp.concatenate([full[f : f + rows, :], full[g : g + rows, :]], axis=1)


def read_pairs(pair_refs, full_s):
    for s in range(Z):
        t = partner(s)
        both = pair_refs[s][...].astype(f32)
        full_s[own_feature(t)] += both[:, :D]
        full_s[shared_feature(t)] += both[:, D:]


def feat_forward(rows, cells_ref, cot_ref, count_ref, w_ref, vec_ref, xhat_ref, rstd_ref, qkv_ref, fo_ref, prob_ref, *rest):
    x_refs, cot_out, (pair_s, cot_s, half_s) = rest[:Z], rest[Z], rest[Z + 1 :]
    cells = cells_ref[...]
    for m in range(3):
        qkv_ref[m] = dot(cells, w_ref[m * D : (m + 1) * D, :]).astype(bf16)
    counts = count_ref[...]
    valid = [counts > g for g in range(FEAT)]
    ones = head_ones()
    keys = qkv_ref[1].astype(f32).reshape(FEAT, rows, D)
    values = qkv_ref[2].astype(f32).reshape(FEAT, rows, D)
    for f in range(FEAT):
        at = slice(f * rows, (f + 1) * rows)
        probs = feat_probs(qkv_ref[0, at, :].astype(f32), keys, valid, ones, rows)
        for g in range(FEAT):
            prob_ref[f, g] = probs[g]
        mixed = functools.reduce(jnp.add, [probs[g] * values[g] for g in range(FEAT)])
        fo_ref[at, :] = mixed.astype(bf16)
    z1 = cells.astype(f32) + dot(fo_ref[...], w_ref[3 * D : 4 * D, :]) + vec_ref[6:7, :]
    xhat, rstd = normed(z1)
    xhat_ref[...] = xhat
    rstd_ref[...] = jnp.broadcast_to(rstd, rstd_ref.shape)
    x1 = (xhat * vec_ref[0:1, :] + vec_ref[3:4, :]).astype(bf16)
    make_pairs(x1, pair_s)
    cot = cot_ref[...]
    make_pairs(cot, cot_s)
    for t in range(Z):
        f = own_feature(t) * rows
        half_s[t] = jnp.concatenate([cot[f : f + rows // 2, :], cot[f + rows // 2 : f + rows, :]], axis=1)
    cot_out[...] = cot_s[task_place()]
    for s in range(Z):
        x_refs[s][:rows, :] = pair_s[partner(s)]
    x_refs[1][rows:, :] = cot_s[partner(1)]
    for s in (2, 3):
        x_refs[s][rows:, :] = half_s[partner(s)]


def key_order(h_n):
    h, core = lax.axis_index("zh"), lax.axis_index("core")
    if h_n == 2:
        near = [(h, c, s) for c in (core, 1 - core) for s in range(Z)]
        return near + [(1 - h, c, s) for pair in ((0, 1), (2, 3)) for c in (core, 1 - core) for s in pair]
    return [(a, b, s) for a in range(h_n) for b in range(2) for s in range(Z)]


def item_prepare(h_n, w_ref, code_ref, kv_w_ref, kv_wt_ref, q_w_ref, key_bias_ref, hot_ref):
    zero = jnp.zeros((D, SLOT_COLS), bf16)
    lane_pad = jnp.zeros((D, LANES - SLOT_COLS), bf16)
    mats = []
    for m in range(3):
        w = w_ref[m * D : (m + 1) * D, :]
        a, b = w[:, :SLOT_COLS], w[:, SLOT_COLS:]
        mats.append([(a, zero), (b, zero), (zero, jnp.where(is_odd(), b, a))])
    for p in range(SLOTS):
        for side in range(2):
            at = slice(side * D, (side + 1) * D)
            q_w_ref[p, at, :] = jnp.concatenate([mats[0][p][side], lane_pad], axis=1)
            kv_w_ref[p, at, :LANES] = jnp.concatenate([mats[1][p][side], lane_pad], axis=1)
            kv_w_ref[p, at, LANES:] = jnp.concatenate([mats[2][p][side], lane_pad], axis=1)
        kv_wt_ref[p] = kv_w_ref[p].astype(f32).T.astype(bf16)

    rows = code_ref.shape[1]
    per = LANES // rows
    place = lax.broadcasted_iota(jnp.int32, (LANES, LANES), 0) - SLOT_COLS
    tagged = (place >= 0) & (place < TABLES)

    def code_rows(blocks):
        codes = [code_ref[pl.ds((h * Z + partner(s)) * 2 + c, 1), :] for h, c, s in blocks]
        code = jnp.concatenate(codes, axis=1)
        table = jnp.floor(code * 0.5)
        return table.astype(jnp.int32), code - 2.0 * table

    order = key_order(h_n)
    for i in range(len(order) // per):
        table, train = code_rows(order[i * per : (i + 1) * per])
        match = (place == table) & (train > 0.5)
        bias = jnp.where(tagged, jnp.where(match, 0.0, BLOCKED), 0.0)
        key_bias_ref[span(i, LANES), :] = bias.T.astype(bf16)
    own = [(lax.axis_index("zh"), lax.axis_index("core"), s) for s in range(Z)]
    for i in range(Z // per):
        table, _ = code_rows(own[i * per : (i + 1) * per])
        hot = jnp.where(place == table, 1.0, 0.0)
        hot_ref[span(i, LANES), :] = hot.T


def only_head(a, h, keep_rest):
    lane = lax.broadcasted_iota(jnp.int32, a.shape, 1)
    mine = (lane >= h * HEAD_DIM) & (lane < (h + 1) * HEAD_DIM)
    if keep_rest:
        mine = mine | (lane >= SLOT_COLS)
    return jnp.where(mine, a, jnp.zeros_like(a))


def each_tile(part_refs, body):
    base = 0
    for ref in part_refs:
        size = min(KEY_TILE, ref.shape[0])

        def one(i, carry, ref=ref, base=base, size=size):
            start = base + i * size
            if not isinstance(i, int):
                start = pl.multiple_of(start, size)
            body(ref[span(i, size), :], pl.ds(start, size))

        loop(ref.shape[0] // size, one)
        base += ref.shape[0]


def take(refs, count):
    return refs[:count], refs[count:]


def at_slot(ref, slot, count):
    return ref.at[slot * count : (slot + 1) * count] if isinstance(slot, int) else ref


def when(condition, body):
    if isinstance(condition, bool):
        if condition:
            body()
    else:
        pl.when(condition)(body)


def task_columns(slot, h):
    start = slot * SLOT_COLS + h * HEAD_DIM
    return pl.ds(start if isinstance(slot, int) else pl.multiple_of(start, HEAD_DIM), HEAD_DIM)


def slots_of(grid):
    return [pl.program_id(0)] if grid else list(range(SLOTS))


def task_lanes(slot):
    if isinstance(slot, int):
        return slice(0, 2 * LANES) if slot < 2 else slice(PAIR - 2 * LANES, PAIR)
    return slice(0, PAIR)


def task_feature(slot):
    if isinstance(slot, int):
        return slice(slot // 2 * D, (slot // 2 + 1) * D), [False, True, is_odd()][slot]
    upper = jnp.where(slot == 2, lax.axis_index("y"), slot) == 1
    return pl.ds(pl.multiple_of(lax.div(slot, 2) * D, D), D), upper


def head_rows(h):
    return slice(h * HEAD_DIM, (h + 1) * HEAD_DIM)


def item_forward(n_parts, n_query, first, last, grid, *refs):
    parts, refs = take(refs, n_parts)
    (kv_w_all, kv_wt_all, key_bias_ref), refs = take(refs, 3)
    if first:
        (q_w_all, hot_ref), refs = take(refs, 2)
        query_parts = parts[:n_query]
        if grid:
            query_parts, refs = take(refs, 1)
    else:
        (q_all, top_in, total_in, mixed_in), refs = take(refs, 4)
    (p_all, top_ref), refs = take(refs, 2)
    if first:
        (q_all,), refs = take(refs, 1)
    if last:
        (end_ref, inv_ref, mixed_ref), refs = take(refs, 3)
        io_refs, refs = take(refs, 3)
    elif first:
        (total_ref, mixed_ref), refs = take(refs, 2)
    else:
        (end_ref, total_ref, mixed_ref), refs = take(refs, 3)
    k_s, vt_s, s_s = refs
    keys = k_s.shape[1]
    queries = q_all.shape[1]
    tile = LANES
    fold = (tile // 8, 8, queries)
    slots = slots_of(grid)
    heads = [(i, slot, h) for i, slot in enumerate(slots) for h in range(SLOT_HEADS)]

    queries_low = []
    for i, slot in enumerate(slots):
        kv_w = at_slot(kv_w_all, slot, 1)
        kv_wt = at_slot(kv_wt_all, slot, 1)
        lanes = task_lanes(slot)

        def project(x, at):
            k = dot(x[:, lanes], kv_w[0, lanes, :LANES])
            k_s[i, at, :] = (k + key_bias_ref[at, :].astype(f32)).astype(bf16)
            vt_s[i, :, at] = dot_t(kv_wt[0, LANES:, lanes], x[:, lanes]).astype(bf16)

        each_tile(parts, project)
        q_ref = at_slot(q_all, slot, 1)
        if first:
            q_w = at_slot(q_w_all, slot, 1)
            query = [dot(x[:, lanes], q_w[0, lanes, :]) for x in query_parts]
            query = (jnp.concatenate(query, axis=0) * SCALE2 + hot_ref[...]).astype(bf16)
            q_ref[0] = query
        else:
            query = q_ref[0]
        queries_low.append(query)

    tops = []
    for i, slot, h in heads:
        query_h = only_head(queries_low[i], h, True)

        def score(n, top):
            at = span(n, tile)
            s = dot_t(k_s[i, at, :], query_h)
            s_s[i * SLOT_HEADS + h, at, :] = s
            return jnp.maximum(top, jnp.max(s.reshape(fold), axis=0))

        top = loop(keys // tile, score, jnp.full((8, queries), 2.0 * BLOCKED, f32))
        tops.append(jnp.max(top, axis=0, keepdims=True))

    totals = []
    for (i, slot, h), top in zip(heads, tops):
        p_ref = at_slot(p_all, slot, SLOT_HEADS)

        def power(n, total):
            at = span(n, tile)
            p = jnp.exp2(s_s[i * SLOT_HEADS + h, at, :] - top)
            p_ref[h, at, :] = p.astype(bf16)
            return total + jnp.sum(p.reshape(fold), axis=0)

        total = loop(keys // tile, power, jnp.zeros((8, queries), f32))
        totals.append(jnp.sum(total, axis=0, keepdims=True))

    def clear():
        mixed_ref[...] = jnp.zeros_like(mixed_ref)

    if last:
        when(slots[0] == 0, clear)
    for (i, slot, h), top, total in zip(heads, tops, totals):
        mixed = dot(vt_s[i, head_rows(h), :], at_slot(p_all, slot, SLOT_HEADS)[h])
        head = pl.ds(slot * SLOT_HEADS + h, 1)
        cols = task_columns(slot, h)
        top_ref[head, :] = top
        if not first:
            end = jnp.maximum(top, top_in[head, :])
            now, before = jnp.exp2(top - end), jnp.exp2(top_in[head, :] - end)
            total = total * now + total_in[head, :] * before
            mixed = mixed * now + mixed_in[cols, :] * before
            end_ref[head, :] = end
        elif last:
            end_ref[head, :] = top
        if last:
            inv = 1.0 / total
            inv_ref[head, :] = inv
            mixed_ref[cols, :] = mixed * inv
        else:
            total_ref[head, :] = total
            mixed_ref[cols, :] = mixed

    def finish():
        half = queries // 2
        io_refs[0][...] = mixed_ref[:D, :].T.astype(bf16)
        shared = mixed_ref[D : D + SLOT_COLS, :].T.astype(bf16)
        io_refs[1][...] = shared[:half]
        io_refs[2][...] = shared[half:]

    if last:
        when(slots[-1] == SLOTS - 1, finish)


def item_turn(counts, grid, *refs):
    groups = []
    for count in counts:
        parts, refs = take(refs, count)
        groups.append(parts)
    (kv_w_all, kv_wt_all, q_all), refs = take(refs, 3)
    qt_all, refs = refs[0], refs[1:]
    for slot in slots_of(grid):
        at_slot(qt_all, slot, 1)[0] = at_slot(q_all, slot, 1)[0].astype(f32).T.astype(bf16)
        kv_w = at_slot(kv_w_all, slot, 1)
        kv_wt = at_slot(kv_wt_all, slot, 1)
        lanes = task_lanes(slot)
        for g, parts in enumerate(groups):
            xt_ref, v_all, kt_all = refs[3 * g : 3 * g + 3]
            v_ref, kt_ref = at_slot(v_all, slot, 1), at_slot(kt_all, slot, 1)

            def one(x, at):
                v_ref[0, at, :] = dot(x[:, lanes], kv_w[0, lanes, LANES:]).astype(bf16)
                kt_ref[0, :, at] = dot_t(kv_wt[0, :LANES, lanes], x[:, lanes]).astype(bf16)

            def turn(x, at):
                xt_ref[:, at] = x.astype(f32).T.astype(bf16)

            each_tile(parts, one)
            when(slot == 0, lambda: each_tile(parts, turn))


def swap_halves(w):
    other = jnp.concatenate([w[SLOT_COLS:], w[:SLOT_COLS]], axis=0)
    return jnp.where(is_odd(), other, w)


def row_middle(shared, w_ref, m_ref, vec_ref, *refs):
    w7 = w_ref[...]
    if shared:
        (lo_ref, *cot_refs, mine_ref, came_ref), refs = refs[:5], refs[5:]
        x1 = lo_ref[...].astype(f32)[:, D:]
        cot = [ref[...].astype(f32)[:, D:] for ref in cot_refs]
        io = jnp.concatenate([mine_ref[...].astype(f32), came_ref[...].astype(f32)], axis=1).astype(bf16)
        w7 = swap_halves(w7)
    else:
        (lo_ref, hi_ref, *cot_refs, own_ref), refs = refs[: 3 + Z], refs[3 + Z :]
        x1 = jnp.concatenate([lo_ref[:, :D], hi_ref[:, :D]], axis=0).astype(f32)
        wide = [ref[...].astype(f32) for ref in cot_refs[2:]]
        cot = [ref[:, :D].astype(f32) for ref in cot_refs[:2]] + [b for a in wide for b in (a[:, :D], a[:, D:])]
        io = own_ref[...]
    dz2_ref, low_refs, full_refs, dio_refs = refs[0], refs[1:8], refs[8:12], refs[12:]
    io_ref, dt2_ref, x2_ref, du_ref, hid_ref, dm_ref, cot_ref = low_refs
    xhat3_ref, dz3_ref, xhat2_ref, dx2_ref = full_refs
    cot = jnp.concatenate(cot, axis=0)
    cot_ref[...] = cot.astype(bf16)
    io_ref[...] = io
    xhat2, rstd2 = normed(x1 + dot(io, w7))
    xhat2_ref[...] = xhat2
    x2 = xhat2 * vec_ref[1:2, :] + vec_ref[4:5, :]
    x2_low = x2.astype(bf16)
    x2_ref[...] = x2_low
    up_w = m_ref[:HIDDEN, :]
    down_w = m_ref[HIDDEN:, :]
    up = dot_t(x2_low, up_w)
    c0 = 0.7978845608028654
    c1 = 0.044715
    up2 = up * up
    tanh = jnp.tanh(c0 * up * (1.0 + c1 * up2))
    half_one = 0.5 + 0.5 * tanh
    hid = (up * half_one).astype(bf16)
    hid_ref[...] = hid
    slope = half_one + 0.5 * up * (1.0 - tanh * tanh) * (c0 + 3.0 * c0 * c1 * up2)
    z3 = x2 + dot(hid, down_w) + vec_ref[7:8, :]
    xhat3, rstd3 = normed(z3)
    xhat3_ref[...] = xhat3
    dz3 = norm_back(xhat3, rstd3, vec_ref[2:3, :], cot)
    dz3_ref[...] = dz3
    dm = dz3.astype(bf16)
    dm_ref[...] = dm
    du = (dot_t(dm, down_w) * slope).astype(bf16)
    du_ref[...] = du
    dx2 = dz3 + dot(du, up_w)
    dx2_ref[...] = dx2
    dz2 = norm_back(xhat2, rstd2, vec_ref[1:2, :], dx2)
    dz2_ref[...] = dz2
    dt2 = dz2.astype(bf16)
    dt2_ref[...] = dt2
    dio = dot_t(dt2, w7).astype(bf16)
    if shared:
        dio_refs[0][...] = dio[:, :SLOT_COLS]
        dio_refs[1][...] = dio[:, SLOT_COLS:]
    else:
        dio_refs[0][...] = dio


def item_backward(n_groups, n_outs, first, last, grid, *refs):
    groups = []
    for _ in range(n_groups):
        group, refs = take(refs, 5)
        groups.append(group)
    if first:
        dio_refs, refs = take(refs, 3)
    else:
        (dt_ref, dz2_own, dz2_shared), refs = take(refs, 3)
    (qt_all, iot_ref, end_ref, inv_ref, kv_w_all), refs = take(refs, 5)
    if last:
        (q_w_all,), refs = take(refs, 1)
        if grid:
            (xtq_ref,), refs = take(refs, 1)
    if not first:
        (dq_past, g_past), refs = take(refs, 2)
    if grid:
        gw_ref, dx_ref, dxq_ref, dt_ref, dkv_s, ds_s = refs
    else:
        out_refs, refs = take(refs, n_outs)
        if last:
            gw_ref, dx_ref, dkv_s, ds_s = refs
            dxq_ref = dx_ref.at[:, : qt_all.shape[2]]
        else:
            dt_ref, ds_s, dkv_s, dx_ref = refs
    queries = qt_all.shape[2]

    def start():
        if first:
            dt_ref[:D, :] = dio_refs[0][...].astype(f32).T
            shared = jnp.concatenate([dio_refs[1][...], dio_refs[2][...]], axis=0)
            dt_ref[D : D + SLOT_COLS, :] = shared.astype(f32).T
        dx_ref[...] = jnp.zeros_like(dx_ref)
        if grid:
            dxq_ref[...] = jnp.zeros_like(dxq_ref)
        if last:
            gw_ref[...] = jnp.zeros_like(gw_ref)

    slots = slots_of(grid)
    when(slots[0] == 0, start)
    heads = [(i, slot, h) for i, slot in enumerate(slots) for h in range(SLOT_HEADS)]
    blank = jnp.zeros((HEAD_DIM, queries), bf16)
    base = 0
    grads = []
    for xt_ref, v_all, kt_all, p_all, top_ref in groups:
        keys = v_all.shape[1]
        for i, slot, h in heads:
            head = pl.ds(slot * SLOT_HEADS + h, 1)
            cols = task_columns(slot, h)
            scale = jnp.exp2(top_ref[head, :] - end_ref[head, :]) * inv_ref[head, :]
            scaled = dt_ref[cols, :] * scale
            delta = jnp.sum(scaled * iot_ref[cols, :], axis=0, keepdims=True)
            grad = scaled.astype(bf16)
            grads.append(grad)
            alone = jnp.concatenate([grad if j == h else blank for j in range(LANES // HEAD_DIM)], axis=0)
            v_ref, p_ref = at_slot(v_all, slot, 1), at_slot(p_all, slot, SLOT_HEADS)

            def score(n, carry):
                at = span(n, KEY_TILE)
                dp = dot(v_ref[0, at, :], alone)
                ds = (p_ref[h, at, :].astype(f32) * (dp - delta)).astype(bf16)
                ds_s[i * SLOT_HEADS + h, span(base // KEY_TILE + n, KEY_TILE), :] = ds
                return carry

            loop(keys // KEY_TILE, score, 0)
        base += keys

    if first:
        dq_heads = [jnp.zeros((HEAD_DIM, queries), f32)] * len(heads)
    else:
        dq_heads = [dq_past[n] for n in range(len(heads))]
    base = 0
    for g, (xt_ref, v_all, kt_all, p_all, top_ref) in enumerate(groups):
        keys = v_all.shape[1]
        for n, (i, slot, h) in enumerate(heads):
            kt_ref, p_ref = at_slot(kt_all, slot, 1), at_slot(p_all, slot, SLOT_HEADS)
            grad = grads[g * len(heads) + n]
            query_t = at_slot(qt_all, slot, 1)[0, head_rows(h), :]
            rows_k, rows_v = head_rows(h), slice(LANES + h * HEAD_DIM, LANES + (h + 1) * HEAD_DIM)

            def sums(t, dq_t):
                at, put = span(t, KEY_TILE), span(base // KEY_TILE + t, KEY_TILE)
                ds = ds_s[i * SLOT_HEADS + h, put, :]
                dkv_s[i, rows_v, put] = dot_t(grad, p_ref[h, at, :]).astype(bf16)
                dkv_s[i, rows_k, put] = (dot_t(query_t, ds) * (1.0 / LOG2E)).astype(bf16)
                return dq_t + dot(kt_ref[0, head_rows(h), at], ds) if last else dq_t

            dq_heads[n] = loop(keys // KEY_TILE, sums, dq_heads[n])
        base += keys

    unused = jnp.zeros((LANES - SLOT_COLS, base), bf16)
    for i, slot in enumerate(slots):
        kv_w = at_slot(kv_w_all, slot, 1)
        feature, upper = task_feature(slot)
        dkv_s[i, SLOT_COLS:LANES, :] = unused
        dkv_s[i, LANES + SLOT_COLS :, :] = unused
        base = 0
        g_kv = jnp.zeros((D, 2 * LANES), f32) if first else g_past[i]
        for xt_ref, v_all, kt_all, p_all, top_ref in groups:
            keys = v_all.shape[1]

            def back(n, carry):
                put = span(base // KEY_TILE + n, KEY_TILE)
                dx_ref[feature, put] += dot(kv_w[0, feature, :], dkv_s[i, :, put])
                return carry

            loop(keys // KEY_TILE, back, 0)
            if last:
                g_kv = g_kv + dot_t(xt_ref[feature, :], dkv_s[i, :, base : base + keys])
            base += keys
        if not last:
            continue
        rest = jnp.zeros((LANES - SLOT_COLS, queries), f32)
        dq_t = jnp.concatenate(dq_heads[i * SLOT_HEADS : (i + 1) * SLOT_HEADS] + [rest], axis=0)
        found = [(1, g_kv[:, :LANES]), (2, g_kv[:, LANES:])]
        dq = (dq_t * SCALE).astype(bf16)
        dxq_ref[feature, :] += dot(at_slot(q_w_all, slot, 1)[0, feature, :], dq)
        xq = xtq_ref[feature, :] if grid else groups[0][0][feature, :queries]
        found.append((0, dot_t(xq, dq)))
        blank = jnp.zeros((D, SLOT_COLS), f32)
        for m, g in found:
            g = g[:, :SLOT_COLS]
            if upper is not True:
                g_low = jnp.concatenate([g, blank], axis=1)
            if upper is not False:
                g_high = jnp.concatenate([blank, g], axis=1)
            whole = g_high if upper is True else g_low if upper is False else jnp.where(upper, g_high, g_low)
            gw_ref[m * D : (m + 1) * D, :] += whole

    if not grid:
        base = 0
        for n, ref in enumerate(out_refs):
            count = ref.shape[0]
            total = dx_ref[:, base : base + count].T
            if last and n < 2:
                shared = dz2_shared[...] if n == 0 else jnp.zeros((count, D), f32)
                total = total + jnp.concatenate([dz2_own[base : base + count, :], shared], axis=1)
            ref[...] = total.astype(ref.dtype)
            base += count


def item_far(*refs):
    groups = (refs[:2], refs[2:4])
    ds_ref, dkv_ref, dq_ref, g_ref = refs[4:]
    for slot in range(SLOTS):
        feature, _ = task_feature(slot)
        base = 0
        for xt_ref, kt_ref in groups:
            at = slice(base, base + xt_ref.shape[1])
            g = dot_t(xt_ref[feature, :], dkv_ref[slot, :, at])
            g_ref[slot] = g_ref[slot] + g if base else g
            for h in range(SLOT_HEADS):
                n = slot * SLOT_HEADS + h
                dq = dot(kt_ref[slot, head_rows(h), :], ds_ref[n, at, :])
                dq_ref[n] = dq_ref[n] + dq if base else dq
            base += xt_ref.shape[1]


def feat_backward(rows, xhat1_ref, rstd1_ref, cells_ref, qkv_ref, fo_ref, prob_ref, w_ref, vec_ref, *refs):
    dx_refs, refs = refs[:Z], refs[Z:]
    gw_ref, gvec_ref, dz1_ref, dqkv_ref, dk_s, dv_s, dfo_s, dx_s = refs
    xhat1, rstd1 = xhat1_ref[...], rstd1_ref[...]
    dx_s[...] = jnp.zeros_like(dx_s)
    read_pairs(dx_refs, dx_s)
    dx1 = dx_s[...].reshape(FEAT * rows, D)
    gvec_ref[...] = jnp.zeros_like(gvec_ref)
    gvec_ref[0:1, :] = col_sum(dx1 * xhat1)
    gvec_ref[3:4, :] = col_sum(dx1)
    dz1 = norm_back(xhat1, rstd1, vec_ref[0:1, :], dx1)
    gvec_ref[6:7, :] = col_sum(dz1)
    dz1_ref[...] = dz1
    dt1 = dz1.astype(bf16)
    gw_ref[3 * D : 4 * D, :] = t_dot(fo_ref[...], dt1)
    dfo_s[...] = dot_t(dt1, w_ref[3 * D : 4 * D, :])
    ones = head_ones()
    keys = qkv_ref[1].astype(f32).reshape(FEAT, rows, D)
    values = qkv_ref[2].astype(f32).reshape(FEAT, rows, D)
    dk_s[...] = jnp.zeros_like(dk_s)
    dv_s[...] = jnp.zeros_like(dv_s)
    for f in range(FEAT):
        at = slice(f * rows, (f + 1) * rows)
        query = qkv_ref[0, at, :].astype(f32)
        probs = [prob_ref[f, g] for g in range(FEAT)]
        dfo = dfo_s[at, :].astype(bf16).astype(f32)
        prod = (values * dfo[None]).reshape(FEAT * rows, D).astype(bf16)
        dfp = dot(prod, ones).reshape(FEAT, rows, D)
        mean = functools.reduce(jnp.add, [probs[g] * dfp[g] for g in range(FEAT)])
        dq = jnp.zeros((rows, D), f32)
        for g in range(FEAT):
            here = slice(g * rows, (g + 1) * rows)
            ds = probs[g] * (dfp[g] - mean)
            dq = dq + ds * keys[g]
            dk_s[here, :] += ds * query
            dv_s[here, :] += probs[g] * dfo
        dqkv_ref[0, at, :] = (dq * SCALE).astype(bf16)
    dqkv_ref[1] = (dk_s[...] * SCALE).astype(bf16)
    dqkv_ref[2] = dv_s[...].astype(bf16)
    for m in range(3):
        gw_ref[m * D : (m + 1) * D, :] = t_dot(cells_ref[...], dqkv_ref[m])


def cell_out(dz1_ref, dqkv_ref, w_ref, out_ref):
    total = dz1_ref[...]
    for m in range(3):
        total = total + dot_t(dqkv_ref[m], w_ref[m * D : (m + 1) * D, :])
    out_ref[...] = total


def middle_grads(vec_ref, *refs):
    sets, refs = (refs[:11], refs[11:22]), refs[22:]
    (gw_ref, gu_ref, gv_ref, gvec_ref), out_refs = refs[:4], refs[4:]
    outs = []
    for i, (io_ref, dt2_ref, x2_ref, du_ref, hid_ref, dm_ref, cot_ref, *full_refs) in enumerate(sets):
        xhat3, dz3, xhat2, dx2 = [ref[...] for ref in full_refs]
        cot = cot_ref[...].astype(f32)
        outs.append(xhat3 * vec_ref[2:3, :] + vec_ref[5:6, :])
        gw = t_dot(io_ref[...], dt2_ref[...])
        gu = t_dot(du_ref[...], x2_ref[...])
        gv = t_dot(hid_ref[...], dm_ref[...])
        rows = {1: dx2 * xhat2, 2: cot * xhat3, 4: dx2, 5: cot, 7: dz3}
        if i == 0:
            gw_ref[...], gu_ref[...], gv_ref[...] = gw, gu, gv
            gvec_ref[...] = jnp.zeros_like(gvec_ref)
        else:
            gw_ref[...] += swap_halves(gw)
            gu_ref[...] += gu
            gv_ref[...] += gv
        for k, a in rows.items():
            gvec_ref[k : k + 1, :] += col_sum(a)
    rows = out_refs[0].shape[0]
    for s in range(Z):
        own = outs[0][s * rows : (s + 1) * rows]
        if s < Z // 2:
            sides = [own, outs[1][s * rows : (s + 1) * rows]]
        else:
            sides = [own[: rows // 2], own[rows // 2 :]]
        out_refs[s][...] = jnp.concatenate(sides, axis=1).astype(bf16)


def out_collect(*refs):
    pair_refs, out_ref, full_s = refs[:Z], refs[Z], refs[Z + 1]
    rows = full_s.shape[1]
    for s in range(Z):
        t = partner(s)
        both = pair_refs[s][...]
        if s < Z // 2:
            full_s[own_feature(t)] = both[:, :D]
            full_s[shared_feature(t)] = both[:, D:]
        else:
            full_s[own_feature(t), : rows // 2, :] = both[:, :D]
            full_s[own_feature(t), rows // 2 :, :] = both[:, D:]
    out_ref[...] = full_s[...].reshape(out_ref.shape)


ATTN_ROWS = 48
MLP_ROWS = 24
VEC_PART = 48
PACK = 112
HALF = LANES // 2


def pack_rows(attn, mlp, extra):
    low, high = slice(0, LANES), slice(LANES, D)
    last = jnp.concatenate([extra, mlp[16:24, high]], axis=0)
    return jnp.concatenate(
        [
            attn[:, low],
            jnp.concatenate([attn[:16, high], attn[16:32, high]], axis=1),
            jnp.concatenate([attn[32:, high], last], axis=1),
            mlp[:, low],
            jnp.concatenate([mlp[:8, high], mlp[8:16, high]], axis=1),
        ],
        axis=0,
    )


def unpack_rows(block):
    attn_high = jnp.concatenate([block[48:64, :HALF], block[48:64, HALF:], block[64:80, :HALF]], axis=0)
    mlp_high = jnp.concatenate([block[104:, :HALF], block[104:, HALF:], block[72:80, HALF:]], axis=0)
    attn = jnp.concatenate([block[:48], attn_high], axis=1)
    mlp = jnp.concatenate([block[80:104], mlp_high], axis=1)
    return attn, mlp, block[64:72, HALF:]


def share_pack(*refs):
    sources, out_refs, targets, sems = refs[:6], refs[6 : 6 + Z], refs[6 + Z : 12 + Z], refs[12 + Z]
    copies = [pltpu.make_async_copy(a, b, sems.at[i]) for i, (a, b) in enumerate(zip(sources, targets))]
    for c in copies:
        c.start()
    for c in copies:
        c.wait()
    attn, mlp, vec, tab, train, cnt = [ref[...].astype(f32) for ref in targets]
    code = tab * 2.0 + jnp.where(train > 0, 1.0, 0.0)
    lines = [jnp.concatenate([a, jnp.zeros((1, HALF - a.shape[1]), f32)], axis=1) for a in (vec, cnt)]
    extra = jnp.concatenate([lines[0], code, lines[1], jnp.zeros((5, HALF), f32)], axis=0)
    block = pack_rows(attn, mlp, extra).astype(bf16)
    for ref in out_refs:
        ref[...] = block


def hold(*refs):
    for i in range(3):
        refs[3 + i][...] = refs[i][...]


def at_place(z_step, dy, dc, dr):
    place = (
        lax.bitwise_xor(lax.axis_index("zh") * 2 + lax.axis_index("zl"), FAR_ORDER[z_step]),
        (lax.axis_index("y") + dy) % 2,
        (lax.axis_index("core") + dc) % 2,
        (lax.axis_index("rep") + dr) % 2,
    )
    z, y, c, r = place
    return ((z * 2 + y) * 2 + c) * 2 + r, place


def share_unpack(*refs):
    part_refs, refs = refs[:8], refs[8:]
    attn_ref, mlp_ref, vec_ref, code_ref, count_ref, mlp_s, vec_s = refs
    _, _, extra = unpack_rows(part_refs[0][0].astype(f32))
    table = jnp.floor(extra[1:2] * 0.5)
    counts = jnp.zeros(table.shape, f32)
    for k in range(TABLES):
        counts = jnp.where(table == k, extra[2:3, k : k + 1], counts)
    count_ref[...] = jnp.broadcast_to(row_to_col(counts, table.shape[1]), count_ref.shape)
    for i, ref in enumerate(part_refs):
        dc, dy, dr = i // 4, FAR_ORDER[i % 4] // 2, FAR_ORDER[i % 4] % 2
        for s in range(Z):
            attn, mlp, extra = unpack_rows(ref[s].astype(f32))
            index, (z, y, c, r) = at_place(s, dy, dc, dr)
            attn_ref[pl.ds(pl.multiple_of(index * ATTN_ROWS, 16), ATTN_ROWS), :] = attn.astype(bf16)
            mlp_s[pl.ds(pl.multiple_of(index * MLP_ROWS, 8), MLP_ROWS), :] = mlp
            vec_s[c * 2 + r, pl.ds(z * 2 + y, 1), :] = extra[:1]
            if dr == 0:
                code_ref[pl.ds((z * 2 + y) * 2 + c, 1), :] = extra[1:2]
    mlp_ref[...] = mlp_s[...].astype(bf16)
    vec_ref[...] = jnp.concatenate([vec_s[j][:, :VEC_PART] for j in range(4)], axis=1)


ATTN_PACK = 80
MLP_PACK = 40


def each_share(keep_ref, give_ref, block_of):
    for dc in range(2):
        for plane in range(4):
            for s in range(Z):
                index, place = at_place(s, FAR_ORDER[plane] // 2, dc, FAR_ORDER[plane] % 2)
                block = block_of(index, place)
                if dc == 0:
                    keep_ref[plane, s] = block
                else:
                    give_ref[plane, s] = block.astype(bf16)


def mlp_pack(up_ref, down_ref, keep_ref, give_ref, mlp_s):
    mlp_s[:HIDDEN, :] = up_ref[...]
    mlp_s[HIDDEN:, :] = down_ref[...]

    def block_of(index, _):
        mlp = mlp_s[pl.ds(pl.multiple_of(index * MLP_ROWS, 8), MLP_ROWS), :]
        high = mlp[:, LANES:]
        return jnp.concatenate(
            [
                mlp[:, :LANES],
                jnp.concatenate([high[:8], high[8:16]], axis=1),
                jnp.concatenate([high[16:], jnp.zeros((8, HALF), f32)], axis=1),
            ],
            axis=0,
        )

    each_share(keep_ref, give_ref, block_of)


def grad_pack(feat_ref, item_ref, w7_ref, veca_ref, vecb_ref, keep_ref, give_ref, attn_s, vec_s):
    attn_s[: 4 * D, :] = feat_ref[...]
    attn_s[4 * D : 7 * D, :] = item_ref[...]
    attn_s[7 * D :, :] = w7_ref[...]
    vec = veca_ref[...] + vecb_ref[...]
    for j in range(4):
        part = vec[:, j * VEC_PART : (j + 1) * VEC_PART]
        vec_s[j] = jnp.concatenate([part, jnp.zeros((8, HALF - VEC_PART), f32)], axis=1)

    def block_of(index, place):
        z, y, c, r = place
        attn = attn_s[pl.ds(pl.multiple_of(index * ATTN_ROWS, 8), ATTN_ROWS), :]
        row = vec_s[c * 2 + r, pl.ds(z * 2 + y, 1), :]
        last = jnp.concatenate([row, jnp.zeros((15, HALF), f32)], axis=0)
        high = attn[:, LANES:]
        return jnp.concatenate(
            [
                attn[:, :LANES],
                jnp.concatenate([high[:16], high[16:32]], axis=1),
                jnp.concatenate([high[32:], last], axis=1),
            ],
            axis=0,
        )

    each_share(keep_ref, give_ref, block_of)


def grad_unpack(own_ref, *refs):
    total = own_ref[...]
    for ref in refs[: Z - 1]:
        total = total + ref[...].astype(f32)
    attn_ref, mlp_ref, vec_ref = refs[Z - 1 :]
    high = jnp.concatenate([total[48:64, :HALF], total[48:64, HALF:], total[64:80, :HALF]], axis=0)
    attn_ref[...] = jnp.concatenate([total[:48], high], axis=1)
    vec_ref[...] = total[64:65, HALF : HALF + VEC_PART]
    mlp = total[ATTN_PACK:]
    high = jnp.concatenate([mlp[24:32, :HALF], mlp[24:32, HALF:], mlp[32:, :HALF]], axis=0)
    mlp_ref[...] = jnp.concatenate([mlp[:24], high], axis=1)


VMEM = pl.BlockSpec(memory_space=pltpu.VMEM)
SMEM = pl.BlockSpec(memory_space=pltpu.SMEM)


def like(shape, kind=f32):
    return jax.ShapeDtypeStruct(shape, kind)


def swap(a, axis):
    return lax.ppermute(a, axis, [(0, 1), (1, 0)])


def exchange(a, axes):
    return lax.all_to_all(a, axes, 0, 0, tiled=True)


def along(axes, blocks):
    order = TASK_ORDER if axes == TASK_AXES else FAR_ORDER
    return blocks[:1] + [
        lax.ppermute(a, axes, [(i, i ^ x) for i in range(Z)]) for a, x in zip(blocks[1:], order[1:])
    ]


def gather_any(w_attn, w_mlp, vectors, table_ids, train_mask, feat_count, cells, cot, _):
    rows = table_ids.shape[1]
    fan, reps = lax.axis_size(FAN), lax.axis_size("rep")
    core = lax.axis_index("core")
    ra, rm, nv = w_attn.shape[0], w_mlp.shape[0], vectors.shape[0]
    code = (table_ids * 2 + (train_mask > 0)).astype(bf16)[0]
    last = jnp.pad(jnp.concatenate([vectors, code]), (0, D - nv - rows)).reshape(1, D)
    block = jnp.concatenate([w_attn, w_mlp, last], axis=0)
    rb = ra + rm + 1
    mine = exchange(jnp.broadcast_to(block[None], (fan, rb, D)), FAN)
    other = swap(mine, "core")
    both = jnp.stack([jnp.where(core == 0, mine, other), jnp.where(core == 0, other, mine)], axis=1)
    both = both.reshape(fan // reps, reps, 2, rb, D).transpose(0, 2, 1, 3, 4)
    attn = both[..., :ra, :].reshape(8 * D, D)
    mlp = both[..., ra : ra + rm, :].reshape(2 * HIDDEN, D)
    tail = both[..., ra + rm, :]
    vec = tail[..., :nv].reshape(8, D).astype(f32)
    codes = lax.dynamic_index_in_dim(tail[..., nv : nv + rows], lax.axis_index("rep"), 2, keepdims=False)
    hit = table_ids[0][:, None] == jnp.arange(TABLES)[None, :]
    counts = jnp.sum(jnp.where(hit, feat_count, 0), axis=1, keepdims=True).astype(f32)
    counts = jnp.broadcast_to(counts, (rows, D))
    return attn, mlp, vec, codes.reshape(-1, rows).astype(f32), counts, cells, cot


def gather_packed(w_attn, w_mlp, vectors, table_ids, train_mask, feat_count, cells, cot, limit):
    shares = (w_attn, w_mlp, vectors[None], table_ids, train_mask, feat_count)
    blocks = pl.pallas_call(
        share_pack,
        out_shape=(like((PACK, LANES), bf16),) * Z,
        in_specs=[pl.BlockSpec(memory_space=pl.ANY)] * 6,
        out_specs=(VMEM,) * Z,
        scratch_shapes=[pltpu.VMEM(a.shape, a.dtype) for a in shares] + [pltpu.SemaphoreType.DMA((6,))],
        compiler_params=pltpu.CompilerParams(vmem_limit_bytes=67000000),
        name="share_pack",
    )(*shares)
    *held, block_held = pl.pallas_call(
        hold,
        out_shape=(like(cells.shape, bf16), like(cells.shape, bf16), like((PACK, LANES), bf16)),
        in_specs=[VMEM] * 3,
        out_specs=(VMEM,) * 3,
        compiler_params=limit,
        name="hold",
    )(cells, cot, blocks[0])
    own = jnp.stack([block_held] + along(Z_AXES, list(blocks))[1:])
    own, held = lax.optimization_barrier((own, held))
    plane = along(PLANE_AXES, [own] * 4)
    *shares, counts = pl.pallas_call(
        share_unpack,
        out_shape=(
            like((8 * D, D), bf16),
            like((2 * HIDDEN, D), bf16),
            like((8, D)),
            like((4 * Z, table_ids.shape[1])),
            like((table_ids.shape[1], D)),
        ),
        in_specs=[VMEM] * 8,
        out_specs=(VMEM,) * 5,
        scratch_shapes=[pltpu.VMEM((2 * HIDDEN, D), f32), pltpu.VMEM((4, 8, HALF), f32)],
        compiler_params=limit,
        name="share_unpack",
    )(*plane, *[swap(a, "core") for a in plane])
    return *shares, counts, *held


def sum_any(grads, share, later, _):
    g_feat, g_item, g_w7, g_up, g_down, g_vec_a, g_vec_b = grads
    ra, rm, nv = share
    rb = ra + rm + 1
    fan, reps = lax.axis_size(FAN), lax.axis_size("rep")
    core = lax.axis_index("core")
    spread = (fan // reps, 2, reps)
    g_attn = jnp.concatenate([g_feat, g_item, g_w7], axis=0).reshape(spread + (ra, D))
    g_mlp = jnp.concatenate([g_up, g_down], axis=0).reshape(spread + (rm, D))
    g_vec = (g_vec_a + g_vec_b).reshape(spread + (1, nv))
    g_vec = jnp.pad(g_vec, ((0, 0),) * 4 + ((0, D - nv),))
    g_all = jnp.concatenate([g_attn, g_mlp, g_vec], axis=3)
    keep = lax.dynamic_index_in_dim(g_all, core, 1, keepdims=False)
    give = lax.dynamic_index_in_dim(g_all, 1 - core, 1, keepdims=False)
    chip = keep + swap(give.astype(bf16), "core").astype(f32)
    shares = exchange(chip.astype(bf16).reshape(fan, rb, D), FAN)
    total = jnp.sum(shares.astype(f32), axis=0)
    return total[:ra], total[ra : ra + rm], total[ra + rm, :nv], later


def over_plane(keep, got):
    sent = [keep[0]] + [(keep[i] + got[i]).astype(bf16) for i in range(1, 4)]
    return keep[0] + got[0], along(PLANE_AXES, sent)[1:]


def pack_call(kernel, grads, rows, scratch, limit, name):
    return pl.pallas_call(
        kernel,
        out_shape=(like((4, Z, rows, LANES)), like((4, Z, rows, LANES), bf16)),
        in_specs=[VMEM] * len(grads),
        out_specs=(VMEM,) * 2,
        scratch_shapes=scratch,
        compiler_params=limit,
        name=name,
    )(*grads)


def sum_packed(grads, mlp_total, share, later, limit):
    ra, rm, nv = share
    scratch = [pltpu.VMEM((8 * D, D), f32), pltpu.VMEM((4, 8, HALF), f32)]
    keep, give = pack_call(grad_pack, grads, ATTN_PACK, scratch, limit, "grad_pack")
    total, came = over_plane(keep, swap(give, "core").astype(f32))
    for a in came:
        total = total + a.astype(f32)
    total = jnp.concatenate([total, mlp_total], axis=1)
    steps = [total[0]] + [total[i].astype(bf16) for i in range(1, Z)]
    steps, later = lax.optimization_barrier((steps, later))
    attn, mlp, vec = pl.pallas_call(
        grad_unpack,
        out_shape=(like((ra, D)), like((rm, D)), like((1, nv))),
        in_specs=[VMEM] * Z,
        out_specs=(VMEM,) * 3,
        compiler_params=limit,
        name="grad_unpack",
    )(*along(Z_AXES, steps))
    return attn, mlp, vec.reshape(nv), later


def local(cell_values, table_ids, train_mask, feat_count, w_attn, w_mlp, vectors, cotangent):
    rows = cell_values.shape[1]
    cells_n = rows * FEAT
    h_n = lax.axis_size("zh")
    fast = h_n == 2
    all_rows = Z * h_n * 2 * rows
    q_rows = Z * rows
    small = pltpu.CompilerParams(vmem_limit_bytes=16 * 2**20)
    limit = small if fast else pltpu.CompilerParams(vmem_limit_bytes=63 * 2**20)

    cells = cell_values[0].transpose(1, 0, 2).reshape(cells_n, D)
    cot = cotangent[0].transpose(1, 0, 2).reshape(cells_n, D)

    shares = gather_packed if fast else gather_any
    attn, mlp, vec, codes, counts, cells, cot = shares(
        w_attn, w_mlp, vectors, table_ids, train_mask, feat_count, cells, cot, small
    )

    pair_block = like((rows, PAIR), bf16)
    half_rows = rows + rows // 2
    xhat1, rstd1, qkv, fo, probs, *x_out, cot_own = pl.pallas_call(
        functools.partial(feat_forward, rows),
        out_shape=(
            like((cells_n, D)),
            like((cells_n, D)),
            like((3, cells_n, D), bf16),
            like((cells_n, D), bf16),
            like((FEAT, FEAT, rows, D)),
            pair_block,
            like((2 * rows, PAIR), bf16),
            like((half_rows, PAIR), bf16),
            like((half_rows, PAIR), bf16),
            pair_block,
        ),
        in_specs=[VMEM] * 5,
        out_specs=(VMEM,) * 10,
        scratch_shapes=[
            pltpu.VMEM((Z, rows, PAIR), bf16),
            pltpu.VMEM((Z, rows, PAIR), bf16),
            pltpu.VMEM((Z, rows // 2, PAIR), bf16),
        ],
        compiler_params=small,
        name="feat_forward",
    )(cells, cot, counts, attn[: 4 * D], vec)

    def whole(*shape):
        return pl.BlockSpec(shape, lambda i: (0,) * len(shape))

    def by_slot(*shape):
        once = {"pipeline_mode": pl.Buffered(1)} if math.prod(shape) > 2**22 else {}
        return pl.BlockSpec(shape, lambda i: (i,) + (0,) * (len(shape) - 1), **once)

    def item_call(kernel, ins, outs, scratch, name):
        def specs(pairs):
            if fast:
                return [VMEM] * len(pairs)
            return [by_slot(a.shape[0] // SLOTS, *a.shape[1:]) if by else whole(*a.shape) for a, by in pairs]

        return pl.pallas_call(
            kernel,
            out_shape=[a for a, _ in outs],
            in_specs=specs(ins),
            out_specs=specs(outs),
            scratch_shapes=scratch,
            compiler_params=limit,
            cost_estimate=pl.CostEstimate(flops=10**8, bytes_accessed=0, transcendentals=0),
            name=name,
            **({} if fast else {"grid": (SLOTS,)}),
        )(*[a for a, _ in ins])

    def shared(*arrays):
        return [(a, False) for a in arrays]

    def tasked(*arrays):
        return [(a, True) for a in arrays]

    heads_block, pair_t = like((16, q_rows)), like((PAIR, q_rows))

    def forward_call(parts, bias, first, last, extra):
        keys = sum(a.shape[0] for a in parts)
        tasks = SLOTS if fast else 1
        outs = tasked(like((SLOTS * SLOT_HEADS, keys, q_rows), bf16)) + shared(heads_block)
        if first:
            outs += tasked(like((SLOTS, q_rows, LANES), bf16))
        if last:
            half_heads = like((q_rows // 2, SLOT_COLS), bf16)
            outs += shared(heads_block, heads_block, pair_t, like((q_rows, D), bf16), half_heads, half_heads)
        else:
            outs += shared(*([heads_block] * (1 if first else 2)), pair_t)
        scratch = [
            pltpu.VMEM((tasks, keys, LANES), bf16),
            pltpu.VMEM((tasks, LANES, keys), bf16),
            pltpu.VMEM((tasks * SLOT_HEADS, keys, q_rows), f32),
        ]
        kernel = functools.partial(item_forward, len(parts), 2, first, last, not fast)
        ins = shared(*parts) + tasked(kv_w, kv_wt) + shared(bias) + extra
        return item_call(kernel, ins, outs, scratch, "item_forward")

    def turn_call(groups, query):
        outs = tasked(like((SLOTS, LANES, q_rows), bf16))
        for parts in groups:
            keys = sum(a.shape[0] for a in parts)
            outs += shared(like((PAIR, keys), bf16))
            outs += tasked(like((SLOTS, keys, LANES), bf16), like((SLOTS, LANES, keys), bf16))
        kernel = functools.partial(item_turn, [len(g) for g in groups], not fast)
        ins = shared(*sum(groups, [])) + tasked(kv_w, kv_wt, query)
        query_t, *rest = item_call(kernel, ins, outs, [], "item_turn")
        return query_t, [tuple(rest[i : i + 3]) for i in range(0, len(rest), 3)]

    def backward_call(groups, parts, first, last, grads, extra):
        keys = sum(g[1].shape[1] for g in groups)
        tasks = SLOTS if fast else 1
        kv_shape, ds_shape = (tasks, 2 * LANES, keys), (tasks * SLOT_HEADS, keys, q_rows)
        scratch = [pltpu.VMEM(kv_shape, bf16), pltpu.VMEM(ds_shape, bf16)]
        if fast:
            outs = shared(*parts)
            outs += shared(like((3 * D, D))) if last else shared(pair_t, like(ds_shape, bf16), like(kv_shape, bf16))
            scratch = [pltpu.VMEM((PAIR, keys), f32)] + (scratch if last else [])
        else:
            outs = shared(like((3 * D, D)), *parts)
            scratch = [pltpu.VMEM((PAIR, q_rows), f32)] + scratch
        ins = []
        for xt, v, kt, p, top in groups:
            ins += shared(xt) + tasked(v, kt, p) + shared(top)
        ins += shared(*grads) + tasked(query_t) + shared(io_t, end, inv) + tasked(kv_w) + extra
        kernel = functools.partial(item_backward, len(groups), len(parts), first, last, not fast)
        return item_call(kernel, ins, outs, scratch, "item_backward")

    kv_w, kv_wt, q_w, key_bias, hot = pl.pallas_call(
        functools.partial(item_prepare, h_n),
        out_shape=(
            like((SLOTS, PAIR, 2 * LANES), bf16),
            like((SLOTS, 2 * LANES, PAIR), bf16),
            like((SLOTS, PAIR, LANES), bf16),
            like((all_rows, LANES), bf16),
            like((q_rows, LANES)),
        ),
        in_specs=[VMEM] * 2,
        out_specs=(VMEM,) * 5,
        compiler_params=limit,
        name="item_prepare",
    )(attn[4 * D : 7 * D], codes)

    def to_task(block, i):
        return lax.ppermute(block, TASK_AXES, [(j, j ^ TASK_ORDER[i]) for j in range(Z)])

    came = [to_task(x_out[i], i) for i in range(1, Z)]
    x_lo = jnp.concatenate([x_out[0], came[0][:rows]], axis=0)
    came[1:], _ = lax.optimization_barrier((came[1:], x_lo))
    x_hi = jnp.concatenate([a[:rows] for a in came[1:]], axis=0)
    cot_in = [cot_own] + [a[rows:] for a in came]
    if fast:
        h_lo, h_hi = swap(x_lo, "zh"), swap(x_hi, "zh")
        near = [x_lo, x_hi, swap(x_lo, "core"), swap(x_hi, "core")]
        ends = (0, 2 * q_rows, 3 * q_rows, 4 * q_rows)
        bias = [key_bias[a:b] for a, b in zip(ends, ends[1:])]
        near_p, near_top, query, total, mixed = forward_call(
            near, bias[0], True, False, tasked(q_w) + shared(hot)
        )
        h_lo, total = lax.optimization_barrier((h_lo, total))
        far_lo = [h_lo, swap(h_lo, "core")]
        lo_p, lo_top, end, total, mixed = forward_call(
            far_lo, bias[1], False, False, tasked(query) + shared(near_top, total, mixed)
        )
        h_hi, total = lax.optimization_barrier((h_hi, total))
        far_hi = [h_hi, swap(h_hi, "core")]
        hi_p, hi_top, end, inv, io_t, io_own, io_mine, io_give = forward_call(
            far_hi, bias[2], False, True, tasked(query) + shared(end, total, mixed)
        )
    else:
        x_q = jnp.concatenate([x_lo, x_hi], axis=0)
        parts = [lax.all_gather(x_q, ("zh", "core"), axis=0, tiled=True)]
        all_p, all_top, query, end, inv, io_t, io_own, io_mine, io_give = forward_call(
            parts, key_bias, True, True, tasked(q_w) + shared(hot, x_q)
        )

    def to_shared(block):
        return lax.ppermute(block, "y", [(0, 1), (1, 0)])

    io_came = to_shared(io_give)
    query, _ = lax.optimization_barrier((query, io_give))
    query_t, turned = turn_call([near, far_lo, far_hi] if fast else [parts], query)

    cells_low = like((cells_n, D), bf16)

    def middle_call(shared, ins, dio_shapes):
        count = q_rows // 2 if shared else q_rows
        low, full, hidden = like((count, D), bf16), like((count, D)), like((count, HIDDEN), bf16)
        dz2, *outs = pl.pallas_call(
            functools.partial(row_middle, shared),
            out_shape=[full] + [low] * 3 + [hidden] * 2 + [low] * 2 + [full] * 4 + dio_shapes,
            in_specs=[VMEM] * (3 + len(ins)),
            out_specs=[VMEM] * (12 + len(dio_shapes)),
            compiler_params=small,
            name="row_middle",
        )(attn[7 * D :], mlp, vec, *ins)
        return dz2, outs[:11], outs[11:]

    half_heads = like(io_mine.shape, bf16)
    dz2_own, kept, (dio_own,) = middle_call(False, [x_lo, x_hi, *cot_in, io_own], [like(io_own.shape, bf16)])
    io_came, dio_own = lax.optimization_barrier((io_came, dio_own))
    dz2_shared, kept_shared, (dio_mine, dio_give) = middle_call(
        True, [x_lo, *cot_in[:2], io_mine, io_came], [half_heads] * 2
    )
    dz2, kept = (dz2_own, dz2_shared), kept + kept_shared
    dio_in = [dio_own, dio_mine, to_shared(dio_give)]

    def rest_of_middle(kept):
        return pl.pallas_call(
            middle_grads,
            out_shape=(like((D, D)), like((HIDDEN, D)), like((HIDDEN, D)), like((8, D)))
            + (pair_block,) * 2
            + (like((rows // 2, PAIR), bf16),) * 2,
            in_specs=[VMEM] * 23,
            out_specs=(VMEM,) * (4 + Z),
            compiler_params=small,
            name="middle_grads",
        )(vec, *kept)

    if fast:
        half_f, half_b = like((2 * rows, PAIR)), like((2 * rows, PAIR), bf16)
        near, far_lo, far_hi = (t + s for t, s in zip(turned, ((near_p, near_top), (lo_p, lo_top), (hi_p, hi_top))))
        g_w7, g_up, g_down, g_vec_b, *out_blocks = rest_of_middle(kept)
        mlp_keep, mlp_give = pack_call(
            mlp_pack, (g_up, g_down), MLP_PACK, [pltpu.VMEM((2 * HIDDEN, D), f32)], small, "mlp_pack"
        )
        dio_in[2], mlp_give = lax.optimization_barrier((dio_in[2], mlp_give))
        lo_h, lo_hc, hi_h, hi_hc, dio_t, ds, dkv = backward_call(
            [far_lo, far_hi], (half_f, half_b) * 2, True, False, dio_in, []
        )
        dq_far, g_far = pl.pallas_call(
            item_far,
            out_shape=(like((SLOTS * SLOT_HEADS, HEAD_DIM, q_rows)), like((SLOTS, D, 2 * LANES))),
            in_specs=[VMEM] * 6,
            out_specs=(VMEM,) * 2,
            compiler_params=small,
            name="item_far",
        )(far_lo[0], far_lo[2], far_hi[0], far_hi[2], ds, dkv)
        from_c = [swap(a, "core") for a in (lo_hc, hi_hc)]
        from_c, dq_far = lax.optimization_barrier((from_c, dq_far))
        sent = [(a + b.astype(f32)).astype(bf16) for a, b in zip((lo_h, hi_h), from_c)]
        sent, dio_t, mlp_give = lax.optimization_barrier((sent, dio_t, mlp_give))
        from_h = [swap(a, "zh") for a in sent]
        mlp_got = swap(mlp_give, "core")
        *own, lo_c, hi_c, g_item = backward_call(
            [near],
            (half_f,) * 2 + (half_b,) * 2,
            False,
            True,
            [dio_t, *dz2],
            tasked(q_w) + shared(dq_far, g_far),
        )
        mlp_got, g_item = lax.optimization_barrier((mlp_got, g_item))
        mlp_total, mlp_came = over_plane(mlp_keep, mlp_got.astype(f32))
        from_h, to_c, out_blocks, mlp_came = lax.optimization_barrier((from_h, (lo_c, hi_c), out_blocks, mlp_came))
        for a in mlp_came:
            mlp_total = mlp_total + a.astype(f32)
        from_c = [swap(a, "core") for a in to_c]
        own = [(a + b.astype(f32) + c.astype(f32)).astype(bf16) for a, b, c in zip(own, from_c, from_h)]
    else:
        (xt, v, kt), = turned
        at_query = (lax.axis_index("zh") * 2 + lax.axis_index("core")) * q_rows
        xt_q = lax.dynamic_slice_in_dim(xt, at_query, q_rows, 1)
        g_item, dx_t, dxq_t = backward_call(
            [(xt, v, kt, all_p, all_top)],
            (like((PAIR, all_rows)), like((PAIR, q_rows))),
            True,
            True,
            dio_in,
            tasked(q_w) + shared(xt_q),
        )
        own = lax.psum_scatter(dx_t.T, ("zh", "core"), scatter_dimension=0, tiled=True) + dxq_t.T
        own = own + jnp.concatenate([dz2[0], jnp.pad(dz2[1], ((0, q_rows // 2), (0, 0)))], axis=1)
        own = jnp.split(own.astype(bf16), 2)
        g_w7, g_up, g_down, g_vec_b, *out_blocks = rest_of_middle(kept)
    dx_blocks = [own[s // 2][s % 2 * rows : (s % 2 + 1) * rows] for s in range(Z)]
    came = [to_task(jnp.concatenate([a, b], axis=0), i) for i, (a, b) in enumerate(zip(dx_blocks, out_blocks)) if i]
    dx_in = dx_blocks[:1] + [a[:rows] for a in came]
    out = pl.pallas_call(
        out_collect,
        out_shape=cells_low,
        in_specs=[VMEM] * Z,
        out_specs=VMEM,
        scratch_shapes=[pltpu.VMEM((FEAT, rows, D), bf16)],
        compiler_params=small,
        name="out_collect",
    )(out_blocks[0], *[a[rows:] for a in came])

    g_feat, g_vec_a, dz1, dqkv = pl.pallas_call(
        functools.partial(feat_backward, rows),
        out_shape=(like((4 * D, D)), like((8, D)), like((cells_n, D)), like((3, cells_n, D), bf16)),
        in_specs=[VMEM] * (8 + Z),
        out_specs=(VMEM,) * 4,
        scratch_shapes=[
            pltpu.VMEM((cells_n, D), f32),
            pltpu.VMEM((cells_n, D), f32),
            pltpu.VMEM((cells_n, D), f32),
            pltpu.VMEM((FEAT, rows, D), f32),
        ],
        compiler_params=small,
        name="feat_backward",
    )(xhat1, rstd1, cells, qkv, fo, probs, attn[: 4 * D], vec, *dx_in)

    share = (w_attn.shape[0], w_mlp.shape[0], vectors.shape[0])
    if fast:
        grads = (g_feat, g_item, g_w7, g_vec_a, g_vec_b)
        attn_share, mlp_share, vec_share, dz1 = sum_packed(grads, mlp_total, share, dz1, small)
    else:
        grads = (g_feat, g_item, g_w7, g_up, g_down, g_vec_a, g_vec_b)
        attn_share, mlp_share, vec_share, dz1 = sum_any(grads, share, dz1, small)

    dcell = pl.pallas_call(
        cell_out,
        out_shape=like((cells_n, D)),
        in_specs=[VMEM] * 3,
        out_specs=VMEM,
        compiler_params=small,
        name="cell_out",
    )(dz1, dqkv, attn[: 3 * D])

    def rows_first(a):
        return a.reshape(FEAT, rows, D).transpose(1, 0, 2)[None]

    return (
        rows_first(out),
        rows_first(dcell),
        attn_share,
        mlp_share,
        vec_share,
    )


def solution(mesh):
    blk_n, rep_n = mesh.devices.shape
    fine = Mesh(mesh.devices.reshape(blk_n // (2 * Z), 2, 2, 2, rep_n), BLK + ("rep",))
    every = BLK + ("rep",)
    in_specs = (
        P("rep", BLK, None, None),
        P("rep", BLK),
        P("rep", BLK),
        P("rep", None),
        P(every, None),
        P(every, None),
        P(every),
        P("rep", BLK, None, None),
    )
    out_specs = (
        P("rep", BLK, None, None),
        P("rep", BLK, None, None),
        P(every, None),
        P(every, None),
        P(every),
    )
    return jax.shard_map(local, mesh=fine, in_specs=in_specs, out_specs=out_specs, check_vma=False)
```

```python
import functools
import math

import jax
import jax.numpy as jnp
from jax import lax
from jax.experimental import pallas as pl
from jax.experimental.pallas import tpu as pltpu
from jax.sharding import Mesh
from jax.sharding import PartitionSpec as P

D = 192
HEADS = 6
HEAD_DIM = 32
HIDDEN = 384
FEAT = 6
TABLES = 16

Z = 4
SLOTS = 3
SLOT_HEADS = 3
SLOT_COLS = SLOT_HEADS * HEAD_DIM
PAIR = 2 * D
LANES = 128
KEY_TILE = 256

EPS = 1e-05
FAR = -1e30
BLOCKED = -(2.0**100)
SCALE = HEAD_DIM ** (-0.5)
LOG2E = 1.4426950408889634
SCALE2 = SCALE * LOG2E

bf16 = jnp.bfloat16
f32 = jnp.float32
BLK = ("zh", "zl", "y", "core")
FAN = ("zh", "zl", "y", "rep")
TASK_AXES = ("zl", "y")
Z_AXES = ("zh", "zl")
PLANE_AXES = ("y", "rep")
TASK_ORDER = (0, 2, 1, 3)
FAR_ORDER = (0, 3, 2, 1)


def dot(a, b):
    return lax.dot_general(a, b, (((1,), (0,)), ((), ())), preferred_element_type=f32)


def dot_t(a, b):
    return lax.dot_general(a, b, (((1,), (1,)), ((), ())), preferred_element_type=f32)


def t_dot(a, b):
    return lax.dot_general(a, b, (((0,), (0,)), ((), ())), preferred_element_type=f32)


def loop(count, body, carry=None):
    if count > 8:
        return lax.fori_loop(0, count, body, carry)
    for i in range(count):
        carry = body(i, carry)
    return carry


def span(i, size):
    if isinstance(i, int):
        return slice(i * size, (i + 1) * size)
    return pl.ds(pl.multiple_of(i * size, size), size)


def task_place():
    return lax.axis_index("zl") * 2 + lax.axis_index("y")


def partner(step):
    return lax.bitwise_xor(task_place(), TASK_ORDER[step])


def own_feature(t):
    return (3 * t + 1) // 2 if isinstance(t, int) else lax.div(3 * t + 1, 2)


def shared_feature(t):
    return 1 + 3 * (t // 2) if isinstance(t, int) else 1 + 3 * lax.div(t, 2)


def is_odd():
    return lax.axis_index("y") == 1


def normed(z):
    centre = z - jnp.mean(z, axis=-1, keepdims=True)
    rstd = lax.rsqrt(jnp.mean(centre * centre, axis=-1, keepdims=True) + EPS)
    return centre * rstd, rstd


def norm_back(xhat, rstd, gain, grad):
    scaled = grad * gain
    mean_a = jnp.mean(scaled, axis=-1, keepdims=True)
    mean_b = jnp.mean(scaled * xhat, axis=-1, keepdims=True)
    return rstd * (scaled - mean_a - xhat * mean_b)


def col_sum(a):
    return jnp.sum(a, axis=0, keepdims=True)


def head_ones():
    a = lax.broadcasted_iota(jnp.int32, (D, D), 0) // HEAD_DIM
    b = lax.broadcasted_iota(jnp.int32, (D, D), 1) // HEAD_DIM
    return (a == b).astype(bf16)


def row_to_col(row, size):
    a = lax.broadcasted_iota(jnp.int32, (size, size), 0)
    b = lax.broadcasted_iota(jnp.int32, (size, size), 1)
    return jnp.sum(jnp.where(a == b, row, 0.0), axis=1, keepdims=True)


def feat_probs(query, keys, valid, ones, rows):
    prod = (keys * query[None]).reshape(FEAT * rows, D).astype(bf16)
    scores = dot(prod, ones).reshape(FEAT, rows, D)
    scores = [jnp.where(valid[g], scores[g] * SCALE2, FAR) for g in range(FEAT)]
    top = functools.reduce(jnp.maximum, scores)
    powers = [jnp.exp2(s - top) for s in scores]
    total = functools.reduce(jnp.add, powers)
    inv = 1.0 / total
    return [p * inv for p in powers]


def make_pairs(full, pair_s):
    rows = pair_s.shape[1]
    for t in range(Z):
        f, g = own_feature(t) * rows, shared_feature(t) * rows
        pair_s[t] = jnp.concatenate([full[f : f + rows, :], full[g : g + rows, :]], axis=1)


def read_pairs(pair_refs, full_s):
    for s in range(Z):
        t = partner(s)
        both = pair_refs[s][...].astype(f32)
        full_s[own_feature(t)] += both[:, :D]
        full_s[shared_feature(t)] += both[:, D:]


def feat_forward(rows, cells_ref, cot_ref, count_ref, w_ref, vec_ref, xhat_ref, rstd_ref, qkv_ref, fo_ref, prob_ref, *rest):
    x_refs, cot_out, (pair_s, cot_s, half_s) = rest[:Z], rest[Z], rest[Z + 1 :]
    cells = cells_ref[...]
    for m in range(3):
        qkv_ref[m] = dot(cells, w_ref[m * D : (m + 1) * D, :]).astype(bf16)
    counts = count_ref[...]
    valid = [counts > g for g in range(FEAT)]
    ones = head_ones()
    keys = qkv_ref[1].astype(f32).reshape(FEAT, rows, D)
    values = qkv_ref[2].astype(f32).reshape(FEAT, rows, D)
    for f in range(FEAT):
        at = slice(f * rows, (f + 1) * rows)
        probs = feat_probs(qkv_ref[0, at, :].astype(f32), keys, valid, ones, rows)
        for g in range(FEAT):
            prob_ref[f, g] = probs[g]
        mixed = functools.reduce(jnp.add, [probs[g] * values[g] for g in range(FEAT)])
        fo_ref[at, :] = mixed.astype(bf16)
    z1 = cells.astype(f32) + dot(fo_ref[...], w_ref[3 * D : 4 * D, :]) + vec_ref[6:7, :]
    xhat, rstd = normed(z1)
    xhat_ref[...] = xhat
    rstd_ref[...] = jnp.broadcast_to(rstd, rstd_ref.shape)
    x1 = (xhat * vec_ref[0:1, :] + vec_ref[3:4, :]).astype(bf16)
    make_pairs(x1, pair_s)
    cot = cot_ref[...]
    make_pairs(cot, cot_s)
    for t in range(Z):
        f = own_feature(t) * rows
        half_s[t] = jnp.concatenate([cot[f : f + rows // 2, :], cot[f + rows // 2 : f + rows, :]], axis=1)
    cot_out[...] = cot_s[task_place()]
    for s in range(Z):
        x_refs[s][:rows, :] = pair_s[partner(s)]
    x_refs[1][rows:, :] = cot_s[partner(1)]
    for s in (2, 3):
        x_refs[s][rows:, :] = half_s[partner(s)]


def key_order(h_n):
    h, core = lax.axis_index("zh"), lax.axis_index("core")
    if h_n == 2:
        near = [(h, c, s) for c in (core, 1 - core) for s in range(Z)]
        return near + [(1 - h, c, s) for pair in ((0, 1), (2, 3)) for c in (core, 1 - core) for s in pair]
    return [(a, b, s) for a in range(h_n) for b in range(2) for s in range(Z)]


def item_prepare(h_n, w_ref, code_ref, kv_w_ref, kv_wt_ref, q_w_ref, key_bias_ref, hot_ref):
    zero = jnp.zeros((D, SLOT_COLS), bf16)
    lane_pad = jnp.zeros((D, LANES - SLOT_COLS), bf16)
    mats = []
    for m in range(3):
        w = w_ref[m * D : (m + 1) * D, :]
        a, b = w[:, :SLOT_COLS], w[:, SLOT_COLS:]
        mats.append([(a, zero), (b, zero), (zero, jnp.where(is_odd(), b, a))])
    for p in range(SLOTS):
        for side in range(2):
            at = slice(side * D, (side + 1) * D)
            q_w_ref[p, at, :] = jnp.concatenate([mats[0][p][side], lane_pad], axis=1)
            kv_w_ref[p, at, :LANES] = jnp.concatenate([mats[1][p][side], lane_pad], axis=1)
            kv_w_ref[p, at, LANES:] = jnp.concatenate([mats[2][p][side], lane_pad], axis=1)
        kv_wt_ref[p] = kv_w_ref[p].astype(f32).T.astype(bf16)

    rows = code_ref.shape[1]
    per = LANES // rows
    place = lax.broadcasted_iota(jnp.int32, (LANES, LANES), 0) - SLOT_COLS
    tagged = (place >= 0) & (place < TABLES)

    def code_rows(blocks):
        codes = [code_ref[pl.ds((h * Z + partner(s)) * 2 + c, 1), :] for h, c, s in blocks]
        code = jnp.concatenate(codes, axis=1)
        table = jnp.floor(code * 0.5)
        return table.astype(jnp.int32), code - 2.0 * table

    order = key_order(h_n)
    for i in range(len(order) // per):
        table, train = code_rows(order[i * per : (i + 1) * per])
        match = (place == table) & (train > 0.5)
        bias = jnp.where(tagged, jnp.where(match, 0.0, BLOCKED), 0.0)
        key_bias_ref[span(i, LANES), :] = bias.T.astype(bf16)
    own = [(lax.axis_index("zh"), lax.axis_index("core"), s) for s in range(Z)]
    for i in range(Z // per):
        table, _ = code_rows(own[i * per : (i + 1) * per])
        hot = jnp.where(place == table, 1.0, 0.0)
        hot_ref[span(i, LANES), :] = hot.T


def only_head(a, h, keep_rest):
    lane = lax.broadcasted_iota(jnp.int32, a.shape, 1)
    mine = (lane >= h * HEAD_DIM) & (lane < (h + 1) * HEAD_DIM)
    if keep_rest:
        mine = mine | (lane >= SLOT_COLS)
    return jnp.where(mine, a, jnp.zeros_like(a))


def each_tile(part_refs, body):
    base = 0
    for ref in part_refs:
        size = min(KEY_TILE, ref.shape[0])

        def one(i, carry, ref=ref, base=base, size=size):
            start = base + i * size
            if not isinstance(i, int):
                start = pl.multiple_of(start, size)
            body(ref[span(i, size), :], pl.ds(start, size))

        loop(ref.shape[0] // size, one)
        base += ref.shape[0]


def take(refs, count):
    return refs[:count], refs[count:]


def at_slot(ref, slot, count):
    return ref.at[slot * count : (slot + 1) * count] if isinstance(slot, int) else ref


def when(condition, body):
    if isinstance(condition, bool):
        if condition:
            body()
    else:
        pl.when(condition)(body)


def task_columns(slot, h):
    start = slot * SLOT_COLS + h * HEAD_DIM
    return pl.ds(start if isinstance(slot, int) else pl.multiple_of(start, HEAD_DIM), HEAD_DIM)


def slots_of(grid):
    return [pl.program_id(0)] if grid else list(range(SLOTS))


def task_lanes(slot):
    if isinstance(slot, int):
        return slice(0, 2 * LANES) if slot < 2 else slice(PAIR - 2 * LANES, PAIR)
    return slice(0, PAIR)


def task_feature(slot):
    if isinstance(slot, int):
        return slice(slot // 2 * D, (slot // 2 + 1) * D), [False, True, is_odd()][slot]
    upper = jnp.where(slot == 2, lax.axis_index("y"), slot) == 1
    return pl.ds(pl.multiple_of(lax.div(slot, 2) * D, D), D), upper


def head_rows(h):
    return slice(h * HEAD_DIM, (h + 1) * HEAD_DIM)


def item_forward(n_parts, n_query, first, last, grid, *refs):
    parts, refs = take(refs, n_parts)
    (kv_w_all, kv_wt_all, key_bias_ref), refs = take(refs, 3)
    if first:
        (q_w_all, hot_ref), refs = take(refs, 2)
        query_parts = parts[:n_query]
        if grid:
            query_parts, refs = take(refs, 1)
    else:
        (q_all, top_in, total_in, mixed_in), refs = take(refs, 4)
    (p_all, top_ref), refs = take(refs, 2)
    if first:
        (q_all,), refs = take(refs, 1)
    if last:
        (end_ref, inv_ref, mixed_ref), refs = take(refs, 3)
        io_refs, refs = take(refs, 3)
    elif first:
        (total_ref, mixed_ref), refs = take(refs, 2)
    else:
        (end_ref, total_ref, mixed_ref), refs = take(refs, 3)
    k_s, vt_s, s_s = refs
    keys = k_s.shape[1]
    queries = q_all.shape[1]
    tile = LANES
    fold = (tile // 8, 8, queries)
    slots = slots_of(grid)
    heads = [(i, slot, h) for i, slot in enumerate(slots) for h in range(SLOT_HEADS)]

    queries_low = []
    for i, slot in enumerate(slots):
        kv_w = at_slot(kv_w_all, slot, 1)
        kv_wt = at_slot(kv_wt_all, slot, 1)
        lanes = task_lanes(slot)

        def project(x, at):
            k = dot(x[:, lanes], kv_w[0, lanes, :LANES])
            k_s[i, at, :] = (k + key_bias_ref[at, :].astype(f32)).astype(bf16)
            vt_s[i, :, at] = dot_t(kv_wt[0, LANES:, lanes], x[:, lanes]).astype(bf16)

        each_tile(parts, project)
        q_ref = at_slot(q_all, slot, 1)
        if first:
            q_w = at_slot(q_w_all, slot, 1)
            query = [dot(x[:, lanes], q_w[0, lanes, :]) for x in query_parts]
            query = (jnp.concatenate(query, axis=0) * SCALE2 + hot_ref[...]).astype(bf16)
            q_ref[0] = query
        else:
            query = q_ref[0]
        queries_low.append(query)

    tops = []
    for i, slot, h in heads:
        query_h = only_head(queries_low[i], h, True)

        def score(n, top):
            at = span(n, tile)
            s = dot_t(k_s[i, at, :], query_h)
            s_s[i * SLOT_HEADS + h, at, :] = s
            return jnp.maximum(top, jnp.max(s.reshape(fold), axis=0))

        top = loop(keys // tile, score, jnp.full((8, queries), 2.0 * BLOCKED, f32))
        tops.append(jnp.max(top, axis=0, keepdims=True))

    totals = []
    for (i, slot, h), top in zip(heads, tops):
        p_ref = at_slot(p_all, slot, SLOT_HEADS)

        def power(n, total):
            at = span(n, tile)
            p = jnp.exp2(s_s[i * SLOT_HEADS + h, at, :] - top)
            p_ref[h, at, :] = p.astype(bf16)
            return total + jnp.sum(p.reshape(fold), axis=0)

        total = loop(keys // tile, power, jnp.zeros((8, queries), f32))
        totals.append(jnp.sum(total, axis=0, keepdims=True))

    def clear():
        mixed_ref[...] = jnp.zeros_like(mixed_ref)

    if last:
        when(slots[0] == 0, clear)
    for (i, slot, h), top, total in zip(heads, tops, totals):
        mixed = dot(vt_s[i, head_rows(h), :], at_slot(p_all, slot, SLOT_HEADS)[h])
        head = pl.ds(slot * SLOT_HEADS + h, 1)
        cols = task_columns(slot, h)
        top_ref[head, :] = top
        if not first:
            end = jnp.maximum(top, top_in[head, :])
            now, before = jnp.exp2(top - end), jnp.exp2(top_in[head, :] - end)
            total = total * now + total_in[head, :] * before
            mixed = mixed * now + mixed_in[cols, :] * before
            end_ref[head, :] = end
        elif last:
            end_ref[head, :] = top
        if last:
            inv = 1.0 / total
            inv_ref[head, :] = inv
            mixed_ref[cols, :] = mixed * inv
        else:
            total_ref[head, :] = total
            mixed_ref[cols, :] = mixed

    def finish():
        half = queries // 2
        io_refs[0][...] = mixed_ref[:D, :].T.astype(bf16)
        shared = mixed_ref[D : D + SLOT_COLS, :].T.astype(bf16)
        io_refs[1][...] = shared[:half]
        io_refs[2][...] = shared[half:]

    if last:
        when(slots[-1] == SLOTS - 1, finish)


def item_turn(counts, grid, *refs):
    groups = []
    for count in counts:
        parts, refs = take(refs, count)
        groups.append(parts)
    (kv_w_all, kv_wt_all, q_all), refs = take(refs, 3)
    qt_all, refs = refs[0], refs[1:]
    for slot in slots_of(grid):
        at_slot(qt_all, slot, 1)[0] = at_slot(q_all, slot, 1)[0].astype(f32).T.astype(bf16)
        kv_w = at_slot(kv_w_all, slot, 1)
        kv_wt = at_slot(kv_wt_all, slot, 1)
        lanes = task_lanes(slot)
        for g, parts in enumerate(groups):
            xt_ref, v_all, kt_all = refs[3 * g : 3 * g + 3]
            v_ref, kt_ref = at_slot(v_all, slot, 1), at_slot(kt_all, slot, 1)

            def one(x, at):
                v_ref[0, at, :] = dot(x[:, lanes], kv_w[0, lanes, LANES:]).astype(bf16)
                kt_ref[0, :, at] = dot_t(kv_wt[0, :LANES, lanes], x[:, lanes]).astype(bf16)

            def turn(x, at):
                xt_ref[:, at] = x.astype(f32).T.astype(bf16)

            each_tile(parts, one)
            when(slot == 0, lambda: each_tile(parts, turn))


def swap_halves(w):
    other = jnp.concatenate([w[SLOT_COLS:], w[:SLOT_COLS]], axis=0)
    return jnp.where(is_odd(), other, w)


def row_middle(shared, w_ref, m_ref, vec_ref, *refs):
    if shared:
        (x1_ref, cot_in, mine_ref, came_ref), refs = refs[:4], refs[4:]
        x1, cot = x1_ref[...], cot_in[...]
        halves = ((mine_ref[...], w_ref[:SLOT_COLS, :]), (came_ref[...], w_ref[SLOT_COLS:, :]))
    else:
        (lo_ref, hi_ref, *cot_refs, own_ref), refs = refs[: 3 + Z], refs[3 + Z :]
        ready_refs, refs = refs[:3], refs[3:]
        lo = lo_ref[...].astype(f32)
        x1 = jnp.concatenate([lo[:, :D], hi_ref[:, :D].astype(f32)], axis=0)
        near = [ref[...].astype(f32) for ref in cot_refs[:2]]
        wide = [ref[...].astype(f32) for ref in cot_refs[2:]]
        cot = [a[:, :D] for a in near] + [b for a in wide for b in (a[:, :D], a[:, D:])]
        cot = jnp.concatenate(cot, axis=0)
        ready_refs[0][...] = lo[:, D:]
        ready_refs[1][...] = jnp.concatenate([a[:, D:] for a in near], axis=0)
        ready_refs[2][...] = swap_halves(w_ref[...])
        halves = ((own_ref[...], w_ref[...]),)
    dz2_ref, low_refs, full_refs, dio_refs = refs[0], refs[1:7], refs[7:11], refs[11:]
    dt2_ref, x2_ref, du_ref, hid_ref, dm_ref, cot_ref = low_refs
    xhat3_ref, dz3_ref, xhat2_ref, dx2_ref = full_refs
    cot_ref[...] = cot.astype(bf16)
    z2 = x1
    for io, w7 in halves:
        z2 = z2 + dot(io, w7)
    xhat2, rstd2 = normed(z2)
    xhat2_ref[...] = xhat2
    x2 = xhat2 * vec_ref[1:2, :] + vec_ref[4:5, :]
    x2_low = x2.astype(bf16)
    x2_ref[...] = x2_low
    up_w = m_ref[:HIDDEN, :]
    down_w = m_ref[HIDDEN:, :]
    up = dot_t(x2_low, up_w)
    c0 = 0.7978845608028654
    c1 = 0.044715
    up2 = up * up
    tanh = jnp.tanh(c0 * up * (1.0 + c1 * up2))
    half_one = 0.5 + 0.5 * tanh
    hid = (up * half_one).astype(bf16)
    hid_ref[...] = hid
    slope = half_one + 0.5 * up * (1.0 - tanh * tanh) * (c0 + 3.0 * c0 * c1 * up2)
    z3 = x2 + dot(hid, down_w) + vec_ref[7:8, :]
    xhat3, rstd3 = normed(z3)
    xhat3_ref[...] = xhat3
    dz3 = norm_back(xhat3, rstd3, vec_ref[2:3, :], cot)
    dz3_ref[...] = dz3
    dm = dz3.astype(bf16)
    dm_ref[...] = dm
    du = (dot_t(dm, down_w) * slope).astype(bf16)
    du_ref[...] = du
    dx2 = dz3 + dot(du, up_w)
    dx2_ref[...] = dx2
    dz2 = norm_back(xhat2, rstd2, vec_ref[1:2, :], dx2)
    dz2_ref[...] = dz2
    dt2 = dz2.astype(bf16)
    dt2_ref[...] = dt2
    for ref, (_, w7) in zip(dio_refs, halves):
        ref[...] = dot_t(dt2, w7).astype(bf16)


def item_backward(n_groups, n_outs, first, last, grid, *refs):
    groups = []
    for _ in range(n_groups):
        group, refs = take(refs, 5)
        groups.append(group)
    if first:
        dio_refs, refs = take(refs, 3)
    else:
        (dt_ref, dz2_own, dz2_shared), refs = take(refs, 3)
    (qt_all, iot_ref, end_ref, inv_ref, kv_w_all), refs = take(refs, 5)
    if last:
        (q_w_all,), refs = take(refs, 1)
        if grid:
            (xtq_ref,), refs = take(refs, 1)
    if not first:
        (dq_past, g_past), refs = take(refs, 2)
    if grid:
        gw_ref, dx_ref, dxq_ref, dt_ref, dkv_s, ds_s = refs
    else:
        out_refs, refs = take(refs, n_outs)
        if last:
            gw_ref, dx_ref, dkv_s, ds_s = refs
            dxq_ref = dx_ref.at[:, : qt_all.shape[2]]
        else:
            dt_ref, ds_s, dkv_s, dx_ref = refs
    queries = qt_all.shape[2]

    def start():
        if first:
            dt_ref[:D, :] = dio_refs[0][...].astype(f32).T
            shared = jnp.concatenate([dio_refs[1][...], dio_refs[2][...]], axis=0)
            dt_ref[D : D + SLOT_COLS, :] = shared.astype(f32).T
        dx_ref[...] = jnp.zeros_like(dx_ref)
        if grid:
            dxq_ref[...] = jnp.zeros_like(dxq_ref)
        if last:
            gw_ref[...] = jnp.zeros_like(gw_ref)

    slots = slots_of(grid)
    when(slots[0] == 0, start)
    heads = [(i, slot, h) for i, slot in enumerate(slots) for h in range(SLOT_HEADS)]
    blank = jnp.zeros((HEAD_DIM, queries), bf16)
    base = 0
    grads = []
    for xt_ref, v_all, kt_all, p_all, top_ref in groups:
        keys = v_all.shape[1]
        for i, slot, h in heads:
            head = pl.ds(slot * SLOT_HEADS + h, 1)
            cols = task_columns(slot, h)
            scale = jnp.exp2(top_ref[head, :] - end_ref[head, :]) * inv_ref[head, :]
            scaled = dt_ref[cols, :] * scale
            delta = jnp.sum(scaled * iot_ref[cols, :], axis=0, keepdims=True)
            grad = scaled.astype(bf16)
            grads.append(grad)
            alone = jnp.concatenate([grad if j == h else blank for j in range(LANES // HEAD_DIM)], axis=0)
            v_ref, p_ref = at_slot(v_all, slot, 1), at_slot(p_all, slot, SLOT_HEADS)

            def score(n, carry):
                at = span(n, KEY_TILE)
                dp = dot(v_ref[0, at, :], alone)
                ds = (p_ref[h, at, :].astype(f32) * (dp - delta)).astype(bf16)
                ds_s[i * SLOT_HEADS + h, span(base // KEY_TILE + n, KEY_TILE), :] = ds
                return carry

            loop(keys // KEY_TILE, score, 0)
        base += keys

    if first:
        dq_heads = [jnp.zeros((HEAD_DIM, queries), f32)] * len(heads)
    else:
        dq_heads = [dq_past[n] for n in range(len(heads))]
    base = 0
    for g, (xt_ref, v_all, kt_all, p_all, top_ref) in enumerate(groups):
        keys = v_all.shape[1]
        for n, (i, slot, h) in enumerate(heads):
            kt_ref, p_ref = at_slot(kt_all, slot, 1), at_slot(p_all, slot, SLOT_HEADS)
            grad = grads[g * len(heads) + n]
            query_t = at_slot(qt_all, slot, 1)[0, head_rows(h), :]
            rows_k, rows_v = head_rows(h), slice(LANES + h * HEAD_DIM, LANES + (h + 1) * HEAD_DIM)

            def sums(t, dq_t):
                at, put = span(t, KEY_TILE), span(base // KEY_TILE + t, KEY_TILE)
                ds = ds_s[i * SLOT_HEADS + h, put, :]
                dkv_s[i, rows_v, put] = dot_t(grad, p_ref[h, at, :]).astype(bf16)
                dkv_s[i, rows_k, put] = (dot_t(query_t, ds) * (1.0 / LOG2E)).astype(bf16)
                return dq_t + dot(kt_ref[0, head_rows(h), at], ds) if last else dq_t

            dq_heads[n] = loop(keys // KEY_TILE, sums, dq_heads[n])
        base += keys

    unused = jnp.zeros((LANES - SLOT_COLS, base), bf16)
    for i, slot in enumerate(slots):
        kv_w = at_slot(kv_w_all, slot, 1)
        feature, upper = task_feature(slot)
        dkv_s[i, SLOT_COLS:LANES, :] = unused
        dkv_s[i, LANES + SLOT_COLS :, :] = unused
        base = 0
        g_kv = jnp.zeros((D, 2 * LANES), f32) if first else g_past[i]
        for xt_ref, v_all, kt_all, p_all, top_ref in groups:
            keys = v_all.shape[1]

            def back(n, carry):
                put = span(base // KEY_TILE + n, KEY_TILE)
                dx_ref[feature, put] += dot(kv_w[0, feature, :], dkv_s[i, :, put])
                return carry

            loop(keys // KEY_TILE, back, 0)
            if last:
                g_kv = g_kv + dot_t(xt_ref[feature, :], dkv_s[i, :, base : base + keys])
            base += keys
        if not last:
            continue
        rest = jnp.zeros((LANES - SLOT_COLS, queries), f32)
        dq_t = jnp.concatenate(dq_heads[i * SLOT_HEADS : (i + 1) * SLOT_HEADS] + [rest], axis=0)
        found = [(1, g_kv[:, :LANES]), (2, g_kv[:, LANES:])]
        dq = (dq_t * SCALE).astype(bf16)
        dxq_ref[feature, :] += dot(at_slot(q_w_all, slot, 1)[0, feature, :], dq)
        xq = xtq_ref[feature, :] if grid else groups[0][0][feature, :queries]
        found.append((0, dot_t(xq, dq)))
        blank = jnp.zeros((D, SLOT_COLS), f32)
        for m, g in found:
            g = g[:, :SLOT_COLS]
            if upper is not True:
                g_low = jnp.concatenate([g, blank], axis=1)
            if upper is not False:
                g_high = jnp.concatenate([blank, g], axis=1)
            whole = g_high if upper is True else g_low if upper is False else jnp.where(upper, g_high, g_low)
            gw_ref[m * D : (m + 1) * D, :] += whole

    if not grid:
        base = 0
        for n, ref in enumerate(out_refs):
            count = ref.shape[0]
            total = dx_ref[:, base : base + count].T
            if last and n < 2:
                shared = dz2_shared[...] if n == 0 else jnp.zeros((count, D), f32)
                total = total + jnp.concatenate([dz2_own[base : base + count, :], shared], axis=1)
            ref[...] = total.astype(ref.dtype)
            base += count


def item_far(*refs):
    groups = (refs[:2], refs[2:4])
    ds_ref, dkv_ref, dq_ref, g_ref = refs[4:]
    for slot in range(SLOTS):
        feature, _ = task_feature(slot)
        base = 0
        for xt_ref, kt_ref in groups:
            at = slice(base, base + xt_ref.shape[1])
            g = dot_t(xt_ref[feature, :], dkv_ref[slot, :, at])
            g_ref[slot] = g_ref[slot] + g if base else g
            for h in range(SLOT_HEADS):
                n = slot * SLOT_HEADS + h
                dq = dot(kt_ref[slot, head_rows(h), :], ds_ref[n, at, :])
                dq_ref[n] = dq_ref[n] + dq if base else dq
            base += xt_ref.shape[1]


def feat_backward(rows, xhat1_ref, rstd1_ref, cells_ref, qkv_ref, fo_ref, prob_ref, w_ref, vec_ref, *refs):
    dx_refs, refs = refs[:Z], refs[Z:]
    gw_ref, gvec_ref, dz1_ref, dqkv_ref, dk_s, dv_s, dfo_s, dx_s = refs
    xhat1, rstd1 = xhat1_ref[...], rstd1_ref[...]
    dx_s[...] = jnp.zeros_like(dx_s)
    read_pairs(dx_refs, dx_s)
    dx1 = dx_s[...].reshape(FEAT * rows, D)
    gvec_ref[...] = jnp.zeros_like(gvec_ref)
    gvec_ref[0:1, :] = col_sum(dx1 * xhat1)
    gvec_ref[3:4, :] = col_sum(dx1)
    dz1 = norm_back(xhat1, rstd1, vec_ref[0:1, :], dx1)
    gvec_ref[6:7, :] = col_sum(dz1)
    dz1_ref[...] = dz1
    dt1 = dz1.astype(bf16)
    gw_ref[3 * D : 4 * D, :] = t_dot(fo_ref[...], dt1)
    dfo_s[...] = dot_t(dt1, w_ref[3 * D : 4 * D, :])
    ones = head_ones()
    keys = qkv_ref[1].astype(f32).reshape(FEAT, rows, D)
    values = qkv_ref[2].astype(f32).reshape(FEAT, rows, D)
    dk_s[...] = jnp.zeros_like(dk_s)
    dv_s[...] = jnp.zeros_like(dv_s)
    for f in range(FEAT):
        at = slice(f * rows, (f + 1) * rows)
        query = qkv_ref[0, at, :].astype(f32)
        probs = [prob_ref[f, g] for g in range(FEAT)]
        dfo = dfo_s[at, :].astype(bf16).astype(f32)
        prod = (values * dfo[None]).reshape(FEAT * rows, D).astype(bf16)
        dfp = dot(prod, ones).reshape(FEAT, rows, D)
        mean = functools.reduce(jnp.add, [probs[g] * dfp[g] for g in range(FEAT)])
        dq = jnp.zeros((rows, D), f32)
        for g in range(FEAT):
            here = slice(g * rows, (g + 1) * rows)
            ds = probs[g] * (dfp[g] - mean)
            dq = dq + ds * keys[g]
            dk_s[here, :] += ds * query
            dv_s[here, :] += probs[g] * dfo
        dqkv_ref[0, at, :] = (dq * SCALE).astype(bf16)
    dqkv_ref[1] = (dk_s[...] * SCALE).astype(bf16)
    dqkv_ref[2] = dv_s[...].astype(bf16)
    for m in range(3):
        gw_ref[m * D : (m + 1) * D, :] = t_dot(cells_ref[...], dqkv_ref[m])


def cell_out(dz1_ref, dqkv_ref, w_ref, out_ref):
    total = dz1_ref[...]
    for m in range(3):
        total = total + dot_t(dqkv_ref[m], w_ref[m * D : (m + 1) * D, :])
    out_ref[...] = total


def middle_grads(vec_ref, *refs):
    (own_ref, mine_ref, came_ref), sets, refs = refs[:3], (refs[3:13], refs[13:23]), refs[23:]
    (gw_ref, gu_ref, gv_ref, gvec_ref), out_refs = refs[:4], refs[4:]
    outs = []
    for i, (dt2_ref, x2_ref, du_ref, hid_ref, dm_ref, cot_ref, *full_refs) in enumerate(sets):
        xhat3, dz3, xhat2, dx2 = [ref[...] for ref in full_refs]
        cot = cot_ref[...].astype(f32)
        outs.append(xhat3 * vec_ref[2:3, :] + vec_ref[5:6, :])
        if i == 0:
            gw = t_dot(own_ref[...], dt2_ref[...])
        else:
            gw = jnp.concatenate([t_dot(mine_ref[...], dt2_ref[...]), t_dot(came_ref[...], dt2_ref[...])], axis=0)
        gu = t_dot(du_ref[...], x2_ref[...])
        gv = t_dot(hid_ref[...], dm_ref[...])
        rows = {1: dx2 * xhat2, 2: cot * xhat3, 4: dx2, 5: cot, 7: dz3}
        if i == 0:
            gw_ref[...], gu_ref[...], gv_ref[...] = gw, gu, gv
            gvec_ref[...] = jnp.zeros_like(gvec_ref)
        else:
            gw_ref[...] += swap_halves(gw)
            gu_ref[...] += gu
            gv_ref[...] += gv
        for k, a in rows.items():
            gvec_ref[k : k + 1, :] += col_sum(a)
    rows = out_refs[0].shape[0]
    for s in range(Z):
        own = outs[0][s * rows : (s + 1) * rows]
        if s < Z // 2:
            sides = [own, outs[1][s * rows : (s + 1) * rows]]
        else:
            sides = [own[: rows // 2], own[rows // 2 :]]
        out_refs[s][...] = jnp.concatenate(sides, axis=1).astype(bf16)


def out_collect(*refs):
    pair_refs, out_ref, full_s = refs[:Z], refs[Z], refs[Z + 1]
    rows = full_s.shape[1]
    for s in range(Z):
        t = partner(s)
        both = pair_refs[s][...]
        if s < Z // 2:
            full_s[own_feature(t)] = both[:, :D]
            full_s[shared_feature(t)] = both[:, D:]
        else:
            full_s[own_feature(t), : rows // 2, :] = both[:, :D]
            full_s[own_feature(t), rows // 2 :, :] = both[:, D:]
    out_ref[...] = full_s[...].reshape(out_ref.shape)


ATTN_ROWS = 48
MLP_ROWS = 24
VEC_PART = 48
PACK = 112
HALF = LANES // 2


def pack_rows(attn, mlp, extra):
    low, high = slice(0, LANES), slice(LANES, D)
    last = jnp.concatenate([extra, mlp[16:24, high]], axis=0)
    return jnp.concatenate(
        [
            attn[:, low],
            jnp.concatenate([attn[:16, high], attn[16:32, high]], axis=1),
            jnp.concatenate([attn[32:, high], last], axis=1),
            mlp[:, low],
            jnp.concatenate([mlp[:8, high], mlp[8:16, high]], axis=1),
        ],
        axis=0,
    )


def unpack_rows(block):
    attn_high = jnp.concatenate([block[48:64, :HALF], block[48:64, HALF:], block[64:80, :HALF]], axis=0)
    mlp_high = jnp.concatenate([block[104:, :HALF], block[104:, HALF:], block[72:80, HALF:]], axis=0)
    attn = jnp.concatenate([block[:48], attn_high], axis=1)
    mlp = jnp.concatenate([block[80:104], mlp_high], axis=1)
    return attn, mlp, block[64:72, HALF:]


def share_pack(*refs):
    sources, out_refs, targets, sems = refs[:6], refs[6 : 6 + Z], refs[6 + Z : 12 + Z], refs[12 + Z]
    copies = [pltpu.make_async_copy(a, b, sems.at[i]) for i, (a, b) in enumerate(zip(sources, targets))]
    for c in copies:
        c.start()
    for c in copies:
        c.wait()
    attn, mlp, vec, tab, train, cnt = [ref[...].astype(f32) for ref in targets]
    code = tab * 2.0 + jnp.where(train > 0, 1.0, 0.0)
    lines = [jnp.concatenate([a, jnp.zeros((1, HALF - a.shape[1]), f32)], axis=1) for a in (vec, cnt)]
    extra = jnp.concatenate([lines[0], code, lines[1], jnp.zeros((5, HALF), f32)], axis=0)
    block = pack_rows(attn, mlp, extra).astype(bf16)
    for ref in out_refs:
        ref[...] = block


def hold(*refs):
    for i in range(3):
        refs[3 + i][...] = refs[i][...]


def at_place(z_step, dy, dc, dr):
    place = (
        lax.bitwise_xor(lax.axis_index("zh") * 2 + lax.axis_index("zl"), FAR_ORDER[z_step]),
        (lax.axis_index("y") + dy) % 2,
        (lax.axis_index("core") + dc) % 2,
        (lax.axis_index("rep") + dr) % 2,
    )
    z, y, c, r = place
    return ((z * 2 + y) * 2 + c) * 2 + r, place


def share_unpack(*refs):
    part_refs, refs = refs[:8], refs[8:]
    attn_ref, mlp_ref, vec_ref, code_ref, count_ref, mlp_s, vec_s = refs
    _, _, extra = unpack_rows(part_refs[0][0].astype(f32))
    table = jnp.floor(extra[1:2] * 0.5)
    counts = jnp.zeros(table.shape, f32)
    for k in range(TABLES):
        counts = jnp.where(table == k, extra[2:3, k : k + 1], counts)
    count_ref[...] = jnp.broadcast_to(row_to_col(counts, table.shape[1]), count_ref.shape)
    for i, ref in enumerate(part_refs):
        dc, dy, dr = i // 4, FAR_ORDER[i % 4] // 2, FAR_ORDER[i % 4] % 2
        for s in range(Z):
            attn, mlp, extra = unpack_rows(ref[s].astype(f32))
            index, (z, y, c, r) = at_place(s, dy, dc, dr)
            attn_ref[pl.ds(pl.multiple_of(index * ATTN_ROWS, 16), ATTN_ROWS), :] = attn.astype(bf16)
            mlp_s[pl.ds(pl.multiple_of(index * MLP_ROWS, 8), MLP_ROWS), :] = mlp
            vec_s[c * 2 + r, pl.ds(z * 2 + y, 1), :] = extra[:1]
            if dr == 0:
                code_ref[pl.ds((z * 2 + y) * 2 + c, 1), :] = extra[1:2]
    mlp_ref[...] = mlp_s[...].astype(bf16)
    vec_ref[...] = jnp.concatenate([vec_s[j][:, :VEC_PART] for j in range(4)], axis=1)


ATTN_PACK = 80
MLP_PACK = 40


def each_share(keep_ref, give_ref, block_of):
    for dc in range(2):
        for plane in range(4):
            for s in range(Z):
                index, place = at_place(s, FAR_ORDER[plane] // 2, dc, FAR_ORDER[plane] % 2)
                block = block_of(index, place)
                if dc == 0:
                    keep_ref[plane, s] = block
                else:
                    give_ref[plane, s] = block.astype(bf16)


def mlp_pack(up_ref, down_ref, keep_ref, give_ref, mlp_s):
    mlp_s[:HIDDEN, :] = up_ref[...]
    mlp_s[HIDDEN:, :] = down_ref[...]

    def block_of(index, _):
        mlp = mlp_s[pl.ds(pl.multiple_of(index * MLP_ROWS, 8), MLP_ROWS), :]
        high = mlp[:, LANES:]
        return jnp.concatenate(
            [
                mlp[:, :LANES],
                jnp.concatenate([high[:8], high[8:16]], axis=1),
                jnp.concatenate([high[16:], jnp.zeros((8, HALF), f32)], axis=1),
            ],
            axis=0,
        )

    each_share(keep_ref, give_ref, block_of)


def grad_pack(feat_ref, item_ref, w7_ref, veca_ref, vecb_ref, keep_ref, give_ref, attn_s, vec_s):
    attn_s[: 4 * D, :] = feat_ref[...]
    attn_s[4 * D : 7 * D, :] = item_ref[...]
    attn_s[7 * D :, :] = w7_ref[...]
    vec = veca_ref[...] + vecb_ref[...]
    for j in range(4):
        part = vec[:, j * VEC_PART : (j + 1) * VEC_PART]
        vec_s[j] = jnp.concatenate([part, jnp.zeros((8, HALF - VEC_PART), f32)], axis=1)

    def block_of(index, place):
        z, y, c, r = place
        attn = attn_s[pl.ds(pl.multiple_of(index * ATTN_ROWS, 8), ATTN_ROWS), :]
        row = vec_s[c * 2 + r, pl.ds(z * 2 + y, 1), :]
        last = jnp.concatenate([row, jnp.zeros((15, HALF), f32)], axis=0)
        high = attn[:, LANES:]
        return jnp.concatenate(
            [
                attn[:, :LANES],
                jnp.concatenate([high[:16], high[16:32]], axis=1),
                jnp.concatenate([high[32:], last], axis=1),
            ],
            axis=0,
        )

    each_share(keep_ref, give_ref, block_of)


def grad_unpack(own_ref, *refs):
    total = own_ref[...]
    for ref in refs[: Z - 1]:
        total = total + ref[...].astype(f32)
    attn_ref, mlp_ref, vec_ref = refs[Z - 1 :]
    high = jnp.concatenate([total[48:64, :HALF], total[48:64, HALF:], total[64:80, :HALF]], axis=0)
    attn_ref[...] = jnp.concatenate([total[:48], high], axis=1)
    vec_ref[...] = total[64:65, HALF : HALF + VEC_PART]
    mlp = total[ATTN_PACK:]
    high = jnp.concatenate([mlp[24:32, :HALF], mlp[24:32, HALF:], mlp[32:, :HALF]], axis=0)
    mlp_ref[...] = jnp.concatenate([mlp[:24], high], axis=1)


VMEM = pl.BlockSpec(memory_space=pltpu.VMEM)
SMEM = pl.BlockSpec(memory_space=pltpu.SMEM)


def like(shape, kind=f32):
    return jax.ShapeDtypeStruct(shape, kind)


def swap(a, axis):
    return lax.ppermute(a, axis, [(0, 1), (1, 0)])


def exchange(a, axes):
    return lax.all_to_all(a, axes, 0, 0, tiled=True)


def along(axes, blocks):
    order = TASK_ORDER if axes == TASK_AXES else FAR_ORDER
    return blocks[:1] + [
        lax.ppermute(a, axes, [(i, i ^ x) for i in range(Z)]) for a, x in zip(blocks[1:], order[1:])
    ]


def gather_any(w_attn, w_mlp, vectors, table_ids, train_mask, feat_count, cells, cot, _):
    rows = table_ids.shape[1]
    fan, reps = lax.axis_size(FAN), lax.axis_size("rep")
    core = lax.axis_index("core")
    ra, rm, nv = w_attn.shape[0], w_mlp.shape[0], vectors.shape[0]
    code = (table_ids * 2 + (train_mask > 0)).astype(bf16)[0]
    last = jnp.pad(jnp.concatenate([vectors, code]), (0, D - nv - rows)).reshape(1, D)
    block = jnp.concatenate([w_attn, w_mlp, last], axis=0)
    rb = ra + rm + 1
    mine = exchange(jnp.broadcast_to(block[None], (fan, rb, D)), FAN)
    other = swap(mine, "core")
    both = jnp.stack([jnp.where(core == 0, mine, other), jnp.where(core == 0, other, mine)], axis=1)
    both = both.reshape(fan // reps, reps, 2, rb, D).transpose(0, 2, 1, 3, 4)
    attn = both[..., :ra, :].reshape(8 * D, D)
    mlp = both[..., ra : ra + rm, :].reshape(2 * HIDDEN, D)
    tail = both[..., ra + rm, :]
    vec = tail[..., :nv].reshape(8, D).astype(f32)
    codes = lax.dynamic_index_in_dim(tail[..., nv : nv + rows], lax.axis_index("rep"), 2, keepdims=False)
    hit = table_ids[0][:, None] == jnp.arange(TABLES)[None, :]
    counts = jnp.sum(jnp.where(hit, feat_count, 0), axis=1, keepdims=True).astype(f32)
    counts = jnp.broadcast_to(counts, (rows, D))
    return attn, mlp, vec, codes.reshape(-1, rows).astype(f32), counts, cells, cot


def gather_packed(w_attn, w_mlp, vectors, table_ids, train_mask, feat_count, cells, cot, limit):
    shares = (w_attn, w_mlp, vectors[None], table_ids, train_mask, feat_count)
    blocks = pl.pallas_call(
        share_pack,
        out_shape=(like((PACK, LANES), bf16),) * Z,
        in_specs=[pl.BlockSpec(memory_space=pl.ANY)] * 6,
        out_specs=(VMEM,) * Z,
        scratch_shapes=[pltpu.VMEM(a.shape, a.dtype) for a in shares] + [pltpu.SemaphoreType.DMA((6,))],
        compiler_params=pltpu.CompilerParams(vmem_limit_bytes=67000000),
        name="share_pack",
    )(*shares)
    *held, block_held = pl.pallas_call(
        hold,
        out_shape=(like(cells.shape, bf16), like(cells.shape, bf16), like((PACK, LANES), bf16)),
        in_specs=[VMEM] * 3,
        out_specs=(VMEM,) * 3,
        compiler_params=limit,
        name="hold",
    )(cells, cot, blocks[0])
    own = jnp.stack([block_held] + along(Z_AXES, list(blocks))[1:])
    own, held = lax.optimization_barrier((own, held))
    plane = along(PLANE_AXES, [own] * 4)
    *shares, counts = pl.pallas_call(
        share_unpack,
        out_shape=(
            like((8 * D, D), bf16),
            like((2 * HIDDEN, D), bf16),
            like((8, D)),
            like((4 * Z, table_ids.shape[1])),
            like((table_ids.shape[1], D)),
        ),
        in_specs=[VMEM] * 8,
        out_specs=(VMEM,) * 5,
        scratch_shapes=[pltpu.VMEM((2 * HIDDEN, D), f32), pltpu.VMEM((4, 8, HALF), f32)],
        compiler_params=limit,
        name="share_unpack",
    )(*plane, *[swap(a, "core") for a in plane])
    return *shares, counts, *held


def sum_any(grads, share, later, _):
    g_feat, g_item, g_w7, g_up, g_down, g_vec_a, g_vec_b = grads
    ra, rm, nv = share
    rb = ra + rm + 1
    fan, reps = lax.axis_size(FAN), lax.axis_size("rep")
    core = lax.axis_index("core")
    spread = (fan // reps, 2, reps)
    g_attn = jnp.concatenate([g_feat, g_item, g_w7], axis=0).reshape(spread + (ra, D))
    g_mlp = jnp.concatenate([g_up, g_down], axis=0).reshape(spread + (rm, D))
    g_vec = (g_vec_a + g_vec_b).reshape(spread + (1, nv))
    g_vec = jnp.pad(g_vec, ((0, 0),) * 4 + ((0, D - nv),))
    g_all = jnp.concatenate([g_attn, g_mlp, g_vec], axis=3)
    keep = lax.dynamic_index_in_dim(g_all, core, 1, keepdims=False)
    give = lax.dynamic_index_in_dim(g_all, 1 - core, 1, keepdims=False)
    chip = keep + swap(give.astype(bf16), "core").astype(f32)
    shares = exchange(chip.astype(bf16).reshape(fan, rb, D), FAN)
    total = jnp.sum(shares.astype(f32), axis=0)
    return total[:ra], total[ra : ra + rm], total[ra + rm, :nv], later


def over_plane(keep, got):
    sent = [keep[0]] + [(keep[i] + got[i]).astype(bf16) for i in range(1, 4)]
    return keep[0] + got[0], along(PLANE_AXES, sent)[1:]


def pack_call(kernel, grads, rows, scratch, limit, name):
    return pl.pallas_call(
        kernel,
        out_shape=(like((4, Z, rows, LANES)), like((4, Z, rows, LANES), bf16)),
        in_specs=[VMEM] * len(grads),
        out_specs=(VMEM,) * 2,
        scratch_shapes=scratch,
        compiler_params=limit,
        name=name,
    )(*grads)


def sum_packed(grads, mlp_total, share, later, limit):
    ra, rm, nv = share
    scratch = [pltpu.VMEM((8 * D, D), f32), pltpu.VMEM((4, 8, HALF), f32)]
    keep, give = pack_call(grad_pack, grads, ATTN_PACK, scratch, limit, "grad_pack")
    total, came = over_plane(keep, swap(give, "core").astype(f32))
    for a in came:
        total = total + a.astype(f32)
    total = jnp.concatenate([total, mlp_total], axis=1)
    steps = [total[0]] + [total[i].astype(bf16) for i in range(1, Z)]
    steps, later = lax.optimization_barrier((steps, later))
    attn, mlp, vec = pl.pallas_call(
        grad_unpack,
        out_shape=(like((ra, D)), like((rm, D)), like((1, nv))),
        in_specs=[VMEM] * Z,
        out_specs=(VMEM,) * 3,
        compiler_params=limit,
        name="grad_unpack",
    )(*along(Z_AXES, steps))
    return attn, mlp, vec.reshape(nv), later


def local(cell_values, table_ids, train_mask, feat_count, w_attn, w_mlp, vectors, cotangent):
    rows = cell_values.shape[1]
    cells_n = rows * FEAT
    h_n = lax.axis_size("zh")
    fast = h_n == 2
    all_rows = Z * h_n * 2 * rows
    q_rows = Z * rows
    small = pltpu.CompilerParams(vmem_limit_bytes=16 * 2**20)
    limit = small if fast else pltpu.CompilerParams(vmem_limit_bytes=63 * 2**20)

    cells = cell_values[0].transpose(1, 0, 2).reshape(cells_n, D)
    cot = cotangent[0].transpose(1, 0, 2).reshape(cells_n, D)

    shares = gather_packed if fast else gather_any
    attn, mlp, vec, codes, counts, cells, cot = shares(
        w_attn, w_mlp, vectors, table_ids, train_mask, feat_count, cells, cot, small
    )

    pair_block = like((rows, PAIR), bf16)
    half_rows = rows + rows // 2
    xhat1, rstd1, qkv, fo, probs, *x_out, cot_own = pl.pallas_call(
        functools.partial(feat_forward, rows),
        out_shape=(
            like((cells_n, D)),
            like((cells_n, D)),
            like((3, cells_n, D), bf16),
            like((cells_n, D), bf16),
            like((FEAT, FEAT, rows, D)),
            pair_block,
            like((2 * rows, PAIR), bf16),
            like((half_rows, PAIR), bf16),
            like((half_rows, PAIR), bf16),
            pair_block,
        ),
        in_specs=[VMEM] * 5,
        out_specs=(VMEM,) * 10,
        scratch_shapes=[
            pltpu.VMEM((Z, rows, PAIR), bf16),
            pltpu.VMEM((Z, rows, PAIR), bf16),
            pltpu.VMEM((Z, rows // 2, PAIR), bf16),
        ],
        compiler_params=small,
        name="feat_forward",
    )(cells, cot, counts, attn[: 4 * D], vec)

    def whole(*shape):
        return pl.BlockSpec(shape, lambda i: (0,) * len(shape))

    def by_slot(*shape):
        once = {"pipeline_mode": pl.Buffered(1)} if math.prod(shape) > 2**22 else {}
        return pl.BlockSpec(shape, lambda i: (i,) + (0,) * (len(shape) - 1), **once)

    def item_call(kernel, ins, outs, scratch, name):
        def specs(pairs):
            if fast:
                return [VMEM] * len(pairs)
            return [by_slot(a.shape[0] // SLOTS, *a.shape[1:]) if by else whole(*a.shape) for a, by in pairs]

        return pl.pallas_call(
            kernel,
            out_shape=[a for a, _ in outs],
            in_specs=specs(ins),
            out_specs=specs(outs),
            scratch_shapes=scratch,
            compiler_params=limit,
            cost_estimate=pl.CostEstimate(flops=10**8, bytes_accessed=0, transcendentals=0),
            name=name,
            **({} if fast else {"grid": (SLOTS,)}),
        )(*[a for a, _ in ins])

    def shared(*arrays):
        return [(a, False) for a in arrays]

    def tasked(*arrays):
        return [(a, True) for a in arrays]

    heads_block, pair_t = like((16, q_rows)), like((PAIR, q_rows))

    def forward_call(parts, bias, first, last, extra):
        keys = sum(a.shape[0] for a in parts)
        tasks = SLOTS if fast else 1
        outs = tasked(like((SLOTS * SLOT_HEADS, keys, q_rows), bf16)) + shared(heads_block)
        if first:
            outs += tasked(like((SLOTS, q_rows, LANES), bf16))
        if last:
            half_heads = like((q_rows // 2, SLOT_COLS), bf16)
            outs += shared(heads_block, heads_block, pair_t, like((q_rows, D), bf16), half_heads, half_heads)
        else:
            outs += shared(*([heads_block] * (1 if first else 2)), pair_t)
        scratch = [
            pltpu.VMEM((tasks, keys, LANES), bf16),
            pltpu.VMEM((tasks, LANES, keys), bf16),
            pltpu.VMEM((tasks * SLOT_HEADS, keys, q_rows), f32),
        ]
        kernel = functools.partial(item_forward, len(parts), 2, first, last, not fast)
        ins = shared(*parts) + tasked(kv_w, kv_wt) + shared(bias) + extra
        return item_call(kernel, ins, outs, scratch, "item_forward")

    def turn_call(groups, query):
        outs = tasked(like((SLOTS, LANES, q_rows), bf16))
        for parts in groups:
            keys = sum(a.shape[0] for a in parts)
            outs += shared(like((PAIR, keys), bf16))
            outs += tasked(like((SLOTS, keys, LANES), bf16), like((SLOTS, LANES, keys), bf16))
        kernel = functools.partial(item_turn, [len(g) for g in groups], not fast)
        ins = shared(*sum(groups, [])) + tasked(kv_w, kv_wt, query)
        query_t, *rest = item_call(kernel, ins, outs, [], "item_turn")
        return query_t, [tuple(rest[i : i + 3]) for i in range(0, len(rest), 3)]

    def backward_call(groups, parts, first, last, grads, extra):
        keys = sum(g[1].shape[1] for g in groups)
        tasks = SLOTS if fast else 1
        kv_shape, ds_shape = (tasks, 2 * LANES, keys), (tasks * SLOT_HEADS, keys, q_rows)
        scratch = [pltpu.VMEM(kv_shape, bf16), pltpu.VMEM(ds_shape, bf16)]
        if fast:
            outs = shared(*parts)
            outs += shared(like((3 * D, D))) if last else shared(pair_t, like(ds_shape, bf16), like(kv_shape, bf16))
            scratch = [pltpu.VMEM((PAIR, keys), f32)] + (scratch if last else [])
        else:
            outs = shared(like((3 * D, D)), *parts)
            scratch = [pltpu.VMEM((PAIR, q_rows), f32)] + scratch
        ins = []
        for xt, v, kt, p, top in groups:
            ins += shared(xt) + tasked(v, kt, p) + shared(top)
        ins += shared(*grads) + tasked(query_t) + shared(io_t, end, inv) + tasked(kv_w) + extra
        kernel = functools.partial(item_backward, len(groups), len(parts), first, last, not fast)
        return item_call(kernel, ins, outs, scratch, "item_backward")

    kv_w, kv_wt, q_w, key_bias, hot = pl.pallas_call(
        functools.partial(item_prepare, h_n),
        out_shape=(
            like((SLOTS, PAIR, 2 * LANES), bf16),
            like((SLOTS, 2 * LANES, PAIR), bf16),
            like((SLOTS, PAIR, LANES), bf16),
            like((all_rows, LANES), bf16),
            like((q_rows, LANES)),
        ),
        in_specs=[VMEM] * 2,
        out_specs=(VMEM,) * 5,
        compiler_params=limit,
        name="item_prepare",
    )(attn[4 * D : 7 * D], codes)

    def to_task(block, i):
        return lax.ppermute(block, TASK_AXES, [(j, j ^ TASK_ORDER[i]) for j in range(Z)])

    came = [to_task(x_out[i], i) for i in range(1, Z)]
    x_lo = jnp.concatenate([x_out[0], came[0][:rows]], axis=0)
    came[1:], _ = lax.optimization_barrier((came[1:], x_lo))
    x_hi = jnp.concatenate([a[:rows] for a in came[1:]], axis=0)
    cot_in = [cot_own] + [a[rows:] for a in came]
    if fast:
        h_lo, h_hi = swap(x_lo, "zh"), swap(x_hi, "zh")
        near = [x_lo, x_hi, swap(x_lo, "core"), swap(x_hi, "core")]
        ends = (0, 2 * q_rows, 3 * q_rows, 4 * q_rows)
        bias = [key_bias[a:b] for a, b in zip(ends, ends[1:])]
        near_p, near_top, query, total, mixed = forward_call(
            near, bias[0], True, False, tasked(q_w) + shared(hot)
        )
        h_lo, total = lax.optimization_barrier((h_lo, total))
        far_lo = [h_lo, swap(h_lo, "core")]
        lo_p, lo_top, end, total, mixed = forward_call(
            far_lo, bias[1], False, False, tasked(query) + shared(near_top, total, mixed)
        )
        h_hi, total = lax.optimization_barrier((h_hi, total))
        far_hi = [h_hi, swap(h_hi, "core")]
        hi_p, hi_top, end, inv, io_t, io_own, io_mine, io_give = forward_call(
            far_hi, bias[2], False, True, tasked(query) + shared(end, total, mixed)
        )
    else:
        x_q = jnp.concatenate([x_lo, x_hi], axis=0)
        parts = [lax.all_gather(x_q, ("zh", "core"), axis=0, tiled=True)]
        all_p, all_top, query, end, inv, io_t, io_own, io_mine, io_give = forward_call(
            parts, key_bias, True, True, tasked(q_w) + shared(hot, x_q)
        )

    def to_shared(block):
        return lax.ppermute(block, "y", [(0, 1), (1, 0)])

    io_came = to_shared(io_give)
    query, _ = lax.optimization_barrier((query, io_give))
    query_t, turned = turn_call([near, far_lo, far_hi] if fast else [parts], query)

    cells_low = like((cells_n, D), bf16)

    def middle_call(shared, w7, ins, ready, dio_shapes):
        count = q_rows // 2 if shared else q_rows
        low, full, hidden = like((count, D), bf16), like((count, D)), like((count, HIDDEN), bf16)
        outs = pl.pallas_call(
            functools.partial(row_middle, shared),
            out_shape=ready + [full] + [low] * 2 + [hidden] * 2 + [low] * 2 + [full] * 4 + dio_shapes,
            in_specs=[VMEM] * (3 + len(ins)),
            out_specs=[VMEM] * (len(ready) + 11 + len(dio_shapes)),
            compiler_params=small,
            name="row_middle",
        )(w7, mlp, vec, *ins)
        ready, (dz2, *outs) = outs[: len(ready)], outs[len(ready) :]
        return ready, dz2, outs[:10], outs[10:]

    half_heads = like(io_mine.shape, bf16)
    ready = [like((q_rows // 2, D)), like((q_rows // 2, D)), like((D, D), bf16)]
    (x1_shared, cot_shared, w7_shared), dz2_own, kept, (dio_own,) = middle_call(
        False, attn[7 * D :], [x_lo, x_hi, *cot_in, io_own], ready, [like(io_own.shape, bf16)]
    )
    io_came, dio_own = lax.optimization_barrier((io_came, dio_own))
    _, dz2_shared, kept_shared, (dio_mine, dio_give) = middle_call(
        True, w7_shared, [x1_shared, cot_shared, io_mine, io_came], [], [half_heads] * 2
    )
    kept = [io_own, io_mine, io_came] + kept
    dz2, kept = (dz2_own, dz2_shared), kept + kept_shared
    dio_in = [dio_own, dio_mine, to_shared(dio_give)]

    def rest_of_middle(kept):
        return pl.pallas_call(
            middle_grads,
            out_shape=(like((D, D)), like((HIDDEN, D)), like((HIDDEN, D)), like((8, D)))
            + (pair_block,) * 2
            + (like((rows // 2, PAIR), bf16),) * 2,
            in_specs=[VMEM] * 24,
            out_specs=(VMEM,) * (4 + Z),
            compiler_params=small,
            name="middle_grads",
        )(vec, *kept)

    if fast:
        half_f, half_b = like((2 * rows, PAIR)), like((2 * rows, PAIR), bf16)
        near, far_lo, far_hi = (t + s for t, s in zip(turned, ((near_p, near_top), (lo_p, lo_top), (hi_p, hi_top))))
        g_w7, g_up, g_down, g_vec_b, *out_blocks = rest_of_middle(kept)
        mlp_keep, mlp_give = pack_call(
            mlp_pack, (g_up, g_down), MLP_PACK, [pltpu.VMEM((2 * HIDDEN, D), f32)], small, "mlp_pack"
        )
        dio_in[2], mlp_give = lax.optimization_barrier((dio_in[2], mlp_give))
        lo_h, lo_hc, hi_h, hi_hc, dio_t, ds, dkv = backward_call(
            [far_lo, far_hi], (half_f, half_b) * 2, True, False, dio_in, []
        )
        dq_far, g_far = pl.pallas_call(
            item_far,
            out_shape=(like((SLOTS * SLOT_HEADS, HEAD_DIM, q_rows)), like((SLOTS, D, 2 * LANES))),
            in_specs=[VMEM] * 6,
            out_specs=(VMEM,) * 2,
            compiler_params=small,
            name="item_far",
        )(far_lo[0], far_lo[2], far_hi[0], far_hi[2], ds, dkv)
        from_c = [swap(a, "core") for a in (lo_hc, hi_hc)]
        from_c, dq_far = lax.optimization_barrier((from_c, dq_far))
        sent = [(a + b.astype(f32)).astype(bf16) for a, b in zip((lo_h, hi_h), from_c)]
        sent, dio_t, mlp_give = lax.optimization_barrier((sent, dio_t, mlp_give))
        from_h = [swap(a, "zh") for a in sent]
        mlp_got = swap(mlp_give, "core")
        *own, lo_c, hi_c, g_item = backward_call(
            [near],
            (half_f,) * 2 + (half_b,) * 2,
            False,
            True,
            [dio_t, *dz2],
            tasked(q_w) + shared(dq_far, g_far),
        )
        mlp_got, g_item = lax.optimization_barrier((mlp_got, g_item))
        mlp_total, mlp_came = over_plane(mlp_keep, mlp_got.astype(f32))
        from_h, to_c, out_blocks, mlp_came = lax.optimization_barrier((from_h, (lo_c, hi_c), out_blocks, mlp_came))
        for a in mlp_came:
            mlp_total = mlp_total + a.astype(f32)
        from_c = [swap(a, "core") for a in to_c]
        own = [(a + b.astype(f32) + c.astype(f32)).astype(bf16) for a, b, c in zip(own, from_c, from_h)]
    else:
        (xt, v, kt), = turned
        at_query = (lax.axis_index("zh") * 2 + lax.axis_index("core")) * q_rows
        xt_q = lax.dynamic_slice_in_dim(xt, at_query, q_rows, 1)
        g_item, dx_t, dxq_t = backward_call(
            [(xt, v, kt, all_p, all_top)],
            (like((PAIR, all_rows)), like((PAIR, q_rows))),
            True,
            True,
            dio_in,
            tasked(q_w) + shared(xt_q),
        )
        own = lax.psum_scatter(dx_t.T, ("zh", "core"), scatter_dimension=0, tiled=True) + dxq_t.T
        own = own + jnp.concatenate([dz2[0], jnp.pad(dz2[1], ((0, q_rows // 2), (0, 0)))], axis=1)
        own = jnp.split(own.astype(bf16), 2)
        g_w7, g_up, g_down, g_vec_b, *out_blocks = rest_of_middle(kept)
    dx_blocks = [own[s // 2][s % 2 * rows : (s % 2 + 1) * rows] for s in range(Z)]
    came = [to_task(jnp.concatenate([a, b], axis=0), i) for i, (a, b) in enumerate(zip(dx_blocks, out_blocks)) if i]
    dx_in = dx_blocks[:1] + [a[:rows] for a in came]
    out = pl.pallas_call(
        out_collect,
        out_shape=cells_low,
        in_specs=[VMEM] * Z,
        out_specs=VMEM,
        scratch_shapes=[pltpu.VMEM((FEAT, rows, D), bf16)],
        compiler_params=small,
        name="out_collect",
    )(out_blocks[0], *[a[rows:] for a in came])

    g_feat, g_vec_a, dz1, dqkv = pl.pallas_call(
        functools.partial(feat_backward, rows),
        out_shape=(like((4 * D, D)), like((8, D)), like((cells_n, D)), like((3, cells_n, D), bf16)),
        in_specs=[VMEM] * (8 + Z),
        out_specs=(VMEM,) * 4,
        scratch_shapes=[
            pltpu.VMEM((cells_n, D), f32),
            pltpu.VMEM((cells_n, D), f32),
            pltpu.VMEM((cells_n, D), f32),
            pltpu.VMEM((FEAT, rows, D), f32),
        ],
        compiler_params=small,
        name="feat_backward",
    )(xhat1, rstd1, cells, qkv, fo, probs, attn[: 4 * D], vec, *dx_in)

    share = (w_attn.shape[0], w_mlp.shape[0], vectors.shape[0])
    if fast:
        grads = (g_feat, g_item, g_w7, g_vec_a, g_vec_b)
        attn_share, mlp_share, vec_share, dz1 = sum_packed(grads, mlp_total, share, dz1, small)
    else:
        grads = (g_feat, g_item, g_w7, g_up, g_down, g_vec_a, g_vec_b)
        attn_share, mlp_share, vec_share, dz1 = sum_any(grads, share, dz1, small)

    dcell = pl.pallas_call(
        cell_out,
        out_shape=like((cells_n, D)),
        in_specs=[VMEM] * 3,
        out_specs=VMEM,
        compiler_params=small,
        name="cell_out",
    )(dz1, dqkv, attn[: 3 * D])

    def rows_first(a):
        return a.reshape(FEAT, rows, D).transpose(1, 0, 2)[None]

    return (
        rows_first(out),
        rows_first(dcell),
        attn_share,
        mlp_share,
        vec_share,
    )


def solution(mesh):
    blk_n, rep_n = mesh.devices.shape
    fine = Mesh(mesh.devices.reshape(blk_n // (2 * Z), 2, 2, 2, rep_n), BLK + ("rep",))
    every = BLK + ("rep",)
    in_specs = (
        P("rep", BLK, None, None),
        P("rep", BLK),
        P("rep", BLK),
        P("rep", None),
        P(every, None),
        P(every, None),
        P(every),
        P("rep", BLK, None, None),
    )
    out_specs = (
        P("rep", BLK, None, None),
        P("rep", BLK, None, None),
        P(every, None),
        P(every, None),
        P(every),
    )
    return jax.shard_map(local, mesh=fine, in_specs=in_specs, out_specs=out_specs, check_vma=False)
```

```python
import functools
import math

import jax
import jax.numpy as jnp
from jax import lax
from jax.experimental import pallas as pl
from jax.experimental.pallas import tpu as pltpu
from jax.sharding import Mesh
from jax.sharding import PartitionSpec as P

D = 192
HEADS = 6
HEAD_DIM = 32
HIDDEN = 384
FEAT = 6
TABLES = 16

Z = 4
SLOTS = 3
SLOT_HEADS = 3
SLOT_COLS = SLOT_HEADS * HEAD_DIM
PAIR = 2 * D
LANES = 128
KEY_TILE = 256

EPS = 1e-05
FAR = -1e30
BLOCKED = -(2.0**100)
SCALE = HEAD_DIM ** (-0.5)
LOG2E = 1.4426950408889634
SCALE2 = SCALE * LOG2E

bf16 = jnp.bfloat16
f32 = jnp.float32
BLK = ("zh", "zl", "y", "core")
FAN = ("zh", "zl", "y", "rep")
TASK_AXES = ("zl", "y")
Z_AXES = ("zh", "zl")
PLANE_AXES = ("y", "rep")
TASK_ORDER = (0, 2, 1, 3)
FAR_ORDER = (0, 3, 2, 1)


def dot(a, b):
    return lax.dot_general(a, b, (((1,), (0,)), ((), ())), preferred_element_type=f32)


def dot_t(a, b):
    return lax.dot_general(a, b, (((1,), (1,)), ((), ())), preferred_element_type=f32)


def t_dot(a, b):
    return lax.dot_general(a, b, (((0,), (0,)), ((), ())), preferred_element_type=f32)


def loop(count, body, carry=None):
    if count > 8:
        return lax.fori_loop(0, count, body, carry)
    for i in range(count):
        carry = body(i, carry)
    return carry


def span(i, size):
    if isinstance(i, int):
        return slice(i * size, (i + 1) * size)
    return pl.ds(pl.multiple_of(i * size, size), size)


def task_place():
    return lax.axis_index("zl") * 2 + lax.axis_index("y")


def partner(step):
    return lax.bitwise_xor(task_place(), TASK_ORDER[step])


def own_feature(t):
    return (3 * t + 1) // 2 if isinstance(t, int) else lax.div(3 * t + 1, 2)


def shared_feature(t):
    return 1 + 3 * (t // 2) if isinstance(t, int) else 1 + 3 * lax.div(t, 2)


def is_odd():
    return lax.axis_index("y") == 1


def normed(z):
    centre = z - jnp.mean(z, axis=-1, keepdims=True)
    rstd = lax.rsqrt(jnp.mean(centre * centre, axis=-1, keepdims=True) + EPS)
    return centre * rstd, rstd


def norm_back(xhat, rstd, gain, grad):
    scaled = grad * gain
    mean_a = jnp.mean(scaled, axis=-1, keepdims=True)
    mean_b = jnp.mean(scaled * xhat, axis=-1, keepdims=True)
    return rstd * (scaled - mean_a - xhat * mean_b)


def col_sum(a):
    return jnp.sum(a, axis=0, keepdims=True)


def head_ones():
    a = lax.broadcasted_iota(jnp.int32, (D, D), 0) // HEAD_DIM
    b = lax.broadcasted_iota(jnp.int32, (D, D), 1) // HEAD_DIM
    return (a == b).astype(bf16)


def row_to_col(row, size):
    a = lax.broadcasted_iota(jnp.int32, (size, size), 0)
    b = lax.broadcasted_iota(jnp.int32, (size, size), 1)
    return jnp.sum(jnp.where(a == b, row, 0.0), axis=1, keepdims=True)


def feat_probs(query, keys, valid, ones, rows):
    prod = (keys * query[None]).reshape(FEAT * rows, D).astype(bf16)
    scores = dot(prod, ones).reshape(FEAT, rows, D)
    scores = [jnp.where(valid[g], scores[g] * SCALE2, FAR) for g in range(FEAT)]
    top = functools.reduce(jnp.maximum, scores)
    powers = [jnp.exp2(s - top) for s in scores]
    total = functools.reduce(jnp.add, powers)
    inv = 1.0 / total
    return [p * inv for p in powers]


def make_pairs(full, pair_s):
    rows = pair_s.shape[1]
    for t in range(Z):
        f, g = own_feature(t) * rows, shared_feature(t) * rows
        pair_s[t] = jnp.concatenate([full[f : f + rows, :], full[g : g + rows, :]], axis=1)


def read_pairs(pair_refs, full_s):
    for s in range(Z):
        t = partner(s)
        both = pair_refs[s][...].astype(f32)
        full_s[own_feature(t)] += both[:, :D]
        full_s[shared_feature(t)] += both[:, D:]


def feat_forward(rows, cells_ref, cot_ref, count_ref, w_ref, vec_ref, xhat_ref, rstd_ref, qkv_ref, fo_ref, prob_ref, *rest):
    x_refs, cot_out, (pair_s, cot_s, half_s) = rest[:Z], rest[Z], rest[Z + 1 :]
    cells = cells_ref[...]
    for m in range(3):
        qkv_ref[m] = dot(cells, w_ref[m * D : (m + 1) * D, :]).astype(bf16)
    counts = count_ref[...]
    valid = [counts > g for g in range(FEAT)]
    ones = head_ones()
    keys = qkv_ref[1].astype(f32).reshape(FEAT, rows, D)
    values = qkv_ref[2].astype(f32).reshape(FEAT, rows, D)
    for f in range(FEAT):
        at = slice(f * rows, (f + 1) * rows)
        probs = feat_probs(qkv_ref[0, at, :].astype(f32), keys, valid, ones, rows)
        for g in range(FEAT):
            prob_ref[f, g] = probs[g]
        mixed = functools.reduce(jnp.add, [probs[g] * values[g] for g in range(FEAT)])
        fo_ref[at, :] = mixed.astype(bf16)
    z1 = cells.astype(f32) + dot(fo_ref[...], w_ref[3 * D : 4 * D, :]) + vec_ref[6:7, :]
    xhat, rstd = normed(z1)
    xhat_ref[...] = xhat
    rstd_ref[...] = jnp.broadcast_to(rstd, rstd_ref.shape)
    x1 = (xhat * vec_ref[0:1, :] + vec_ref[3:4, :]).astype(bf16)
    make_pairs(x1, pair_s)
    cot = cot_ref[...]
    make_pairs(cot, cot_s)
    for t in range(Z):
        f = own_feature(t) * rows
        half_s[t] = jnp.concatenate([cot[f : f + rows // 2, :], cot[f + rows // 2 : f + rows, :]], axis=1)
    cot_out[...] = cot_s[task_place()]
    for s in range(Z):
        x_refs[s][:rows, :] = pair_s[partner(s)]
    x_refs[1][rows:, :] = cot_s[partner(1)]
    for s in (2, 3):
        x_refs[s][rows:, :] = half_s[partner(s)]


def key_order(h_n):
    h, core = lax.axis_index("zh"), lax.axis_index("core")
    if h_n == 2:
        near = [(h, c, s) for c in (core, 1 - core) for s in range(Z)]
        return near + [(1 - h, c, s) for pair in ((0, 1), (2, 3)) for c in (core, 1 - core) for s in pair]
    return [(a, b, s) for a in range(h_n) for b in range(2) for s in range(Z)]


def item_prepare(h_n, w_ref, code_ref, kv_w_ref, kv_wt_ref, q_w_ref, key_bias_ref, hot_ref):
    zero = jnp.zeros((D, SLOT_COLS), bf16)
    lane_pad = jnp.zeros((D, LANES - SLOT_COLS), bf16)
    mats = []
    for m in range(3):
        w = w_ref[m * D : (m + 1) * D, :]
        a, b = w[:, :SLOT_COLS], w[:, SLOT_COLS:]
        mats.append([(a, zero), (b, zero), (zero, jnp.where(is_odd(), b, a))])
    for p in range(SLOTS):
        for side in range(2):
            at = slice(side * D, (side + 1) * D)
            q_w_ref[p, at, :] = jnp.concatenate([mats[0][p][side], lane_pad], axis=1)
            kv_w_ref[p, at, :LANES] = jnp.concatenate([mats[1][p][side], lane_pad], axis=1)
            kv_w_ref[p, at, LANES:] = jnp.concatenate([mats[2][p][side], lane_pad], axis=1)
        kv_wt_ref[p] = kv_w_ref[p].T

    rows = code_ref.shape[1]
    per = LANES // rows
    place = lax.broadcasted_iota(jnp.int32, (LANES, LANES), 0) - SLOT_COLS
    tagged = (place >= 0) & (place < TABLES)

    def code_rows(blocks):
        codes = [code_ref[pl.ds((h * Z + partner(s)) * 2 + c, 1), :] for h, c, s in blocks]
        code = jnp.concatenate(codes, axis=1)
        table = jnp.floor(code * 0.5)
        return table.astype(jnp.int32), code - 2.0 * table

    order = key_order(h_n)
    for i in range(len(order) // per):
        table, train = code_rows(order[i * per : (i + 1) * per])
        match = (place == table) & (train > 0.5)
        bias = jnp.where(tagged, jnp.where(match, 0.0, BLOCKED), 0.0)
        key_bias_ref[span(i, LANES), :] = bias.T.astype(bf16)
    own = [(lax.axis_index("zh"), lax.axis_index("core"), s) for s in range(Z)]
    for i in range(Z // per):
        table, _ = code_rows(own[i * per : (i + 1) * per])
        hot = jnp.where(place == table, 1.0, 0.0)
        hot_ref[span(i, LANES), :] = hot.T


def only_head(a, h, keep_rest):
    lane = lax.broadcasted_iota(jnp.int32, a.shape, 1)
    mine = (lane >= h * HEAD_DIM) & (lane < (h + 1) * HEAD_DIM)
    if keep_rest:
        mine = mine | (lane >= SLOT_COLS)
    return jnp.where(mine, a, jnp.zeros_like(a))


def each_tile(part_refs, body):
    base = 0
    for ref in part_refs:
        size = min(KEY_TILE, ref.shape[0])

        def one(i, carry, ref=ref, base=base, size=size):
            start = base + i * size
            if not isinstance(i, int):
                start = pl.multiple_of(start, size)
            body(ref[span(i, size), :], pl.ds(start, size))

        loop(ref.shape[0] // size, one)
        base += ref.shape[0]


def take(refs, count):
    return refs[:count], refs[count:]


def at_slot(ref, slot, count):
    return ref.at[slot * count : (slot + 1) * count] if isinstance(slot, int) else ref


def when(condition, body):
    if isinstance(condition, bool):
        if condition:
            body()
    else:
        pl.when(condition)(body)


def task_columns(slot, h):
    start = slot * SLOT_COLS + h * HEAD_DIM
    return pl.ds(start if isinstance(slot, int) else pl.multiple_of(start, HEAD_DIM), HEAD_DIM)


def slots_of(grid):
    return [pl.program_id(0)] if grid else list(range(SLOTS))


def task_lanes(slot):
    if isinstance(slot, int):
        return slice(0, 2 * LANES) if slot < 2 else slice(PAIR - 2 * LANES, PAIR)
    return slice(0, PAIR)


def task_feature(slot):
    if isinstance(slot, int):
        return slice(slot // 2 * D, (slot // 2 + 1) * D), [False, True, is_odd()][slot]
    upper = jnp.where(slot == 2, lax.axis_index("y"), slot) == 1
    return pl.ds(pl.multiple_of(lax.div(slot, 2) * D, D), D), upper


def head_rows(h):
    return slice(h * HEAD_DIM, (h + 1) * HEAD_DIM)


def item_forward(n_parts, n_query, first, last, grid, *refs):
    parts, refs = take(refs, n_parts)
    (kv_w_all, kv_wt_all, key_bias_ref), refs = take(refs, 3)
    if first:
        (q_w_all, hot_ref), refs = take(refs, 2)
        query_parts = parts[:n_query]
        if grid:
            query_parts, refs = take(refs, 1)
    else:
        (q_all, top_in, total_in, mixed_in), refs = take(refs, 4)
    (p_all, top_ref), refs = take(refs, 2)
    if first:
        (q_all,), refs = take(refs, 1)
    if last:
        (end_ref, inv_ref, mixed_ref), refs = take(refs, 3)
        io_refs, refs = take(refs, 3)
    elif first:
        (total_ref, mixed_ref), refs = take(refs, 2)
    else:
        (end_ref, total_ref, mixed_ref), refs = take(refs, 3)
    k_s, vt_s, s_s = refs
    keys = k_s.shape[1]
    queries = q_all.shape[1]
    tile = LANES
    fold = (tile // 8, 8, queries)
    slots = slots_of(grid)
    heads = [(i, slot, h) for i, slot in enumerate(slots) for h in range(SLOT_HEADS)]

    queries_low = []
    for i, slot in enumerate(slots):
        kv_w = at_slot(kv_w_all, slot, 1)
        kv_wt = at_slot(kv_wt_all, slot, 1)
        lanes = task_lanes(slot)

        def project(x, at):
            k = dot(x[:, lanes], kv_w[0, lanes, :LANES])
            k_s[i, at, :] = (k + key_bias_ref[at, :].astype(f32)).astype(bf16)
            vt_s[i, :, at] = dot_t(kv_wt[0, LANES:, lanes], x[:, lanes]).astype(bf16)

        each_tile(parts, project)
        q_ref = at_slot(q_all, slot, 1)
        if first:
            q_w = at_slot(q_w_all, slot, 1)
            query = [dot(x[:, lanes], q_w[0, lanes, :]) for x in query_parts]
            query = (jnp.concatenate(query, axis=0) * SCALE2 + hot_ref[...]).astype(bf16)
            q_ref[0] = query
        else:
            query = q_ref[0]
        queries_low.append(query)

    tops = []
    for i, slot, h in heads:
        query_h = only_head(queries_low[i], h, True)

        def score(n, top):
            at = span(n, tile)
            s = dot_t(k_s[i, at, :], query_h)
            s_s[i * SLOT_HEADS + h, at, :] = s
            return jnp.maximum(top, jnp.max(s.reshape(fold), axis=0))

        top = loop(keys // tile, score, jnp.full((8, queries), 2.0 * BLOCKED, f32))
        tops.append(jnp.max(top, axis=0, keepdims=True))

    totals = []
    for (i, slot, h), top in zip(heads, tops):
        p_ref = at_slot(p_all, slot, SLOT_HEADS)

        def power(n, total):
            at = span(n, tile)
            p = jnp.exp2(s_s[i * SLOT_HEADS + h, at, :] - top)
            p_ref[h, at, :] = p.astype(bf16)
            return total + jnp.sum(p.reshape(fold), axis=0)

        total = loop(keys // tile, power, jnp.zeros((8, queries), f32))
        totals.append(jnp.sum(total, axis=0, keepdims=True))

    def clear():
        mixed_ref[...] = jnp.zeros_like(mixed_ref)

    if last:
        when(slots[0] == 0, clear)
    for (i, slot, h), top, total in zip(heads, tops, totals):
        mixed = dot(vt_s[i, head_rows(h), :], at_slot(p_all, slot, SLOT_HEADS)[h])
        head = pl.ds(slot * SLOT_HEADS + h, 1)
        cols = task_columns(slot, h)
        top_ref[head, :] = top
        if not first:
            end = jnp.maximum(top, top_in[head, :])
            now, before = jnp.exp2(top - end), jnp.exp2(top_in[head, :] - end)
            total = total * now + total_in[head, :] * before
            mixed = mixed * now + mixed_in[cols, :] * before
            end_ref[head, :] = end
        elif last:
            end_ref[head, :] = top
        if last:
            inv = 1.0 / total
            inv_ref[head, :] = inv
            mixed_ref[cols, :] = mixed * inv
        else:
            total_ref[head, :] = total
            mixed_ref[cols, :] = mixed

    def finish():
        half = queries // 2
        io_refs[0][...] = mixed_ref[:D, :].T.astype(bf16)
        shared = mixed_ref[D : D + SLOT_COLS, :].T.astype(bf16)
        io_refs[1][...] = shared[:half]
        io_refs[2][...] = shared[half:]

    if last:
        when(slots[-1] == SLOTS - 1, finish)


def item_turn(counts, grid, *refs):
    groups = []
    for count in counts:
        parts, refs = take(refs, count)
        groups.append(parts)
    (kv_w_all, kv_wt_all, q_all), refs = take(refs, 3)
    qt_all, refs = refs[0], refs[1:]
    for slot in slots_of(grid):
        at_slot(qt_all, slot, 1)[0] = at_slot(q_all, slot, 1)[0].astype(f32).T.astype(bf16)
        kv_w = at_slot(kv_w_all, slot, 1)
        kv_wt = at_slot(kv_wt_all, slot, 1)
        lanes = task_lanes(slot)
        for g, parts in enumerate(groups):
            xt_ref, v_all, kt_all = refs[3 * g : 3 * g + 3]
            v_ref, kt_ref = at_slot(v_all, slot, 1), at_slot(kt_all, slot, 1)

            def one(x, at):
                v_ref[0, at, :] = dot(x[:, lanes], kv_w[0, lanes, LANES:]).astype(bf16)
                kt_ref[0, :, at] = dot_t(kv_wt[0, :LANES, lanes], x[:, lanes]).astype(bf16)

            def turn(x, at):
                xt_ref[:, at] = x.astype(f32).T.astype(bf16)

            each_tile(parts, one)
            when(slot == 0, lambda: each_tile(parts, turn))


def swap_halves(w):
    other = jnp.concatenate([w[SLOT_COLS:], w[:SLOT_COLS]], axis=0)
    return jnp.where(is_odd(), other, w)


def row_middle(shared, w_ref, m_ref, vec_ref, *refs):
    if shared:
        (x1_ref, cot_in, mine_ref, came_ref), refs = refs[:4], refs[4:]
        x1, cot = x1_ref[...], cot_in[...]
        halves = ((mine_ref[...], w_ref[:SLOT_COLS, :]), (came_ref[...], w_ref[SLOT_COLS:, :]))
    else:
        (lo_ref, hi_ref, *cot_refs, own_ref), refs = refs[: 3 + Z], refs[3 + Z :]
        ready_refs, refs = refs[:3], refs[3:]
        lo = lo_ref[...].astype(f32)
        x1 = jnp.concatenate([lo[:, :D], hi_ref[:, :D].astype(f32)], axis=0)
        near = [ref[...].astype(f32) for ref in cot_refs[:2]]
        wide = [ref[...].astype(f32) for ref in cot_refs[2:]]
        cot = [a[:, :D] for a in near] + [b for a in wide for b in (a[:, :D], a[:, D:])]
        cot = jnp.concatenate(cot, axis=0)
        ready_refs[0][...] = lo[:, D:]
        ready_refs[1][...] = jnp.concatenate([a[:, D:] for a in near], axis=0)
        ready_refs[2][...] = swap_halves(w_ref[...])
        halves = ((own_ref[...], w_ref[...]),)
    dz2_ref, low_refs, full_refs, dio_refs = refs[0], refs[1:7], refs[7:11], refs[11:]
    dt2_ref, x2_ref, du_ref, hid_ref, dm_ref, cot_ref = low_refs
    xhat3_ref, dz3_ref, xhat2_ref, dx2_ref = full_refs
    cot_ref[...] = cot.astype(bf16)
    z2 = x1
    for io, w7 in halves:
        z2 = z2 + dot(io, w7)
    xhat2, rstd2 = normed(z2)
    xhat2_ref[...] = xhat2
    x2 = xhat2 * vec_ref[1:2, :] + vec_ref[4:5, :]
    x2_low = x2.astype(bf16)
    x2_ref[...] = x2_low
    up_w = m_ref[:HIDDEN, :]
    down_w = m_ref[HIDDEN:, :]
    up = dot_t(x2_low, up_w)
    c0 = 0.7978845608028654
    c1 = 0.044715
    up2 = up * up
    tanh = jnp.tanh(c0 * up * (1.0 + c1 * up2))
    half_one = 0.5 + 0.5 * tanh
    hid = (up * half_one).astype(bf16)
    hid_ref[...] = hid
    slope = half_one + 0.5 * up * (1.0 - tanh * tanh) * (c0 + 3.0 * c0 * c1 * up2)
    z3 = x2 + dot(hid, down_w) + vec_ref[7:8, :]
    xhat3, rstd3 = normed(z3)
    xhat3_ref[...] = xhat3
    dz3 = norm_back(xhat3, rstd3, vec_ref[2:3, :], cot)
    dz3_ref[...] = dz3
    dm = dz3.astype(bf16)
    dm_ref[...] = dm
    du = (dot_t(dm, down_w) * slope).astype(bf16)
    du_ref[...] = du
    dx2 = dz3 + dot(du, up_w)
    dx2_ref[...] = dx2
    dz2 = norm_back(xhat2, rstd2, vec_ref[1:2, :], dx2)
    dz2_ref[...] = dz2
    dt2 = dz2.astype(bf16)
    dt2_ref[...] = dt2
    for ref, (_, w7) in zip(dio_refs, halves):
        ref[...] = dot_t(dt2, w7).astype(bf16)


def item_backward(n_groups, n_outs, first, last, grid, *refs):
    groups = []
    for _ in range(n_groups):
        group, refs = take(refs, 5)
        groups.append(group)
    if first:
        dio_refs, refs = take(refs, 3)
    else:
        (dt_ref, dz2_own, dz2_shared), refs = take(refs, 3)
    (qt_all, iot_ref, end_ref, inv_ref, kv_w_all), refs = take(refs, 5)
    if last:
        (q_w_all,), refs = take(refs, 1)
        if grid:
            (xtq_ref,), refs = take(refs, 1)
    if not first:
        (dq_past, g_past), refs = take(refs, 2)
    if grid:
        gw_ref, dx_ref, dxq_ref, dt_ref, dkv_s, ds_s = refs
    else:
        out_refs, refs = take(refs, n_outs)
        if last:
            gw_ref, dx_ref, dkv_s, ds_s = refs
            dxq_ref = dx_ref.at[:, : qt_all.shape[2]]
        else:
            dt_ref, ds_s, dkv_s, dx_ref = refs
    queries = qt_all.shape[2]

    def start():
        if first:
            dt_ref[:D, :] = dio_refs[0][...].astype(f32).T
            shared = jnp.concatenate([dio_refs[1][...], dio_refs[2][...]], axis=0)
            dt_ref[D : D + SLOT_COLS, :] = shared.astype(f32).T
        dx_ref[...] = jnp.zeros_like(dx_ref)
        if grid:
            dxq_ref[...] = jnp.zeros_like(dxq_ref)
        if last:
            gw_ref[...] = jnp.zeros_like(gw_ref)

    slots = slots_of(grid)
    when(slots[0] == 0, start)
    heads = [(i, slot, h) for i, slot in enumerate(slots) for h in range(SLOT_HEADS)]
    blank = jnp.zeros((HEAD_DIM, queries), bf16)
    base = 0
    grads = []
    for xt_ref, v_all, kt_all, p_all, top_ref in groups:
        keys = v_all.shape[1]
        for i, slot, h in heads:
            head = pl.ds(slot * SLOT_HEADS + h, 1)
            cols = task_columns(slot, h)
            scale = jnp.exp2(top_ref[head, :] - end_ref[head, :]) * inv_ref[head, :]
            scaled = dt_ref[cols, :] * scale
            delta = jnp.sum(scaled * iot_ref[cols, :], axis=0, keepdims=True)
            grad = scaled.astype(bf16)
            grads.append(grad)
            alone = jnp.concatenate([grad if j == h else blank for j in range(LANES // HEAD_DIM)], axis=0)
            v_ref, p_ref = at_slot(v_all, slot, 1), at_slot(p_all, slot, SLOT_HEADS)

            def score(n, carry):
                at = span(n, KEY_TILE)
                dp = dot(v_ref[0, at, :], alone)
                ds = (p_ref[h, at, :].astype(f32) * (dp - delta)).astype(bf16)
                ds_s[i * SLOT_HEADS + h, span(base // KEY_TILE + n, KEY_TILE), :] = ds
                return carry

            loop(keys // KEY_TILE, score, 0)
        base += keys

    if first:
        dq_heads = [jnp.zeros((HEAD_DIM, queries), f32)] * len(heads)
    else:
        dq_heads = [dq_past[n] for n in range(len(heads))]
    base = 0
    for g, (xt_ref, v_all, kt_all, p_all, top_ref) in enumerate(groups):
        keys = v_all.shape[1]
        for n, (i, slot, h) in enumerate(heads):
            kt_ref, p_ref = at_slot(kt_all, slot, 1), at_slot(p_all, slot, SLOT_HEADS)
            grad = grads[g * len(heads) + n]
            query_t = at_slot(qt_all, slot, 1)[0, head_rows(h), :]
            rows_k, rows_v = head_rows(h), slice(LANES + h * HEAD_DIM, LANES + (h + 1) * HEAD_DIM)

            def sums(t, dq_t):
                at, put = span(t, KEY_TILE), span(base // KEY_TILE + t, KEY_TILE)
                ds = ds_s[i * SLOT_HEADS + h, put, :]
                dkv_s[i, rows_v, put] = dot_t(grad, p_ref[h, at, :]).astype(bf16)
                dkv_s[i, rows_k, put] = (dot_t(query_t, ds) * (1.0 / LOG2E)).astype(bf16)
                return dq_t + dot(kt_ref[0, head_rows(h), at], ds) if last else dq_t

            dq_heads[n] = loop(keys // KEY_TILE, sums, dq_heads[n])
        base += keys

    unused = jnp.zeros((LANES - SLOT_COLS, base), bf16)
    for i, slot in enumerate(slots):
        kv_w = at_slot(kv_w_all, slot, 1)
        feature, upper = task_feature(slot)
        dkv_s[i, SLOT_COLS:LANES, :] = unused
        dkv_s[i, LANES + SLOT_COLS :, :] = unused
        base = 0
        g_kv = jnp.zeros((D, 2 * LANES), f32) if first else g_past[i]
        for xt_ref, v_all, kt_all, p_all, top_ref in groups:
            keys = v_all.shape[1]

            def back(n, carry):
                put = span(base // KEY_TILE + n, KEY_TILE)
                dx_ref[feature, put] += dot(kv_w[0, feature, :], dkv_s[i, :, put])
                return carry

            loop(keys // KEY_TILE, back, 0)
            if last:
                g_kv = g_kv + dot_t(xt_ref[feature, :], dkv_s[i, :, base : base + keys])
            base += keys
        if not last:
            continue
        rest = jnp.zeros((LANES - SLOT_COLS, queries), f32)
        dq_t = jnp.concatenate(dq_heads[i * SLOT_HEADS : (i + 1) * SLOT_HEADS] + [rest], axis=0)
        found = [(1, g_kv[:, :LANES]), (2, g_kv[:, LANES:])]
        dq = (dq_t * SCALE).astype(bf16)
        dxq_ref[feature, :] += dot(at_slot(q_w_all, slot, 1)[0, feature, :], dq)
        xq = xtq_ref[feature, :] if grid else groups[0][0][feature, :queries]
        found.append((0, dot_t(xq, dq)))
        blank = jnp.zeros((D, SLOT_COLS), f32)
        for m, g in found:
            g = g[:, :SLOT_COLS]
            if upper is not True:
                g_low = jnp.concatenate([g, blank], axis=1)
            if upper is not False:
                g_high = jnp.concatenate([blank, g], axis=1)
            whole = g_high if upper is True else g_low if upper is False else jnp.where(upper, g_high, g_low)
            gw_ref[m * D : (m + 1) * D, :] += whole

    if not grid:
        base = 0
        for n, ref in enumerate(out_refs):
            count = ref.shape[0]
            total = dx_ref[:, base : base + count].T
            if last and n < 2:
                shared = dz2_shared[...] if n == 0 else jnp.zeros((count, D), f32)
                total = total + jnp.concatenate([dz2_own[base : base + count, :], shared], axis=1)
            ref[...] = total.astype(ref.dtype)
            base += count


def item_far(*refs):
    groups = (refs[:2], refs[2:4])
    ds_ref, dkv_ref, dq_ref, g_ref = refs[4:]
    for slot in range(SLOTS):
        feature, _ = task_feature(slot)
        base = 0
        for xt_ref, kt_ref in groups:
            at = slice(base, base + xt_ref.shape[1])
            g = dot_t(xt_ref[feature, :], dkv_ref[slot, :, at])
            g_ref[slot] = g_ref[slot] + g if base else g
            for h in range(SLOT_HEADS):
                n = slot * SLOT_HEADS + h
                dq = dot(kt_ref[slot, head_rows(h), :], ds_ref[n, at, :])
                dq_ref[n] = dq_ref[n] + dq if base else dq
            base += xt_ref.shape[1]


def feat_backward(rows, xhat1_ref, rstd1_ref, cells_ref, qkv_ref, fo_ref, prob_ref, w_ref, vec_ref, *refs):
    dx_refs, refs = refs[:Z], refs[Z:]
    gw_ref, gvec_ref, dz1_ref, dqkv_ref, dk_s, dv_s, dfo_s, dx_s = refs
    xhat1, rstd1 = xhat1_ref[...], rstd1_ref[...]
    dx_s[...] = jnp.zeros_like(dx_s)
    read_pairs(dx_refs, dx_s)
    dx1 = dx_s[...].reshape(FEAT * rows, D)
    gvec_ref[...] = jnp.zeros_like(gvec_ref)
    gvec_ref[0:1, :] = col_sum(dx1 * xhat1)
    gvec_ref[3:4, :] = col_sum(dx1)
    dz1 = norm_back(xhat1, rstd1, vec_ref[0:1, :], dx1)
    gvec_ref[6:7, :] = col_sum(dz1)
    dz1_ref[...] = dz1
    dt1 = dz1.astype(bf16)
    gw_ref[3 * D : 4 * D, :] = t_dot(fo_ref[...], dt1)
    dfo_s[...] = dot_t(dt1, w_ref[3 * D : 4 * D, :])
    ones = head_ones()
    keys = qkv_ref[1].astype(f32).reshape(FEAT, rows, D)
    values = qkv_ref[2].astype(f32).reshape(FEAT, rows, D)
    dk_s[...] = jnp.zeros_like(dk_s)
    dv_s[...] = jnp.zeros_like(dv_s)
    for f in range(FEAT):
        at = slice(f * rows, (f + 1) * rows)
        query = qkv_ref[0, at, :].astype(f32)
        probs = [prob_ref[f, g] for g in range(FEAT)]
        dfo = dfo_s[at, :].astype(bf16).astype(f32)
        prod = (values * dfo[None]).reshape(FEAT * rows, D).astype(bf16)
        dfp = dot(prod, ones).reshape(FEAT, rows, D)
        mean = functools.reduce(jnp.add, [probs[g] * dfp[g] for g in range(FEAT)])
        dq = jnp.zeros((rows, D), f32)
        for g in range(FEAT):
            here = slice(g * rows, (g + 1) * rows)
            ds = probs[g] * (dfp[g] - mean)
            dq = dq + ds * keys[g]
            dk_s[here, :] += ds * query
            dv_s[here, :] += probs[g] * dfo
        dqkv_ref[0, at, :] = (dq * SCALE).astype(bf16)
    dqkv_ref[1] = (dk_s[...] * SCALE).astype(bf16)
    dqkv_ref[2] = dv_s[...].astype(bf16)
    for m in range(3):
        gw_ref[m * D : (m + 1) * D, :] = t_dot(cells_ref[...], dqkv_ref[m])


def cell_out(dz1_ref, dqkv_ref, w_ref, out_ref):
    total = dz1_ref[...]
    for m in range(3):
        total = total + dot_t(dqkv_ref[m], w_ref[m * D : (m + 1) * D, :])
    out_ref[...] = total


def middle_grads(vec_ref, *refs):
    (own_ref, mine_ref, came_ref), sets, refs = refs[:3], (refs[3:13], refs[13:23]), refs[23:]
    (gw_ref, gu_ref, gv_ref, gvec_ref), out_refs = refs[:4], refs[4:]
    outs = []
    for i, (dt2_ref, x2_ref, du_ref, hid_ref, dm_ref, cot_ref, *full_refs) in enumerate(sets):
        xhat3, dz3, xhat2, dx2 = [ref[...] for ref in full_refs]
        cot = cot_ref[...].astype(f32)
        outs.append(xhat3 * vec_ref[2:3, :] + vec_ref[5:6, :])
        if i == 0:
            gw = t_dot(own_ref[...], dt2_ref[...])
        else:
            gw = jnp.concatenate([t_dot(mine_ref[...], dt2_ref[...]), t_dot(came_ref[...], dt2_ref[...])], axis=0)
        gu = t_dot(du_ref[...], x2_ref[...])
        gv = t_dot(hid_ref[...], dm_ref[...])
        rows = {1: dx2 * xhat2, 2: cot * xhat3, 4: dx2, 5: cot, 7: dz3}
        if i == 0:
            gw_ref[...], gu_ref[...], gv_ref[...] = gw, gu, gv
            gvec_ref[...] = jnp.zeros_like(gvec_ref)
        else:
            gw_ref[...] += swap_halves(gw)
            gu_ref[...] += gu
            gv_ref[...] += gv
        for k, a in rows.items():
            gvec_ref[k : k + 1, :] += col_sum(a)
    rows = out_refs[0].shape[0]
    for s in range(Z):
        own = outs[0][s * rows : (s + 1) * rows]
        if s < Z // 2:
            sides = [own, outs[1][s * rows : (s + 1) * rows]]
        else:
            sides = [own[: rows // 2], own[rows // 2 :]]
        out_refs[s][...] = jnp.concatenate(sides, axis=1).astype(bf16)


def out_collect(*refs):
    pair_refs, out_ref, full_s = refs[:Z], refs[Z], refs[Z + 1]
    rows = full_s.shape[1]
    for s in range(Z):
        t = partner(s)
        both = pair_refs[s][...]
        if s < Z // 2:
            full_s[own_feature(t)] = both[:, :D]
            full_s[shared_feature(t)] = both[:, D:]
        else:
            full_s[own_feature(t), : rows // 2, :] = both[:, :D]
            full_s[own_feature(t), rows // 2 :, :] = both[:, D:]
    out_ref[...] = full_s[...].reshape(out_ref.shape)


ATTN_ROWS = 48
MLP_ROWS = 24
VEC_PART = 48
PACK = 112
HALF = LANES // 2


def pack_rows(attn, mlp, extra):
    low, high = slice(0, LANES), slice(LANES, D)
    last = jnp.concatenate([extra, mlp[16:24, high]], axis=0)
    return jnp.concatenate(
        [
            attn[:, low],
            jnp.concatenate([attn[:16, high], attn[16:32, high]], axis=1),
            jnp.concatenate([attn[32:, high], last], axis=1),
            mlp[:, low],
            jnp.concatenate([mlp[:8, high], mlp[8:16, high]], axis=1),
        ],
        axis=0,
    )


def unpack_rows(block):
    attn_high = jnp.concatenate([block[48:64, :HALF], block[48:64, HALF:], block[64:80, :HALF]], axis=0)
    mlp_high = jnp.concatenate([block[104:, :HALF], block[104:, HALF:], block[72:80, HALF:]], axis=0)
    attn = jnp.concatenate([block[:48], attn_high], axis=1)
    mlp = jnp.concatenate([block[80:104], mlp_high], axis=1)
    return attn, mlp, block[64:72, HALF:]


def share_pack(*refs):
    sources, out_refs, targets, sems = refs[:6], refs[6 : 6 + Z], refs[6 + Z : 12 + Z], refs[12 + Z]
    copies = [pltpu.make_async_copy(a, b, sems.at[i]) for i, (a, b) in enumerate(zip(sources, targets))]
    for c in copies:
        c.start()
    for c in copies:
        c.wait()
    attn, mlp, vec, tab, train, cnt = [ref[...].astype(f32) for ref in targets]
    code = tab * 2.0 + jnp.where(train > 0, 1.0, 0.0)
    lines = [jnp.concatenate([a, jnp.zeros((1, HALF - a.shape[1]), f32)], axis=1) for a in (vec, cnt)]
    extra = jnp.concatenate([lines[0], code, lines[1], jnp.zeros((5, HALF), f32)], axis=0)
    block = pack_rows(attn, mlp, extra).astype(bf16)
    for ref in out_refs:
        ref[...] = block


def hold(*refs):
    for i in range(3):
        refs[3 + i][...] = refs[i][...]


def at_place(z_step, dy, dc, dr):
    place = (
        lax.bitwise_xor(lax.axis_index("zh") * 2 + lax.axis_index("zl"), FAR_ORDER[z_step]),
        (lax.axis_index("y") + dy) % 2,
        (lax.axis_index("core") + dc) % 2,
        (lax.axis_index("rep") + dr) % 2,
    )
    z, y, c, r = place
    return ((z * 2 + y) * 2 + c) * 2 + r, place


def share_unpack(*refs):
    part_refs, refs = refs[:8], refs[8:]
    attn_ref, mlp_ref, vec_ref, code_ref, count_ref, mlp_s, vec_s = refs
    _, _, extra = unpack_rows(part_refs[0][0].astype(f32))
    table = jnp.floor(extra[1:2] * 0.5)
    counts = jnp.zeros(table.shape, f32)
    for k in range(TABLES):
        counts = jnp.where(table == k, extra[2:3, k : k + 1], counts)
    count_ref[...] = jnp.broadcast_to(row_to_col(counts, table.shape[1]), count_ref.shape)
    for i, ref in enumerate(part_refs):
        dc, dy, dr = i // 4, FAR_ORDER[i % 4] // 2, FAR_ORDER[i % 4] % 2
        for s in range(Z):
            attn, mlp, extra = unpack_rows(ref[s].astype(f32))
            index, (z, y, c, r) = at_place(s, dy, dc, dr)
            attn_ref[pl.ds(pl.multiple_of(index * ATTN_ROWS, 16), ATTN_ROWS), :] = attn.astype(bf16)
            mlp_s[pl.ds(pl.multiple_of(index * MLP_ROWS, 8), MLP_ROWS), :] = mlp
            vec_s[c * 2 + r, pl.ds(z * 2 + y, 1), :] = extra[:1]
            if dr == 0:
                code_ref[pl.ds((z * 2 + y) * 2 + c, 1), :] = extra[1:2]
    mlp_ref[...] = mlp_s[...].astype(bf16)
    vec_ref[...] = jnp.concatenate([vec_s[j][:, :VEC_PART] for j in range(4)], axis=1)


ATTN_PACK = 80
MLP_PACK = 40


def each_share(keep_ref, give_ref, block_of):
    for dc in range(2):
        for plane in range(4):
            for s in range(Z):
                index, place = at_place(s, FAR_ORDER[plane] // 2, dc, FAR_ORDER[plane] % 2)
                block = block_of(index, place)
                if dc == 0:
                    keep_ref[plane, s] = block
                else:
                    give_ref[plane, s] = block.astype(bf16)


def mlp_pack(up_ref, down_ref, keep_ref, give_ref, mlp_s):
    mlp_s[:HIDDEN, :] = up_ref[...]
    mlp_s[HIDDEN:, :] = down_ref[...]

    def block_of(index, _):
        mlp = mlp_s[pl.ds(pl.multiple_of(index * MLP_ROWS, 8), MLP_ROWS), :]
        high = mlp[:, LANES:]
        return jnp.concatenate(
            [
                mlp[:, :LANES],
                jnp.concatenate([high[:8], high[8:16]], axis=1),
                jnp.concatenate([high[16:], jnp.zeros((8, HALF), f32)], axis=1),
            ],
            axis=0,
        )

    each_share(keep_ref, give_ref, block_of)


def grad_pack(feat_ref, item_ref, w7_ref, veca_ref, vecb_ref, keep_ref, give_ref, attn_s, vec_s):
    attn_s[: 4 * D, :] = feat_ref[...]
    attn_s[4 * D : 7 * D, :] = item_ref[...]
    attn_s[7 * D :, :] = w7_ref[...]
    vec = veca_ref[...] + vecb_ref[...]
    for j in range(4):
        part = vec[:, j * VEC_PART : (j + 1) * VEC_PART]
        vec_s[j] = jnp.concatenate([part, jnp.zeros((8, HALF - VEC_PART), f32)], axis=1)

    def block_of(index, place):
        z, y, c, r = place
        attn = attn_s[pl.ds(pl.multiple_of(index * ATTN_ROWS, 8), ATTN_ROWS), :]
        row = vec_s[c * 2 + r, pl.ds(z * 2 + y, 1), :]
        last = jnp.concatenate([row, jnp.zeros((15, HALF), f32)], axis=0)
        high = attn[:, LANES:]
        return jnp.concatenate(
            [
                attn[:, :LANES],
                jnp.concatenate([high[:16], high[16:32]], axis=1),
                jnp.concatenate([high[32:], last], axis=1),
            ],
            axis=0,
        )

    each_share(keep_ref, give_ref, block_of)


def grad_unpack(own_ref, *refs):
    total = own_ref[...]
    for ref in refs[: Z - 1]:
        total = total + ref[...].astype(f32)
    attn_ref, mlp_ref, vec_ref = refs[Z - 1 :]
    high = jnp.concatenate([total[48:64, :HALF], total[48:64, HALF:], total[64:80, :HALF]], axis=0)
    attn_ref[...] = jnp.concatenate([total[:48], high], axis=1)
    vec_ref[...] = total[64:65, HALF : HALF + VEC_PART]
    mlp = total[ATTN_PACK:]
    high = jnp.concatenate([mlp[24:32, :HALF], mlp[24:32, HALF:], mlp[32:, :HALF]], axis=0)
    mlp_ref[...] = jnp.concatenate([mlp[:24], high], axis=1)


VMEM = pl.BlockSpec(memory_space=pltpu.VMEM)
SMEM = pl.BlockSpec(memory_space=pltpu.SMEM)


def like(shape, kind=f32):
    return jax.ShapeDtypeStruct(shape, kind)


def swap(a, axis):
    return lax.ppermute(a, axis, [(0, 1), (1, 0)])


def exchange(a, axes):
    return lax.all_to_all(a, axes, 0, 0, tiled=True)


def along(axes, blocks):
    order = TASK_ORDER if axes == TASK_AXES else FAR_ORDER
    return blocks[:1] + [
        lax.ppermute(a, axes, [(i, i ^ x) for i in range(Z)]) for a, x in zip(blocks[1:], order[1:])
    ]


def gather_any(w_attn, w_mlp, vectors, table_ids, train_mask, feat_count, cells, cot, _):
    rows = table_ids.shape[1]
    fan, reps = lax.axis_size(FAN), lax.axis_size("rep")
    core = lax.axis_index("core")
    ra, rm, nv = w_attn.shape[0], w_mlp.shape[0], vectors.shape[0]
    code = (table_ids * 2 + (train_mask > 0)).astype(bf16)[0]
    last = jnp.pad(jnp.concatenate([vectors, code]), (0, D - nv - rows)).reshape(1, D)
    block = jnp.concatenate([w_attn, w_mlp, last], axis=0)
    rb = ra + rm + 1
    mine = exchange(jnp.broadcast_to(block[None], (fan, rb, D)), FAN)
    other = swap(mine, "core")
    both = jnp.stack([jnp.where(core == 0, mine, other), jnp.where(core == 0, other, mine)], axis=1)
    both = both.reshape(fan // reps, reps, 2, rb, D).transpose(0, 2, 1, 3, 4)
    attn = both[..., :ra, :].reshape(8 * D, D)
    mlp = both[..., ra : ra + rm, :].reshape(2 * HIDDEN, D)
    tail = both[..., ra + rm, :]
    vec = tail[..., :nv].reshape(8, D).astype(f32)
    codes = lax.dynamic_index_in_dim(tail[..., nv : nv + rows], lax.axis_index("rep"), 2, keepdims=False)
    hit = table_ids[0][:, None] == jnp.arange(TABLES)[None, :]
    counts = jnp.sum(jnp.where(hit, feat_count, 0), axis=1, keepdims=True).astype(f32)
    counts = jnp.broadcast_to(counts, (rows, D))
    return attn, mlp, vec, codes.reshape(-1, rows).astype(f32), counts, cells, cot


def gather_packed(w_attn, w_mlp, vectors, table_ids, train_mask, feat_count, cells, cot, limit):
    shares = (w_attn, w_mlp, vectors[None], table_ids, train_mask, feat_count)
    blocks = pl.pallas_call(
        share_pack,
        out_shape=(like((PACK, LANES), bf16),) * Z,
        in_specs=[pl.BlockSpec(memory_space=pl.ANY)] * 6,
        out_specs=(VMEM,) * Z,
        scratch_shapes=[pltpu.VMEM(a.shape, a.dtype) for a in shares] + [pltpu.SemaphoreType.DMA((6,))],
        compiler_params=pltpu.CompilerParams(vmem_limit_bytes=67000000),
        name="share_pack",
    )(*shares)
    *held, block_held = pl.pallas_call(
        hold,
        out_shape=(like(cells.shape, bf16), like(cells.shape, bf16), like((PACK, LANES), bf16)),
        in_specs=[VMEM] * 3,
        out_specs=(VMEM,) * 3,
        compiler_params=limit,
        name="hold",
    )(cells, cot, blocks[0])
    own = jnp.stack([block_held] + along(Z_AXES, list(blocks))[1:])
    own, held = lax.optimization_barrier((own, held))
    plane = along(PLANE_AXES, list(lax.optimization_barrier((own,) * 4)))
    *shares, counts = pl.pallas_call(
        share_unpack,
        out_shape=(
            like((8 * D, D), bf16),
            like((2 * HIDDEN, D), bf16),
            like((8, D)),
            like((4 * Z, table_ids.shape[1])),
            like((table_ids.shape[1], D)),
        ),
        in_specs=[VMEM] * 8,
        out_specs=(VMEM,) * 5,
        scratch_shapes=[pltpu.VMEM((2 * HIDDEN, D), f32), pltpu.VMEM((4, 8, HALF), f32)],
        compiler_params=limit,
        name="share_unpack",
    )(*plane, *[swap(a, "core") for a in plane])
    return *shares, counts, *held


def sum_any(grads, share, later, _):
    g_feat, g_item, g_w7, g_up, g_down, g_vec_a, g_vec_b = grads
    ra, rm, nv = share
    rb = ra + rm + 1
    fan, reps = lax.axis_size(FAN), lax.axis_size("rep")
    core = lax.axis_index("core")
    spread = (fan // reps, 2, reps)
    g_attn = jnp.concatenate([g_feat, g_item, g_w7], axis=0).reshape(spread + (ra, D))
    g_mlp = jnp.concatenate([g_up, g_down], axis=0).reshape(spread + (rm, D))
    g_vec = (g_vec_a + g_vec_b).reshape(spread + (1, nv))
    g_vec = jnp.pad(g_vec, ((0, 0),) * 4 + ((0, D - nv),))
    g_all = jnp.concatenate([g_attn, g_mlp, g_vec], axis=3)
    keep = lax.dynamic_index_in_dim(g_all, core, 1, keepdims=False)
    give = lax.dynamic_index_in_dim(g_all, 1 - core, 1, keepdims=False)
    chip = keep + swap(give.astype(bf16), "core").astype(f32)
    shares = exchange(chip.astype(bf16).reshape(fan, rb, D), FAN)
    total = jnp.sum(shares.astype(f32), axis=0)
    return total[:ra], total[ra : ra + rm], total[ra + rm, :nv], later


def over_plane(keep, got):
    sent = [keep[0]] + [(keep[i] + got[i]).astype(bf16) for i in range(1, 4)]
    return keep[0] + got[0], along(PLANE_AXES, sent)[1:]


def pack_call(kernel, grads, rows, scratch, limit, name):
    return pl.pallas_call(
        kernel,
        out_shape=(like((4, Z, rows, LANES)), like((4, Z, rows, LANES), bf16)),
        in_specs=[VMEM] * len(grads),
        out_specs=(VMEM,) * 2,
        scratch_shapes=scratch,
        compiler_params=limit,
        name=name,
    )(*grads)


def sum_packed(grads, mlp_total, share, later, limit):
    ra, rm, nv = share
    scratch = [pltpu.VMEM((8 * D, D), f32), pltpu.VMEM((4, 8, HALF), f32)]
    keep, give = pack_call(grad_pack, grads, ATTN_PACK, scratch, limit, "grad_pack")
    total, came = over_plane(keep, swap(give, "core").astype(f32))
    for a in came:
        total = total + a.astype(f32)
    total = jnp.concatenate([total, mlp_total], axis=1)
    steps = [total[0]] + [total[i].astype(bf16) for i in range(1, Z)]
    steps, later = lax.optimization_barrier((steps, later))
    attn, mlp, vec = pl.pallas_call(
        grad_unpack,
        out_shape=(like((ra, D)), like((rm, D)), like((1, nv))),
        in_specs=[VMEM] * Z,
        out_specs=(VMEM,) * 3,
        compiler_params=limit,
        name="grad_unpack",
    )(*along(Z_AXES, steps))
    return attn, mlp, vec.reshape(nv), later


def local(cell_values, table_ids, train_mask, feat_count, w_attn, w_mlp, vectors, cotangent):
    rows = cell_values.shape[1]
    cells_n = rows * FEAT
    h_n = lax.axis_size("zh")
    fast = h_n == 2
    all_rows = Z * h_n * 2 * rows
    q_rows = Z * rows
    small = pltpu.CompilerParams(vmem_limit_bytes=16 * 2**20)
    limit = small if fast else pltpu.CompilerParams(vmem_limit_bytes=63 * 2**20)

    cells = cell_values[0].transpose(1, 0, 2).reshape(cells_n, D)
    cot = cotangent[0].transpose(1, 0, 2).reshape(cells_n, D)

    shares = gather_packed if fast else gather_any
    attn, mlp, vec, codes, counts, cells, cot = shares(
        w_attn, w_mlp, vectors, table_ids, train_mask, feat_count, cells, cot, small
    )

    pair_block = like((rows, PAIR), bf16)
    half_rows = rows + rows // 2
    xhat1, rstd1, qkv, fo, probs, *x_out, cot_own = pl.pallas_call(
        functools.partial(feat_forward, rows),
        out_shape=(
            like((cells_n, D)),
            like((cells_n, D)),
            like((3, cells_n, D), bf16),
            like((cells_n, D), bf16),
            like((FEAT, FEAT, rows, D)),
            pair_block,
            like((2 * rows, PAIR), bf16),
            like((half_rows, PAIR), bf16),
            like((half_rows, PAIR), bf16),
            pair_block,
        ),
        in_specs=[VMEM] * 5,
        out_specs=(VMEM,) * 10,
        scratch_shapes=[
            pltpu.VMEM((Z, rows, PAIR), bf16),
            pltpu.VMEM((Z, rows, PAIR), bf16),
            pltpu.VMEM((Z, rows // 2, PAIR), bf16),
        ],
        compiler_params=small,
        name="feat_forward",
    )(cells, cot, counts, attn[: 4 * D], vec)

    def whole(*shape):
        return pl.BlockSpec(shape, lambda i: (0,) * len(shape))

    def by_slot(*shape):
        once = {"pipeline_mode": pl.Buffered(1)} if math.prod(shape) > 2**22 else {}
        return pl.BlockSpec(shape, lambda i: (i,) + (0,) * (len(shape) - 1), **once)

    def item_call(kernel, ins, outs, scratch, name):
        def specs(pairs):
            if fast:
                return [VMEM] * len(pairs)
            return [by_slot(a.shape[0] // SLOTS, *a.shape[1:]) if by else whole(*a.shape) for a, by in pairs]

        return pl.pallas_call(
            kernel,
            out_shape=[a for a, _ in outs],
            in_specs=specs(ins),
            out_specs=specs(outs),
            scratch_shapes=scratch,
            compiler_params=limit,
            cost_estimate=pl.CostEstimate(flops=10**8, bytes_accessed=0, transcendentals=0),
            name=name,
            **({} if fast else {"grid": (SLOTS,)}),
        )(*[a for a, _ in ins])

    def shared(*arrays):
        return [(a, False) for a in arrays]

    def tasked(*arrays):
        return [(a, True) for a in arrays]

    heads_block, pair_t = like((16, q_rows)), like((PAIR, q_rows))

    def forward_call(parts, bias, first, last, extra):
        keys = sum(a.shape[0] for a in parts)
        tasks = SLOTS if fast else 1
        outs = tasked(like((SLOTS * SLOT_HEADS, keys, q_rows), bf16)) + shared(heads_block)
        if first:
            outs += tasked(like((SLOTS, q_rows, LANES), bf16))
        if last:
            half_heads = like((q_rows // 2, SLOT_COLS), bf16)
            outs += shared(heads_block, heads_block, pair_t, like((q_rows, D), bf16), half_heads, half_heads)
        else:
            outs += shared(*([heads_block] * (1 if first else 2)), pair_t)
        scratch = [
            pltpu.VMEM((tasks, keys, LANES), bf16),
            pltpu.VMEM((tasks, LANES, keys), bf16),
            pltpu.VMEM((tasks * SLOT_HEADS, keys, q_rows), f32),
        ]
        kernel = functools.partial(item_forward, len(parts), 2, first, last, not fast)
        ins = shared(*parts) + tasked(kv_w, kv_wt) + shared(bias) + extra
        return item_call(kernel, ins, outs, scratch, "item_forward")

    def turn_call(groups, query):
        outs = tasked(like((SLOTS, LANES, q_rows), bf16))
        for parts in groups:
            keys = sum(a.shape[0] for a in parts)
            outs += shared(like((PAIR, keys), bf16))
            outs += tasked(like((SLOTS, keys, LANES), bf16), like((SLOTS, LANES, keys), bf16))
        kernel = functools.partial(item_turn, [len(g) for g in groups], not fast)
        ins = shared(*sum(groups, [])) + tasked(kv_w, kv_wt, query)
        query_t, *rest = item_call(kernel, ins, outs, [], "item_turn")
        return query_t, [tuple(rest[i : i + 3]) for i in range(0, len(rest), 3)]

    def backward_call(groups, parts, first, last, grads, extra):
        keys = sum(g[1].shape[1] for g in groups)
        tasks = SLOTS if fast else 1
        kv_shape, ds_shape = (tasks, 2 * LANES, keys), (tasks * SLOT_HEADS, keys, q_rows)
        scratch = [pltpu.VMEM(kv_shape, bf16), pltpu.VMEM(ds_shape, bf16)]
        if fast:
            outs = shared(*parts)
            outs += shared(like((3 * D, D))) if last else shared(pair_t, like(ds_shape, bf16), like(kv_shape, bf16))
            scratch = [pltpu.VMEM((PAIR, keys), f32)] + (scratch if last else [])
        else:
            outs = shared(like((3 * D, D)), *parts)
            scratch = [pltpu.VMEM((PAIR, q_rows), f32)] + scratch
        ins = []
        for xt, v, kt, p, top in groups:
            ins += shared(xt) + tasked(v, kt, p) + shared(top)
        ins += shared(*grads) + tasked(query_t) + shared(io_t, end, inv) + tasked(kv_w) + extra
        kernel = functools.partial(item_backward, len(groups), len(parts), first, last, not fast)
        return item_call(kernel, ins, outs, scratch, "item_backward")

    kv_w, kv_wt, q_w, key_bias, hot = pl.pallas_call(
        functools.partial(item_prepare, h_n),
        out_shape=(
            like((SLOTS, PAIR, 2 * LANES), bf16),
            like((SLOTS, 2 * LANES, PAIR), bf16),
            like((SLOTS, PAIR, LANES), bf16),
            like((all_rows, LANES), bf16),
            like((q_rows, LANES)),
        ),
        in_specs=[VMEM] * 2,
        out_specs=(VMEM,) * 5,
        compiler_params=limit,
        name="item_prepare",
    )(attn[4 * D : 7 * D], codes)

    def to_task(block, i):
        return lax.ppermute(block, TASK_AXES, [(j, j ^ TASK_ORDER[i]) for j in range(Z)])

    came = [to_task(x_out[i], i) for i in range(1, Z)]
    x_lo = jnp.concatenate([x_out[0], came[0][:rows]], axis=0)
    came[1:], _ = lax.optimization_barrier((came[1:], x_lo))
    x_hi = jnp.concatenate([a[:rows] for a in came[1:]], axis=0)
    cot_in = [cot_own] + [a[rows:] for a in came]
    if fast:
        h_lo, h_hi = swap(x_lo, "zh"), swap(x_hi, "zh")
        near = [x_lo, x_hi, swap(x_lo, "core"), swap(x_hi, "core")]
        ends = (0, 2 * q_rows, 3 * q_rows, 4 * q_rows)
        bias = [key_bias[a:b] for a, b in zip(ends, ends[1:])]
        near_p, near_top, query, total, mixed = forward_call(
            near, bias[0], True, False, tasked(q_w) + shared(hot)
        )
        h_lo, total = lax.optimization_barrier((h_lo, total))
        far_lo = [h_lo, swap(h_lo, "core")]
        lo_p, lo_top, end, total, mixed = forward_call(
            far_lo, bias[1], False, False, tasked(query) + shared(near_top, total, mixed)
        )
        h_hi, total = lax.optimization_barrier((h_hi, total))
        far_hi = [h_hi, swap(h_hi, "core")]
        hi_p, hi_top, end, inv, io_t, io_own, io_mine, io_give = forward_call(
            far_hi, bias[2], False, True, tasked(query) + shared(end, total, mixed)
        )
    else:
        x_q = jnp.concatenate([x_lo, x_hi], axis=0)
        parts = [lax.all_gather(x_q, ("zh", "core"), axis=0, tiled=True)]
        all_p, all_top, query, end, inv, io_t, io_own, io_mine, io_give = forward_call(
            parts, key_bias, True, True, tasked(q_w) + shared(hot, x_q)
        )

    def to_shared(block):
        return lax.ppermute(block, "y", [(0, 1), (1, 0)])

    io_came = to_shared(io_give)
    query, _ = lax.optimization_barrier((query, io_give))
    query_t, turned = turn_call([near, far_lo, far_hi] if fast else [parts], query)

    cells_low = like((cells_n, D), bf16)

    def middle_call(shared, w7, ins, ready, dio_shapes):
        count = q_rows // 2 if shared else q_rows
        low, full, hidden = like((count, D), bf16), like((count, D)), like((count, HIDDEN), bf16)
        outs = pl.pallas_call(
            functools.partial(row_middle, shared),
            out_shape=ready + [full] + [low] * 2 + [hidden] * 2 + [low] * 2 + [full] * 4 + dio_shapes,
            in_specs=[VMEM] * (3 + len(ins)),
            out_specs=[VMEM] * (len(ready) + 11 + len(dio_shapes)),
            compiler_params=small,
            name="row_middle",
        )(w7, mlp, vec, *ins)
        ready, (dz2, *outs) = outs[: len(ready)], outs[len(ready) :]
        return ready, dz2, outs[:10], outs[10:]

    half_heads = like(io_mine.shape, bf16)
    ready = [like((q_rows // 2, D)), like((q_rows // 2, D)), like((D, D), bf16)]
    (x1_shared, cot_shared, w7_shared), dz2_own, kept, (dio_own,) = middle_call(
        False, attn[7 * D :], [x_lo, x_hi, *cot_in, io_own], ready, [like(io_own.shape, bf16)]
    )
    io_came, dio_own = lax.optimization_barrier((io_came, dio_own))
    _, dz2_shared, kept_shared, (dio_mine, dio_give) = middle_call(
        True, w7_shared, [x1_shared, cot_shared, io_mine, io_came], [], [half_heads] * 2
    )
    kept = [io_own, io_mine, io_came] + kept
    dz2, kept = (dz2_own, dz2_shared), kept + kept_shared
    dio_in = [dio_own, dio_mine, to_shared(dio_give)]

    def rest_of_middle(kept):
        return pl.pallas_call(
            middle_grads,
            out_shape=(like((D, D)), like((HIDDEN, D)), like((HIDDEN, D)), like((8, D)))
            + (pair_block,) * 2
            + (like((rows // 2, PAIR), bf16),) * 2,
            in_specs=[VMEM] * 24,
            out_specs=(VMEM,) * (4 + Z),
            compiler_params=small,
            name="middle_grads",
        )(vec, *kept)

    if fast:
        half_f, half_b = like((2 * rows, PAIR)), like((2 * rows, PAIR), bf16)
        near, far_lo, far_hi = (t + s for t, s in zip(turned, ((near_p, near_top), (lo_p, lo_top), (hi_p, hi_top))))
        g_w7, g_up, g_down, g_vec_b, *out_blocks = rest_of_middle(kept)
        mlp_keep, mlp_give = pack_call(
            mlp_pack, (g_up, g_down), MLP_PACK, [pltpu.VMEM((2 * HIDDEN, D), f32)], small, "mlp_pack"
        )
        dio_in[2], mlp_give = lax.optimization_barrier((dio_in[2], mlp_give))
        lo_h, lo_hc, hi_h, hi_hc, dio_t, ds, dkv = backward_call(
            [far_lo, far_hi], (half_f, half_b) * 2, True, False, dio_in, []
        )
        dq_far, g_far = pl.pallas_call(
            item_far,
            out_shape=(like((SLOTS * SLOT_HEADS, HEAD_DIM, q_rows)), like((SLOTS, D, 2 * LANES))),
            in_specs=[VMEM] * 6,
            out_specs=(VMEM,) * 2,
            compiler_params=small,
            name="item_far",
        )(far_lo[0], far_lo[2], far_hi[0], far_hi[2], ds, dkv)
        from_c = [swap(a, "core") for a in (lo_hc, hi_hc)]
        from_c, dq_far = lax.optimization_barrier((from_c, dq_far))
        sent = [(a + b.astype(f32)).astype(bf16) for a, b in zip((lo_h, hi_h), from_c)]
        sent, dio_t, mlp_give = lax.optimization_barrier((sent, dio_t, mlp_give))
        from_h = [swap(a, "zh") for a in sent]
        mlp_got = swap(mlp_give, "core")
        *own, lo_c, hi_c, g_item = backward_call(
            [near],
            (half_f,) * 2 + (half_b,) * 2,
            False,
            True,
            [dio_t, *dz2],
            tasked(q_w) + shared(dq_far, g_far),
        )
        mlp_got, g_item = lax.optimization_barrier((mlp_got, g_item))
        mlp_total, mlp_came = over_plane(mlp_keep, mlp_got.astype(f32))
        from_h, to_c, out_blocks, mlp_came = lax.optimization_barrier(
            (from_h, (lo_c, hi_c), out_blocks, mlp_came[::-1])
        )
        for a in mlp_came:
            mlp_total = mlp_total + a.astype(f32)
        from_c = [swap(a, "core") for a in to_c]
        own = [(a + b.astype(f32) + c.astype(f32)).astype(bf16) for a, b, c in zip(own, from_c, from_h)]
    else:
        (xt, v, kt), = turned
        at_query = (lax.axis_index("zh") * 2 + lax.axis_index("core")) * q_rows
        xt_q = lax.dynamic_slice_in_dim(xt, at_query, q_rows, 1)
        g_item, dx_t, dxq_t = backward_call(
            [(xt, v, kt, all_p, all_top)],
            (like((PAIR, all_rows)), like((PAIR, q_rows))),
            True,
            True,
            dio_in,
            tasked(q_w) + shared(xt_q),
        )
        own = lax.psum_scatter(dx_t.T, ("zh", "core"), scatter_dimension=0, tiled=True) + dxq_t.T
        own = own + jnp.concatenate([dz2[0], jnp.pad(dz2[1], ((0, q_rows // 2), (0, 0)))], axis=1)
        own = jnp.split(own.astype(bf16), 2)
        g_w7, g_up, g_down, g_vec_b, *out_blocks = rest_of_middle(kept)
    dx_blocks = [own[s // 2][s % 2 * rows : (s % 2 + 1) * rows] for s in range(Z)]
    came = [to_task(jnp.concatenate([a, b], axis=0), i) for i, (a, b) in enumerate(zip(dx_blocks, out_blocks)) if i]
    dx_in = dx_blocks[:1] + [a[:rows] for a in came]
    out = pl.pallas_call(
        out_collect,
        out_shape=cells_low,
        in_specs=[VMEM] * Z,
        out_specs=VMEM,
        scratch_shapes=[pltpu.VMEM((FEAT, rows, D), bf16)],
        compiler_params=small,
        name="out_collect",
    )(out_blocks[0], *[a[rows:] for a in came])

    g_feat, g_vec_a, dz1, dqkv = pl.pallas_call(
        functools.partial(feat_backward, rows),
        out_shape=(like((4 * D, D)), like((8, D)), like((cells_n, D)), like((3, cells_n, D), bf16)),
        in_specs=[VMEM] * (8 + Z),
        out_specs=(VMEM,) * 4,
        scratch_shapes=[
            pltpu.VMEM((cells_n, D), f32),
            pltpu.VMEM((cells_n, D), f32),
            pltpu.VMEM((cells_n, D), f32),
            pltpu.VMEM((FEAT, rows, D), f32),
        ],
        compiler_params=small,
        name="feat_backward",
    )(xhat1, rstd1, cells, qkv, fo, probs, attn[: 4 * D], vec, *dx_in)

    share = (w_attn.shape[0], w_mlp.shape[0], vectors.shape[0])
    if fast:
        grads = (g_feat, g_item, g_w7, g_vec_a, g_vec_b)
        attn_share, mlp_share, vec_share, dz1 = sum_packed(grads, mlp_total, share, dz1, small)
    else:
        grads = (g_feat, g_item, g_w7, g_up, g_down, g_vec_a, g_vec_b)
        attn_share, mlp_share, vec_share, dz1 = sum_any(grads, share, dz1, small)

    dcell = pl.pallas_call(
        cell_out,
        out_shape=like((cells_n, D)),
        in_specs=[VMEM] * 3,
        out_specs=VMEM,
        compiler_params=small,
        name="cell_out",
    )(dz1, dqkv, attn[: 3 * D])

    def rows_first(a):
        return a.reshape(FEAT, rows, D).transpose(1, 0, 2)[None]

    return (
        rows_first(out),
        rows_first(dcell),
        attn_share,
        mlp_share,
        vec_share,
    )


def solution(mesh):
    blk_n, rep_n = mesh.devices.shape
    fine = Mesh(mesh.devices.reshape(blk_n // (2 * Z), 2, 2, 2, rep_n), BLK + ("rep",))
    every = BLK + ("rep",)
    in_specs = (
        P("rep", BLK, None, None),
        P("rep", BLK),
        P("rep", BLK),
        P("rep", None),
        P(every, None),
        P(every, None),
        P(every),
        P("rep", BLK, None, None),
    )
    out_specs = (
        P("rep", BLK, None, None),
        P("rep", BLK, None, None),
        P(every, None),
        P(every, None),
        P(every),
    )
    return jax.shard_map(local, mesh=fine, in_specs=in_specs, out_specs=out_specs, check_vma=False)
```
